32 devices in a mesh: stream: 2 (over x), batch: 16 (over z, y, core).
Axes of the slice: x: 2, y: 2, z: 4, core: 2. Of those that a mesh axis runs over, the one named last changes fastest.
Arguments:
- text_embed: bfloat16 [16, 512, 768], P('batch'), may hold values from -6 to 6
- visual_maps: bfloat16 [16, 512, 2048], P('batch', None, 'stream'), may hold values from -6 to 6
- visual_bucket: int32 [16], P('batch'), may hold values from 0 to 1
- rel_bucket: int32 [2, 16, 512, 512], P('stream', 'batch'), may hold values from 0 to 31
- joined_grad: bfloat16 [16, 512, 768], P('batch'), may hold values from -6 to 6
- attn_weight: float32 [2, 768, 3072], P('stream', 'batch')
- attn_moment: float32 [2, 768, 3072], P('stream', 'batch')
- attn_average: float32 [2, 768, 3072], P('stream', 'batch')
- ffn_weight: float32 [2, 768, 6144], P('stream', 'batch'), may hold values from -0.21875 to 0.21875
- ffn_moment: float32 [2, 768, 6144], P('stream', 'batch')
- ffn_average: float32 [2, 768, 6144], P('stream', 'batch'), may hold values from -0.0234375 to 0.0234375
- vector_weight: float32 [2, 9216], P('stream', 'batch')
- vector_moment: float32 [2, 9216], P('stream', 'batch')
- vector_average: float32 [2, 9216], P('stream', 'batch')
- project_weight: float32 [2048, 768], P(('stream', 'batch')), may hold values from -0.125 to 0.125
- project_moment: float32 [2048, 768], P(('stream', 'batch'))
- project_average: float32 [2048, 768], P(('stream', 'batch')), may hold values from -0.013671875 to 0.013671875
- shared_weight: float32 [1920], P('batch')
- shared_moment: float32 [1920], P('batch')
- shared_average: float32 [1920], P('batch')
Outputs:
- joined_out: bfloat16 [16, 512, 768], P('batch')
- stream_input_grad: float32 [2, 16, 512, 768], P('stream', 'batch')
- maps_grad: float32 [16, 512, 2048], P('batch', None, 'stream')
- attn_new: float32 [2, 768, 3072], P('stream', 'batch')
- attn_moment_new: float32 [2, 768, 3072], P('stream', 'batch')
- attn_average_new: float32 [2, 768, 3072], P('stream', 'batch')
- ffn_new: float32 [2, 768, 6144], P('stream', 'batch')
- ffn_moment_new: float32 [2, 768, 6144], P('stream', 'batch')
- ffn_average_new: float32 [2, 768, 6144], P('stream', 'batch')
- vector_new: float32 [2, 9216], P('stream', 'batch')
- vector_moment_new: float32 [2, 9216], P('stream', 'batch')
- vector_average_new: float32 [2, 9216], P('stream', 'batch')
- project_new: float32 [2048, 768], P(('stream', 'batch'))
- project_moment_new: float32 [2048, 768], P(('stream', 'batch'))
- project_average_new: float32 [2048, 768], P(('stream', 'batch'))
- shared_new: float32 [1920], P('batch')
- shared_moment_new: float32 [1920], P('batch')
- shared_average_new: float32 [1920], P('batch')
The draws below stay inside these ranges and needn't reach their ends.
Inputs may be any that keep to these rules, and one draw needn't show every extreme that they name: `visual_bucket`: 1 marks a page with 512 visual tokens, 0 one with 256.
All inputs are finite; a program needn't handle non-finite values.
Results may differ from the reference program's by a relative error of at most 0.039.
Values may be sent and summed in bfloat16 or wider, within the bound.
No kernel may reach another device: no remote copies, remote signals or barrier semaphores. Data moves between devices by JAX's collectives and lax.ppermute only.
A program may use at most 192 MiB of HBM per device.

```python
import math
import jax
import jax.numpy as jnp
from jax import lax

D = 768
HEADS = 12
HEAD_DIM = 64
FF = 3072
CNN = 2048
TLEN = 512
BUCKETS = 32
PAGES = 16


def attention_law(key, scale):
    sample_values = jnp.clip(jax.random.normal(key, (2, D, 4 * D), jnp.float32), -4.0, 4.0)
    column = jnp.arange(4 * D)
    factor = jnp.where(column < 3 * D, 1.0, 8.0) * D ** (-0.5)
    return sample_values * factor * scale


def vector_law(key, scale):
    sample_values = jax.random.uniform(key, (2, 8 * D + FF), jnp.float32, -1.0, 1.0)
    position = jnp.arange(8 * D + FF)
    gain_slots = (position >= 3 * D) & (position < 4 * D) | (position >= 6 * D + FF) & (position < 7 * D + FF)
    return jnp.where(gain_slots, 1.0 + 0.4 * sample_values, 0.5 * sample_values) * scale


def shared_law(key, scale):
    table_key, rest_key = jax.random.split(key)
    table_values = jnp.clip(jax.random.normal(table_key, (BUCKETS * HEADS,), jnp.float32), -4.0, 4.0)
    rest_values = jax.random.uniform(rest_key, (2 * D,), jnp.float32, -1.0, 1.0)
    position = jnp.arange(2 * D)
    rest_values = jnp.where(position < D, 1.0 + 0.4 * rest_values, 0.5 * rest_values)
    return jnp.concatenate([table_values, rest_values]) * scale


def moment_law(key, array_shape):
    sample_values = jnp.clip(jax.random.normal(key, array_shape, jnp.float32), -4.0, 4.0)
    return sample_values * (0.5 * jnp.sqrt(jnp.float32(PAGES * TLEN)))


def draw_attn_weight(key, part):
    key = jax.random.fold_in(key, 1)
    return attention_law(key, 1.0)


def draw_attn_average(key, part):
    key = jax.random.fold_in(key, 2)
    return attention_law(key, 0.1)


def draw_attn_moment(key, part):
    key = jax.random.fold_in(key, 3)
    return moment_law(key, (2, D, 4 * D))


def draw_ffn_moment(key, part):
    key = jax.random.fold_in(key, 4)
    return moment_law(key, (2, D, 2 * FF))


def draw_vector_weight(key, part):
    key = jax.random.fold_in(key, 5)
    return vector_law(key, 1.0)


def draw_vector_average(key, part):
    key = jax.random.fold_in(key, 6)
    return vector_law(key, 0.1)


def draw_vector_moment(key, part):
    key = jax.random.fold_in(key, 7)
    return moment_law(key, (2, 8 * D + FF))


def draw_project_moment(key, part):
    key = jax.random.fold_in(key, 8)
    return moment_law(key, (CNN, D))


def draw_shared_weight(key, part):
    key = jax.random.fold_in(key, 9)
    return shared_law(key, 1.0)


def draw_shared_average(key, part):
    key = jax.random.fold_in(key, 10)
    return shared_law(key, 0.1)


def draw_shared_moment(key, part):
    key = jax.random.fold_in(key, 11)
    return moment_law(key, (BUCKETS * HEADS + 2 * D,))


def touch_ends(values, key, least, high):
    longest = values.shape.index(max(values.shape))
    spots = []
    for shift in (0, 1):
        where = [jax.random.randint(jax.random.fold_in(key, axis), (), 0, length) for axis, length in enumerate(values.shape)]
        where[longest] = (where[longest] + shift) % values.shape[longest]
        spots.append(tuple(where))
    return values.at[spots[0]].set(least).at[spots[1]].set(high)


def levels(key, shape, cuts, low, high):
    loudness = 1.0
    for dim, blocks in cuts:
        draws = jax.random.uniform(jax.random.fold_in(jax.random.fold_in(key, 6), dim), (blocks,), jnp.float32, low / len(cuts), high / len(cuts))
        loudness = loudness * jnp.repeat(jnp.exp(draws), shape[dim] // blocks).reshape((-1,) + (1,) * (len(shape) - 1 - dim))
    return loudness


def scatter_about(key, shape, scale, limit, cuts=(), kind=jnp.bfloat16):
    array = jax.random.normal(key, shape, jnp.float32) * scale
    if len(cuts) > 0:
        array = levels(key, shape, cuts, -0.22, 0.18) * array
    return jnp.clip(array, min=-limit, max=limit).astype(kind)


def setup_inputs(seed: int = 0) -> dict:
    key_list = jax.random.split(jax.random.key(seed), 21)
    text_embed = scatter_about(key_list[0], (PAGES, TLEN, D), 1.0, 6.0, ((0, 16),))
    visual_maps = scatter_about(key_list[1], (PAGES, TLEN, CNN), 1.0, 6.0, ((0, 16), (2, 2)))
    visual_bucket = touch_ends(jax.random.randint(key_list[2], (PAGES,), 0, 2), jax.random.fold_in(key_list[2], 1), 0, 1).astype(jnp.int32)
    rel_bucket = touch_ends(jax.random.randint(key_list[3], (2, PAGES, TLEN, TLEN), 0, BUCKETS), jax.random.fold_in(key_list[3], 1), 0, BUCKETS - 1).astype(jnp.int32)
    joined_grad = scatter_about(key_list[4], (PAGES, TLEN, D), 1.0, 6.0, ((0, 16),))
    attn_weight = draw_attn_weight(jax.random.fold_in(key_list[20], 71), 0)
    attn_moment = draw_attn_moment(jax.random.fold_in(key_list[20], 71), 0)
    attn_average = draw_attn_average(jax.random.fold_in(key_list[20], 71), 0)
    ffn_weight = scatter_about(key_list[8], (2, D, 2 * FF), D ** -0.5, 0.21875, ((0, 2), (1, 16)), jnp.float32)
    ffn_moment = draw_ffn_moment(jax.random.fold_in(key_list[20], 71), 0)
    ffn_average = scatter_about(key_list[10], (2, D, 2 * FF), (100 * D) ** -0.5, 0.0234375, ((0, 2), (1, 16)), jnp.float32)
    vector_weight = draw_vector_weight(jax.random.fold_in(key_list[20], 71), 0)
    vector_moment = draw_vector_moment(jax.random.fold_in(key_list[20], 71), 0)
    vector_average = draw_vector_average(jax.random.fold_in(key_list[20], 71), 0)
    project_weight = scatter_about(key_list[14], (CNN, D), CNN ** -0.5, 0.125, ((0, 32),), jnp.float32)
    project_moment = draw_project_moment(jax.random.fold_in(key_list[20], 71), 0)
    project_average = scatter_about(key_list[16], (CNN, D), (100 * CNN) ** -0.5, 0.013671875, ((0, 32),), jnp.float32)
    shared_weight = draw_shared_weight(jax.random.fold_in(key_list[20], 71), 0)
    shared_moment = draw_shared_moment(jax.random.fold_in(key_list[20], 71), 0)
    shared_average = draw_shared_average(jax.random.fold_in(key_list[20], 71), 0)
    return {"text_embed": text_embed, "visual_maps": visual_maps, "visual_bucket": visual_bucket, "rel_bucket": rel_bucket, "joined_grad": joined_grad, "attn_weight": attn_weight, "attn_moment": attn_moment, "attn_average": attn_average, "ffn_weight": ffn_weight, "ffn_moment": ffn_moment, "ffn_average": ffn_average, "vector_weight": vector_weight, "vector_moment": vector_moment, "vector_average": vector_average, "project_weight": project_weight, "project_moment": project_moment, "project_average": project_average, "shared_weight": shared_weight, "shared_moment": shared_moment, "shared_average": shared_average}


EPS = 1e-05
MOMENTUM = 0.9
AVERAGE = 0.95
HIGHEST = lax.Precision.HIGHEST

@jax.custom_vjp
def low(v):
    return lax.optimization_barrier(v.astype(jnp.bfloat16)).astype(jnp.float32)

@jax.custom_vjp
def low_back(v):
    return v

def low_keep(v):
    return (low(v), None)

def low_pass(kept, grad):
    return (grad,)

def back_keep(v):
    return (v, None)

def back_low(kept, grad):
    return (low(grad),)
low.defvjp(low_keep, low_pass)
low_back.defvjp(back_keep, back_low)

def matmul(left_side, right_side):
    return jnp.dot(left_side, right_side, precision=HIGHEST, preferred_element_type=jnp.float32)

def layer_norm(values, norm_gain, norm_shift):
    centre = values - lax.optimization_barrier(jnp.mean(values, axis=-1, keepdims=True))
    spread = lax.optimization_barrier(jnp.mean(centre * centre, axis=-1, keepdims=True))
    return centre * lax.rsqrt(spread + EPS) * norm_gain + norm_shift

def split_vector(vector):
    bounds = [0, D, 2 * D, 3 * D, 4 * D, 5 * D, 5 * D + FF, 6 * D + FF, 7 * D + FF, 8 * D + FF]
    return [vector[bounds[i]:bounds[i + 1]] for i in range(9)]

def page_layer(inputs, table, attn_low, ffn_low, vector):
    x_page, live_len, bucket = inputs
    q_bias, v_bias, out_bias, gain_one, shift_one, hidden_bias, ffn_bias, gain_two, shift_two = split_vector(vector)
    positions = jnp.arange(TLEN, dtype=jnp.int32)
    key_valid = positions < live_len
    row_mask = key_valid.astype(jnp.float32)[:, None]
    x_low = low(x_page)
    zero_bias = jnp.zeros((D,), jnp.float32)
    projected = low(low_back(matmul(x_low, attn_low[:, :3 * D]) + jnp.concatenate([q_bias, zero_bias, v_bias])))
    projected = projected.reshape(TLEN, 3, HEADS, HEAD_DIM)
    query_heads = projected[:, 0]
    key_heads = projected[:, 1]
    value_heads = projected[:, 2]
    spatial_bias = jnp.transpose(table[bucket], (2, 0, 1))
    raw_scores = jnp.einsum('ihd,jhd->hij', query_heads, key_heads, precision=HIGHEST) * HEAD_DIM ** (-0.5)
    scores = low_back(raw_scores + spatial_bias)
    scores = jnp.where(key_valid[None, None, :], scores, -1000000000.0)
    row_peak = lax.optimization_barrier(jnp.max(scores, axis=-1, keepdims=True))
    exp_scores = jnp.exp(scores - row_peak)
    attn_probs = exp_scores / lax.optimization_barrier(jnp.sum(exp_scores, axis=-1, keepdims=True))
    context = jnp.einsum('hij,jhd->ihd', low(attn_probs), value_heads, precision=HIGHEST).reshape(TLEN, D)
    context = low(low_back(context))
    attended = low_back(matmul(context, attn_low[:, 3 * D:]) + out_bias)
    first_norm = layer_norm(x_page + attended, gain_one, shift_one)
    inner_units = low_back(matmul(low(first_norm), ffn_low[:, :FF]) + hidden_bias)
    active = low(jax.nn.gelu(inner_units, approximate=True))
    output = low_back(matmul(active, ffn_low[:, FF:].T) + ffn_bias)
    return layer_norm(first_norm + output, gain_two, shift_two) * row_mask

def run_stream(x_stream, lengths, buckets, table, attn_low, ffn_low, vector):
    page_step = jax.checkpoint(lambda inputs: page_layer(inputs, table, attn_low, ffn_low, vector))
    return lax.map(page_step, (x_stream, lengths, buckets))

def front(maps_float, project, shared, live_mask):
    pre_norm = low_back(jnp.einsum('ptc,cd->ptd', maps_float, low(project), precision=HIGHEST))
    shared_low = low(shared)
    bn_gain = shared_low[BUCKETS * HEADS:BUCKETS * HEADS + D]
    bn_shift = shared_low[BUCKETS * HEADS + D:]
    live_total = jnp.sum(live_mask)
    weighted = live_mask[..., None]
    batch_mean = lax.optimization_barrier(jnp.sum(pre_norm * weighted, axis=(0, 1))) / live_total
    centred = pre_norm - batch_mean
    batch_var = lax.optimization_barrier(jnp.sum(centred * centred * weighted, axis=(0, 1))) / live_total
    return (centred * lax.rsqrt(batch_var + EPS) * bn_gain + bn_shift) * weighted

def nesterov(weight, moment, average, gradient, rate):
    moment_new = MOMENTUM * moment + gradient
    weight_new = weight - rate * (gradient + MOMENTUM * moment_new)
    return (weight_new, moment_new, AVERAGE * average + (1.0 - AVERAGE) * weight_new)

def reference(text_embed, visual_maps, visual_bucket, rel_bucket, joined_grad, attn_weight, attn_moment, attn_average, ffn_weight, ffn_moment, ffn_average, vector_weight, vector_moment, vector_average, project_weight, project_moment, project_average, shared_weight, shared_moment, shared_average):
    visual_len = ((visual_bucket + 1) * (TLEN // 2)).astype(jnp.int32)
    positions = jnp.arange(TLEN, dtype=jnp.int32)
    live_mask = (positions[None, :] < visual_len[:, None]).astype(jnp.float32)
    text_len = jnp.full((PAGES,), TLEN, jnp.int32)
    maps_float = visual_maps.astype(jnp.float32)
    text_float = text_embed.astype(jnp.float32)

    def whole(text_in, visual_in, attn_all, ffn_all, vector_all, shared):
        shared_low = low(shared)
        table = shared_low[:BUCKETS * HEADS].reshape(BUCKETS, HEADS)
        attn_low = low(attn_all)
        ffn_low = low(ffn_all)
        vector_low = low(vector_all)
        text_out = run_stream(text_in, text_len, rel_bucket[0], table, attn_low[0], ffn_low[0], vector_low[0])
        visual_out = run_stream(visual_in, visual_len, rel_bucket[1], table, attn_low[1], ffn_low[1], vector_low[1])
        return (text_out, visual_out)
    visual_in, front_back = jax.vjp(lambda maps_in, project, shared: front(maps_in, project, shared, live_mask), maps_float, project_weight, shared_weight)
    (text_out, visual_out), layer_back = jax.vjp(whole, text_float, visual_in, attn_weight, ffn_weight, vector_weight, shared_weight)
    joined_out = (text_out + visual_out).astype(jnp.bfloat16)
    cotangent = joined_grad.astype(jnp.float32)
    grad_text, grad_visual, grad_attn, grad_ffn, grad_vector, grad_shared_layer = layer_back((cotangent, cotangent))
    grad_maps, grad_project, grad_shared_front = front_back(grad_visual)
    grad_shared = grad_shared_layer + grad_shared_front
    stream_input_grad = jnp.stack([grad_text, grad_visual])
    tokens_all = PAGES * TLEN
    rate_attention = 1.5 / math.sqrt(D * tokens_all)
    rate_matrix = 0.6 / math.sqrt(D * tokens_all)
    rate_vector = 0.12 / math.sqrt(tokens_all)
    attn_new = nesterov(attn_weight, attn_moment, attn_average, grad_attn, rate_attention)
    ffn_new = nesterov(ffn_weight, ffn_moment, ffn_average, grad_ffn, rate_matrix)
    vector_new = nesterov(vector_weight, vector_moment, vector_average, grad_vector, rate_vector)
    project_new = nesterov(project_weight, project_moment, project_average, grad_project, rate_matrix)
    shared_new = nesterov(shared_weight, shared_moment, shared_average, grad_shared, rate_vector)
    return (joined_out, stream_input_grad, grad_maps, attn_new[0], attn_new[1], attn_new[2], ffn_new[0], ffn_new[1], ffn_new[2], vector_new[0], vector_new[1], vector_new[2], project_new[0], project_new[1], project_new[2], shared_new[0], shared_new[1], shared_new[2])
```

```python
import functools
import math

import jax
import jax.numpy as jnp
import numpy as np
from jax import lax
from jax.experimental import pallas as pl
from jax.experimental.pallas import tpu as pltpu
from jax.sharding import PartitionSpec as P

D = 768
HEADS = 12
HEAD_DIM = 64
FF = 3072
TLEN = 512
BUCKETS = 32
PAIRS = HEADS // 2
ROWS = 128
STEPS = TLEN // ROWS
CHUNKS = FF // D

EPS = 1e-05
MOMENTUM = 0.9
AVERAGE = 0.95
SCALE = HEAD_DIM ** (-0.5)

BF16 = jnp.bfloat16
F32 = jnp.float32
ANY = pl.BlockSpec(memory_space=pl.ANY)
SMEM = pl.BlockSpec(memory_space=pltpu.SMEM)
VMEM = pl.BlockSpec(memory_space=pltpu.VMEM)
MIB = 1024 * 1024

CYCLE = ((0, 0), (1, 0), (2, 0), (3, 0), (3, 1), (2, 1), (1, 1), (0, 1))
CHIP = [z * 2 + y for z, y in CYCLE]
PLACE = [CHIP.index(k) for k in range(8)]


def cycle_perm(shift):
    return [
        (CHIP[r] * 2 + c, CHIP[(r + shift) % 8] * 2 + c) for r in range(8) for c in range(2)
    ]


def across(v):
    return lax.ppermute(v, "stream", [(0, 1), (1, 0)])


def swap(v, bit):
    n = lax.axis_size("batch")
    return lax.ppermute(v, "batch", [(i, i ^ bit) for i in range(n)])


def gather_shifts():
    return [0, -1, 1, -2, 2, -3, 3, -4]


def gather_sources():
    table = np.zeros((16, 16), np.int32)
    for b in range(16):
        place, core = PLACE[b // 2], b % 2
        for slot, shift in enumerate(gather_shifts()):
            chip = CHIP[(place + shift) % 8]
            table[b, slot] = chip * 2 + core
            table[b, 8 + slot] = chip * 2 + 1 - core
    return table


def scatter_targets():
    table = np.zeros((16, 16), np.int32)
    for b in range(16):
        place, core = PLACE[b // 2], b % 2
        for ahead in range(8):
            chip = CHIP[(place + ahead) % 8]
            table[b, ahead] = chip * 2 + core
            table[b, 8 + ahead] = chip * 2 + 1 - core
    return table


def ring_gather(block):
    up, down = cycle_perm(1), cycle_perm(-1)
    low = high = block
    own = [block]
    for _ in range(3):
        low = lax.ppermute(low, "batch", up)
        high = lax.ppermute(high, "batch", down)
        own += [low, high]
    own.append(lax.ppermute(low, "batch", up))
    return own + [swap(v, 1) for v in own]


def ring_scatter(mine, theirs):
    up, down = cycle_perm(1), cycle_perm(-1)
    other = swap(theirs, 1)

    def term(j):
        return mine[j].astype(F32) + other[j].astype(F32)

    def passed(v, j):
        return (v.astype(F32) + term(j)).astype(BF16)

    low = lax.ppermute(term(4).astype(BF16), "batch", up)
    high = lax.ppermute(term(5).astype(BF16), "batch", down)
    low = lax.ppermute(passed(low, 3), "batch", up)
    high = lax.ppermute(passed(high, 6), "batch", down)
    low = lax.ppermute(passed(low, 2), "batch", up)
    high = lax.ppermute(passed(high, 7), "batch", down)
    low = lax.ppermute(passed(low, 1), "batch", up)
    return low.astype(F32) + high.astype(F32) + term(0)


def reduce_grad(parts):
    if len(parts) == 1:
        return lax.psum_scatter(parts[0][0], "batch", scatter_dimension=0, tiled=True).astype(F32)
    return ring_scatter(parts[0], parts[1])


def dot(left, right):
    return jnp.dot(left, right, preferred_element_type=F32)


def dot_nt(left, right):
    return lax.dot_general(left, right, (((1,), (1,)), ((), ())), preferred_element_type=F32)


def load_blocks(offs, blocks, dst, sems, start):
    for i, block in enumerate(blocks):
        rows = block.shape[0]
        at = pl.multiple_of(offs[i], 16) if len(blocks) > 1 else 0
        copy = pltpu.make_async_copy(block, dst.at[pl.ds(at, rows), :], sems.at[i])
        if start:
            copy.start()
        else:
            copy.wait()


def store_blocks(offs, src, parts, sems):
    copies = []
    if len(parts) == 1:
        copies.append(pltpu.make_async_copy(src, parts[0].at[0], sems.at[0]))
    else:
        for k in range(16):
            part = parts[k // 8]
            rows = part.shape[1]
            at = pl.multiple_of(offs[k], 16)
            copies.append(
                pltpu.make_async_copy(src.at[pl.ds(at, rows), :], part.at[k % 8], sems.at[k])
            )
    for copy in copies:
        copy.start()
    for copy in copies:
        copy.wait()


def grad_shapes(n_blocks, rows, cols):
    if n_blocks == 1:
        return [jax.ShapeDtypeStruct((1, rows, cols), BF16)]
    return [jax.ShapeDtypeStruct((8, rows // 16, cols), BF16)] * 2


def params(mib):
    return pltpu.CompilerParams(vmem_limit_bytes=mib * MIB)


def cost(flops, size):
    return pl.CostEstimate(flops=int(flops), bytes_accessed=int(size), transcendentals=0)


def norm_rows(values):
    centre = values - jnp.mean(values, axis=-1, keepdims=True)
    inverse = lax.rsqrt(jnp.mean(centre * centre, axis=-1, keepdims=True) + EPS)
    return centre * inverse, inverse


def norm_back(upstream, normed, inverse, gain):
    scaled = upstream * gain
    return inverse * (
        scaled
        - jnp.mean(scaled, axis=-1, keepdims=True)
        - normed * jnp.mean(scaled * normed, axis=-1, keepdims=True)
    )


def half_mask(rows, half):
    lane = lax.broadcasted_iota(jnp.int32, (rows, 128), 1)
    return (lane < HEAD_DIM) if half == 0 else (lane >= HEAD_DIM)


def project_kernel(n_blocks, offs, maps, *refs):
    blocks, refs = refs[:n_blocks], refs[n_blocks:]
    pre, whole, small, sems, small_sems = refs
    copies = []
    rows = whole.shape[0] // n_blocks
    for i, block in enumerate(blocks):
        which = offs[i] if n_blocks > 1 else 0
        at = pl.multiple_of(which * rows, 16)
        copies.append(
            pltpu.make_async_copy(block.at[pl.ds(0, rows), :], whole.at[pl.ds(at, rows), :], sems.at[i])
        )
        copies.append(
            pltpu.make_async_copy(block.at[pl.ds(rows, 16), :], small.at[which], small_sems.at[i])
        )
    for copy in copies:
        copy.start()
    for copy in copies:
        copy.wait()
    for i in range(2):
        pick = pl.ds(i * (TLEN // 2), TLEN // 2)
        pre[pick, :] = dot(maps[pick, :], whole[...]).astype(BF16)


def project(offs, maps, blocks):
    n = len(blocks)
    rows = blocks[0].shape[0] - 16
    channels = n * rows
    return pl.pallas_call(
        functools.partial(project_kernel, n),
        out_shape=[
            jax.ShapeDtypeStruct((TLEN, D), BF16),
            jax.ShapeDtypeStruct((channels, D), BF16),
            jax.ShapeDtypeStruct((n, 16, D), BF16),
        ],
        in_specs=[SMEM, VMEM] + [ANY] * n,
        out_specs=[VMEM] * 3,
        scratch_shapes=[pltpu.SemaphoreType.DMA((n,)), pltpu.SemaphoreType.DMA((n,))],
        compiler_params=params(24),
        cost_estimate=cost(2 * TLEN * channels * D, 6e6),
        name="project_maps",
    )(offs, maps, *blocks)


def attn_fwd_kernel(n_blocks, offs, live, *refs):
    blocks, refs = refs[:n_blocks], refs[n_blocks:]
    x, bucket, table, vec, qkv, probs, ctx, normed, inverse, weight, sems = refs
    pair = pl.program_id(0)

    @pl.when(pair == 0)
    def _():
        load_blocks(offs, blocks, weight, sems, True)
        load_blocks(offs, blocks, weight, sems, False)
        x_low = x[...].astype(BF16)
        for part in range(3):
            cols = slice(part * D, (part + 1) * D)
            value = dot(x_low, weight[:, cols])
            if part != 1:
                value = value + vec[part // 2 : part // 2 + 1, :]
            qkv[:, cols] = value.astype(BF16)

    at = pl.multiple_of(pair * 128, 128)
    keys = qkv[:, pl.ds(pl.multiple_of(D + pair * 128, 128), 128)]
    values = qkv[:, pl.ds(pl.multiple_of(2 * D + pair * 128, 128), 128)]
    key_valid = lax.broadcasted_iota(jnp.int32, (ROWS, TLEN), 1) < live[0]

    def block(i, carry):
        rows = pl.ds(pl.multiple_of(i * ROWS, ROWS), ROWS)
        query = qkv[rows, pl.ds(at, 128)] * SCALE
        result = []
        for half in range(2):
            mask = half_mask(ROWS, half)
            scores = dot_nt(jnp.where(mask, query, jnp.zeros_like(query)), keys)
            row = jnp.broadcast_to(table[pl.ds(pair * 2 + half, 1), :], (ROWS, 128))
            bias = jnp.concatenate(
                [
                    jnp.take_along_axis(row, bucket[rows, t * 128 : (t + 1) * 128], axis=1)
                    for t in range(TLEN // 128)
                ],
                axis=1,
            )
            scores = jnp.where(key_valid, scores + bias, -1000000000.0)
            peak = jnp.max(scores, axis=-1, keepdims=True)
            raised = jnp.exp(scores - peak)
            total = jnp.sum(raised, axis=-1, keepdims=True)
            prob = (raised * (1.0 / total)).astype(BF16)
            probs[half, rows, :] = prob
            result.append(dot(prob, values))
        ctx[rows, pl.ds(at, 128)] = jnp.where(half_mask(ROWS, 0), result[0], result[1]).astype(BF16)
        return carry

    lax.fori_loop(0, STEPS, block, 0)

    @pl.when(pair == PAIRS - 1)
    def _():
        for i in range(STEPS):
            rows = pl.ds(i * ROWS, ROWS)
            att = dot(ctx[rows, :], weight[:, 3 * D :]) + vec[2:3, :]
            normal, inv = norm_rows(x[rows, :] + att)
            normed[rows, :] = normal
            inverse[rows, :] = jnp.broadcast_to(inv, (ROWS, 128))


def attn_fwd(offs, live, blocks, x, bucket, table, vec):
    n = len(blocks)

    def whole(shape):
        return pl.BlockSpec(shape, lambda i: (0,) * len(shape))

    return pl.pallas_call(
        functools.partial(attn_fwd_kernel, n),
        grid=(PAIRS,),
        out_shape=[
            jax.ShapeDtypeStruct((TLEN, 3 * D), BF16),
            jax.ShapeDtypeStruct((HEADS, TLEN, TLEN), BF16),
            jax.ShapeDtypeStruct((TLEN, D), BF16),
            jax.ShapeDtypeStruct((TLEN, D), F32),
            jax.ShapeDtypeStruct((TLEN, 128), F32),
        ],
        in_specs=[SMEM, SMEM]
        + [ANY] * n
        + [whole((TLEN, D)), whole((TLEN, TLEN)), whole((16, 128)), whole((16, D))],
        out_specs=[
            whole((TLEN, 3 * D)),
            pl.BlockSpec((2, TLEN, TLEN), lambda i: (i, 0, 0)),
            whole((TLEN, D)),
            whole((TLEN, D)),
            whole((TLEN, 128)),
        ],
        scratch_shapes=[pltpu.VMEM((D, 4 * D), BF16), pltpu.SemaphoreType.DMA((n,))],
        compiler_params=params(40),
        cost_estimate=cost(4e9 * 3, 20e6),
        name="attention_forward",
    )(offs, live, *blocks, x, bucket, table, vec)


def ffn_fwd_kernel(n_parts, offs, live, ffn, normed, vec, joined_grad, *refs):
    parts, refs = refs[:n_parts], refs[n_parts:]
    result, slope, grad_second, grad_low, grads, up, down, active, total, grad, sems, out_sems = refs

    def load(k):
        return (
            pltpu.make_async_copy(ffn.at[:, pl.ds(k * D, D)], up.at[k % 2], sems.at[k]),
            pltpu.make_async_copy(ffn.at[:, pl.ds(FF + k * D, D)], down.at[k % 2], sems.at[CHUNKS + k]),
        )

    for k in range(2):
        for copy in load(k):
            copy.start()
    first = normed[...] * vec[3:4, :] + vec[4:5, :]
    first_low = first.astype(BF16)
    for k in range(CHUNKS):
        for copy in load(k):
            copy.wait()
        for i in range(STEPS):
            rows = slice(i * ROWS, (i + 1) * ROWS)
            units = dot(first_low[rows, :], up[k % 2]) + vec[5 + k : 6 + k, :]
            square = units * units
            root = math.sqrt(2.0 / math.pi)
            bend = jnp.tanh(root * units * (1.0 + 0.044715 * square))
            half = 0.5 * (1.0 + bend)
            act = (units * half).astype(BF16)
            active[k, rows, :] = act
            slope[k, rows, :] = (
                half + 0.5 * root * units * (1.0 - bend * bend) * (1.0 + 3.0 * 0.044715 * square)
            ).astype(BF16)
            add = dot_nt(act, down[k % 2])
            if k == 0:
                total[rows, :] = add
            else:
                total[rows, :] += add
        if k + 2 < CHUNKS:
            for copy in load(k + 2):
                copy.start()
    normal, inv = norm_rows(first + total[...] + vec[9:10, :])
    mask = lax.broadcasted_iota(jnp.int32, (TLEN, 1), 0) < live[0]
    result[...] = jnp.where(mask, normal * vec[10:11, :] + vec[11:12, :], 0.0).astype(BF16)
    upstream = jnp.where(mask, joined_grad[...].astype(F32), 0.0)
    second = norm_back(upstream, normal, inv, vec[10:11, :])
    second_low = second.astype(BF16)
    grad_second[...] = second
    grad_low[...] = second_low
    grads[0:1, :] = jnp.sum(second_low.astype(F32), axis=0, keepdims=True)
    grads[1:2, :] = jnp.sum(upstream * normal, axis=0, keepdims=True)
    grads[2:3, :] = jnp.sum(upstream, axis=0, keepdims=True)
    turned = second_low.T
    for k in range(CHUNKS):
        grad[:, k * D : (k + 1) * D] = dot(turned, active[k]).astype(BF16)
    store_blocks(offs, grad, parts, out_sems)


def ffn_fwd(offs, n_blocks, live, ffn, normed, vec, joined_grad):
    parts = grad_shapes(n_blocks, D, FF)
    out = pl.pallas_call(
        functools.partial(ffn_fwd_kernel, len(parts)),
        out_shape=parts
        + [
            jax.ShapeDtypeStruct((TLEN, D), BF16),
            jax.ShapeDtypeStruct((CHUNKS, TLEN, D), BF16),
            jax.ShapeDtypeStruct((TLEN, D), F32),
            jax.ShapeDtypeStruct((TLEN, D), BF16),
            jax.ShapeDtypeStruct((8, D), F32),
        ],
        in_specs=[SMEM, SMEM, ANY, VMEM, VMEM, VMEM],
        out_specs=[ANY] * len(parts) + [VMEM] * 5,
        scratch_shapes=[
            pltpu.VMEM((2, D, D), BF16),
            pltpu.VMEM((2, D, D), BF16),
            pltpu.VMEM((CHUNKS, TLEN, D), BF16),
            pltpu.VMEM((TLEN, D), F32),
            pltpu.VMEM((D, FF), BF16),
            pltpu.SemaphoreType.DMA((2 * CHUNKS,)),
            pltpu.SemaphoreType.DMA((16,)),
        ],
        compiler_params=params(48),
        cost_estimate=cost(3 * 2 * TLEN * D * FF * 2, 30e6),
        name="feed_forward",
    )(offs, live, ffn, normed, vec, joined_grad)
    return out[: len(parts)], out[len(parts) :]


def ffn_bwd_kernel(n_parts, offs, ffn, normed, inverse, vec, slope, grad_second, grad_low, *refs):
    parts, refs = refs[:n_parts], refs[n_parts:]
    grad_residual, grad_attended, grads, up, down, total, grad, sems, out_sems = refs

    def load(k):
        return (
            pltpu.make_async_copy(ffn.at[:, pl.ds(k * D, D)], up.at[k % 2], sems.at[k]),
            pltpu.make_async_copy(ffn.at[:, pl.ds(FF + k * D, D)], down.at[k % 2], sems.at[CHUNKS + k]),
        )

    for k in range(2):
        for copy in load(k):
            copy.start()
    first_low = (normed[...] * vec[3:4, :] + vec[4:5, :]).astype(BF16)
    turned = first_low.T
    total[...] = grad_second[...]
    for k in range(CHUNKS):
        for copy in load(k):
            copy.wait()
        inner = (dot(grad_low[...], down[k % 2]) * slope[k].astype(F32)).astype(BF16)
        grads[k : k + 1, :] = jnp.sum(inner.astype(F32), axis=0, keepdims=True)
        total[...] += dot_nt(inner, up[k % 2])
        grad[:, k * D : (k + 1) * D] = dot(turned, inner).astype(BF16)
        if k + 2 < CHUNKS:
            for copy in load(k + 2):
                copy.start()
    upstream = total[...]
    grads[4:5, :] = jnp.sum(upstream * normed[...], axis=0, keepdims=True)
    grads[5:6, :] = jnp.sum(upstream, axis=0, keepdims=True)
    residual = norm_back(upstream, normed[...], inverse[:, 0:1], vec[3:4, :])
    grad_residual[...] = residual
    attended = residual.astype(BF16)
    grad_attended[...] = attended
    grads[6:7, :] = jnp.sum(attended.astype(F32), axis=0, keepdims=True)
    store_blocks(offs, grad, parts, out_sems)


def ffn_bwd(offs, n_blocks, ffn, normed, inverse, vec, slope, grad_second, grad_low):
    parts = grad_shapes(n_blocks, D, FF)
    out = pl.pallas_call(
        functools.partial(ffn_bwd_kernel, len(parts)),
        out_shape=parts
        + [
            jax.ShapeDtypeStruct((TLEN, D), F32),
            jax.ShapeDtypeStruct((TLEN, D), BF16),
            jax.ShapeDtypeStruct((8, D), F32),
        ],
        in_specs=[SMEM, ANY] + [VMEM] * 6,
        out_specs=[ANY] * len(parts) + [VMEM] * 3,
        scratch_shapes=[
            pltpu.VMEM((2, D, D), BF16),
            pltpu.VMEM((2, D, D), BF16),
            pltpu.VMEM((TLEN, D), F32),
            pltpu.VMEM((D, FF), BF16),
            pltpu.SemaphoreType.DMA((2 * CHUNKS,)),
            pltpu.SemaphoreType.DMA((16,)),
        ],
        compiler_params=params(48),
        cost_estimate=cost(3 * 2 * TLEN * D * FF * 2, 30e6),
        name="feed_forward_backward",
    )(offs, ffn, normed, inverse, vec, slope, grad_second, grad_low)
    return out[: len(parts)], out[len(parts) :]


def attn_bwd_kernel(n_blocks, offs, *refs):
    blocks, refs = refs[:n_blocks], refs[n_blocks:]
    (
        grad_attended,
        grad_residual,
        qkv,
        probs,
        ctx,
        bucket,
        grad_qkv,
        grad_input,
        grads,
        grad_table,
        weight,
        grad_ctx,
        grad_ctx_t,
        query_t,
        grad_key_t,
        grad_value_t,
        grad_scores,
        one_hot,
        table_sum,
        sems,
    ) = refs
    step = pl.program_id(0)

    @pl.when(step == 0)
    def _():
        load_blocks(offs, blocks, weight, sems, True)
        load_blocks(offs, blocks, weight, sems, False)
        back = dot_nt(grad_attended[...], weight[:, 3 * D :]).astype(BF16)
        grad_ctx[...] = back
        grad_ctx_t[...] = back.T
        query_t[...] = (qkv[:, :D] * SCALE).T
        grad_key_t[...] = jnp.zeros_like(grad_key_t)
        grad_value_t[...] = jnp.zeros_like(grad_value_t)
        table_sum[...] = jnp.zeros_like(table_sum)

    start = pl.multiple_of(step * ROWS, ROWS)
    rows = pl.ds(start, ROWS)

    def pair_step(pair, carry):
        cols = pl.ds(pl.multiple_of(pair * 128, 128), 128)
        keys = qkv[:, pl.ds(pl.multiple_of(D + pair * 128, 128), 128)]
        values = qkv[:, pl.ds(pl.multiple_of(2 * D + pair * 128, 128), 128)]
        back = grad_ctx[rows, cols]
        context = ctx[rows, cols].astype(F32)
        grad_query = jnp.zeros((ROWS, 128), F32)
        for half in range(2):
            head = pair * 2 + half
            masked = jnp.where(half_mask(ROWS, half), back, jnp.zeros_like(back))
            grad_probs = dot_nt(masked, values)
            delta = jnp.sum(masked.astype(F32) * context, axis=-1, keepdims=True)
            prob = probs[head]
            slopes = (prob.astype(F32) * (grad_probs - delta)).astype(BF16)
            grad_scores[head] = slopes
            near = jnp.where(half_mask(TLEN, half), keys, jnp.zeros_like(keys))
            grad_query = grad_query + dot(slopes, near)
            lines = pl.ds(pl.multiple_of(head * HEAD_DIM, HEAD_DIM), HEAD_DIM)
            grad_key_t[lines, :] += dot(query_t[lines, rows], slopes)
            grad_value_t[lines, :] += dot(grad_ctx_t[lines, rows], prob)
        grad_qkv[rows, cols] = (grad_query * SCALE).astype(BF16)
        return carry

    lax.fori_loop(0, PAIRS, pair_step, 0)

    def table_step(group, carry):
        lines = pl.ds(pl.multiple_of(group * 16, 16), 16)
        which = bucket[lines, :]
        for b in range(BUCKETS):
            one_hot[b * 16 : (b + 1) * 16, :] = jnp.where(which == b, 1.0, 0.0).astype(BF16)
        slopes = grad_scores[:, lines, :].reshape(HEADS * 16, TLEN)
        table_sum[...] += dot_nt(one_hot[...], slopes)
        return carry

    lax.fori_loop(0, ROWS // 16, table_step, 0)

    @pl.when(step == STEPS - 1)
    def _():
        grad_qkv[:, D : 2 * D] = grad_key_t[...].astype(BF16).T
        grad_qkv[:, 2 * D :] = grad_value_t[...].astype(BF16).T
        grads[0:1, :] = jnp.sum(grad_qkv[:, :D].astype(F32), axis=0, keepdims=True)
        grads[1:2, :] = jnp.sum(grad_qkv[:, 2 * D :].astype(F32), axis=0, keepdims=True)
        grad_input[...] = grad_residual[...] + dot_nt(grad_qkv[...], weight[:, : 3 * D])
        line = lax.broadcasted_iota(jnp.int32, (BUCKETS * 16, HEADS * 16), 0) % 16
        lane = lax.broadcasted_iota(jnp.int32, (BUCKETS * 16, HEADS * 16), 1) % 16
        kept = jnp.where(line == lane, table_sum[...], 0.0)
        grad_table[...] = jnp.sum(kept.reshape(BUCKETS, 16, HEADS * 16), axis=1)


def attn_bwd(offs, blocks, grad_attended, grad_residual, qkv, probs, ctx, bucket):
    n = len(blocks)

    def whole(shape):
        return pl.BlockSpec(shape, lambda i: (0,) * len(shape))

    return pl.pallas_call(
        functools.partial(attn_bwd_kernel, n),
        grid=(STEPS,),
        out_shape=[
            jax.ShapeDtypeStruct((TLEN, 3 * D), BF16),
            jax.ShapeDtypeStruct((TLEN, D), F32),
            jax.ShapeDtypeStruct((8, D), F32),
            jax.ShapeDtypeStruct((BUCKETS, HEADS * 16), F32),
        ],
        in_specs=[SMEM]
        + [ANY] * n
        + [
            whole((TLEN, D)),
            whole((TLEN, D)),
            whole((TLEN, 3 * D)),
            pl.BlockSpec((HEADS, ROWS, TLEN), lambda i: (0, i, 0)),
            whole((TLEN, D)),
            pl.BlockSpec((ROWS, TLEN), lambda i: (i, 0)),
        ],
        out_specs=[
            whole((TLEN, 3 * D)),
            whole((TLEN, D)),
            whole((8, D)),
            whole((BUCKETS, HEADS * 16)),
        ],
        scratch_shapes=[
            pltpu.VMEM((D, 4 * D), BF16),
            pltpu.VMEM((TLEN, D), BF16),
            pltpu.VMEM((D, TLEN), BF16),
            pltpu.VMEM((D, TLEN), BF16),
            pltpu.VMEM((D, TLEN), F32),
            pltpu.VMEM((D, TLEN), F32),
            pltpu.VMEM((HEADS, ROWS, TLEN), BF16),
            pltpu.VMEM((BUCKETS * 16, TLEN), BF16),
            pltpu.VMEM((BUCKETS * 16, HEADS * 16), F32),
            pltpu.SemaphoreType.DMA((n,)),
        ],
        compiler_params=params(52),
        cost_estimate=cost(20e9, 20e6),
        name="attention_backward",
    )(offs, *blocks, grad_attended, grad_residual, qkv, probs, ctx, bucket)


def outer_kernel(n_parts, widths, offs, *refs):
    count = len(widths)
    lefts, rights, refs = refs[:count], refs[count : 2 * count], refs[2 * count :]
    parts, (grad, sems) = refs[:n_parts], refs[n_parts:]
    at = 0
    for left, right, width in zip(lefts, rights, widths):
        turned = left[...].astype(BF16).T
        for lo in range(0, width, D):
            grad[:, at + lo : at + lo + D] = dot(turned, right[:, lo : lo + D]).astype(BF16)
        at += width
    store_blocks(offs, grad, parts, sems)


def outer(offs, n_blocks, lefts, rights):
    widths = tuple(right.shape[1] for right in rights)
    rows = lefts[0].shape[1]
    parts = grad_shapes(n_blocks, rows, sum(widths))
    out = pl.pallas_call(
        functools.partial(outer_kernel, len(parts), widths),
        out_shape=parts,
        in_specs=[SMEM] + [VMEM] * (2 * len(widths)),
        out_specs=[ANY] * len(parts),
        scratch_shapes=[
            pltpu.VMEM((rows, sum(widths)), BF16),
            pltpu.SemaphoreType.DMA((16,)),
        ],
        compiler_params=params(40),
        cost_estimate=cost(2 * TLEN * rows * sum(widths) * 2, 12e6),
        name="weight_gradient",
    )(offs, *lefts, *rights)
    return list(out)


def nesterov(weight, moment, average, gradient, rate):
    moment_new = MOMENTUM * moment + gradient
    weight_new = weight - rate * (gradient + MOMENTUM * moment_new)
    return (weight_new, moment_new, AVERAGE * average + (1.0 - AVERAGE) * weight_new)


def merge_stats(pre, mask, count):
    safe = jnp.maximum(count, 1.0)
    mean = jnp.sum(pre * mask, axis=0) / safe
    centre = (pre - mean) * mask
    stats = jnp.stack([mean, jnp.sum(centre * centre, axis=0), jnp.full((D,), count, F32)])
    bit = 1
    while bit < lax.axis_size("batch"):
        other = swap(stats, bit)
        n_here, n_there = stats[2], other[2]
        total = n_here + n_there
        safe = jnp.maximum(total, 1.0)
        gap = other[0] - stats[0]
        stats = jnp.stack(
            [
                (stats[0] * n_here + other[0] * n_there) / safe,
                stats[1] + other[1] + gap * gap * (n_here * n_there / safe),
                total,
            ]
        )
        bit *= 2
    return stats[0], stats[1] / stats[2], stats[2]


def on_device(
    text_embed,
    visual_maps,
    visual_bucket,
    rel_bucket,
    joined_grad,
    attn_weight,
    attn_moment,
    attn_average,
    ffn_weight,
    ffn_moment,
    ffn_average,
    vector_weight,
    vector_moment,
    vector_average,
    project_weight,
    project_moment,
    project_average,
    shared_weight,
    shared_moment,
    shared_average,
):
    n_batch = lax.axis_size("batch")
    me = lax.axis_index("batch")
    ringed = n_batch == 16
    is_text = lax.axis_index("stream") == 0
    maps = visual_maps.reshape(TLEN, -1)

    attn_low = attn_weight[0].astype(BF16)
    ffn_low = ffn_weight[0].astype(BF16)
    small = jnp.zeros((16, D), BF16)
    small = small.at[0, : vector_weight.shape[1]].set(vector_weight[0].astype(BF16))
    small = small.at[1, : shared_weight.shape[0]].set(shared_weight.astype(BF16))
    if ringed:
        sources = jnp.asarray(gather_sources())[me]
        targets = jnp.asarray(scatter_targets())[me]
        project_blocks = ring_gather(
            jnp.concatenate([project_weight.astype(BF16), small], axis=0)
        )
        attn_blocks = ring_gather(attn_low)
        n_blocks = 16
    else:
        sources = jnp.zeros((1,), jnp.int32)
        targets = jnp.zeros((1,), jnp.int32)
        rows = lax.all_gather(project_weight.astype(BF16), "batch", axis=0, tiled=True)
        project_blocks = [jnp.concatenate([rows, jnp.zeros((16, D), BF16)], axis=0)]
        attn_blocks = [lax.all_gather(attn_low, "batch", axis=0, tiled=True)]
        n_blocks = 1
    ffn_full = lax.all_gather(ffn_low, "batch", axis=0, tiled=True)
    project_offs = sources
    attn_offs = sources * attn_low.shape[0]
    weight_offs = targets * attn_low.shape[0]
    project_grad_offs = targets * project_weight.shape[0]

    partial_pre, project_half, small_all = project(project_offs, maps, project_blocks)
    if not ringed:
        small_all = lax.all_gather(small, "batch", axis=0, tiled=False)
    vector_rows = (
        small_all[:, 0, : vector_weight.shape[1]].reshape(12, D).astype(F32)
    )
    vec = jnp.concatenate([vector_rows, jnp.zeros((4, D), F32)], axis=0)
    shared_full = small_all[:, 1, : shared_weight.shape[0]].reshape(-1).astype(F32)
    table = jnp.zeros((16, 128), F32)
    table = table.at[:HEADS, :BUCKETS].set(
        shared_full[: BUCKETS * HEADS].reshape(BUCKETS, HEADS).T
    )
    bn_gain = shared_full[BUCKETS * HEADS : BUCKETS * HEADS + D]
    bn_shift = shared_full[BUCKETS * HEADS + D :]

    pre = (partial_pre + across(partial_pre)).astype(F32)
    visual_len = ((visual_bucket + 1) * (TLEN // 2)).astype(jnp.int32)
    positions = jnp.arange(TLEN, dtype=jnp.int32)
    visual_mask = (positions < visual_len[0]).astype(F32)[:, None]
    mean, variance, total_count = merge_stats(pre, visual_mask, visual_len[0].astype(F32))
    inverse_std = lax.rsqrt(variance + EPS)
    normed_pre = (pre - mean) * inverse_std
    bn_out = (normed_pre * bn_gain + bn_shift) * visual_mask
    live = jnp.where(is_text, TLEN, visual_len)
    x_input = jnp.where(is_text, text_embed.reshape(TLEN, D).astype(F32), bn_out)
    bucket = rel_bucket.reshape(TLEN, TLEN)

    qkv, probs, ctx, normed, inverse = attn_fwd(
        attn_offs, live, attn_blocks, x_input, bucket, table, vec
    )
    down_parts, (result, slope, grad_second, grad_low, grads_two) = ffn_fwd(
        weight_offs, n_blocks, live, ffn_full, normed, vec, joined_grad.reshape(TLEN, D)
    )
    joined = result + across(result)
    down_grad = reduce_grad(down_parts)
    up_parts, (grad_residual, grad_attended, grads_one) = ffn_bwd(
        weight_offs, n_blocks, ffn_full, normed, inverse, vec, slope, grad_second, grad_low
    )
    up_grad = reduce_grad(up_parts)
    grad_qkv, grad_input, grads_zero, grad_table = attn_bwd(
        attn_offs, attn_blocks, grad_attended, grad_residual, qkv, probs, ctx, bucket
    )

    grad_bn = jnp.where(is_text, 0.0, grad_input) * visual_mask
    grad_bn_low = grad_bn.astype(BF16)
    grad_bn_both = (grad_bn_low + across(grad_bn_low)).astype(F32)
    table_row = jnp.sum(grad_table.reshape(BUCKETS, HEADS, 16), axis=-1).reshape(1, -1)
    sums = jnp.concatenate(
        [
            grads_zero[0:2],
            grads_one[6:7],
            grads_one[4:6],
            grads_one[0:4],
            grads_two[0:3],
            jnp.sum(grad_bn * normed_pre, axis=0)[None],
            jnp.sum(grad_bn, axis=0)[None],
            jnp.pad(table_row, ((0, 0), (0, D - BUCKETS * HEADS))),
            jnp.zeros((1, D), F32),
        ],
        axis=0,
    )
    bit = 1
    while bit < n_batch:
        sums = sums + swap(sums, bit)
        bit *= 2
    shared_sums = sums[12:]
    shared_sums = shared_sums + across(shared_sums)
    total_gain, total_shift = shared_sums[0], shared_sums[1]
    shared_grad = jnp.concatenate([shared_sums[2, : BUCKETS * HEADS], total_gain, total_shift])

    attn_parts = outer(weight_offs, n_blocks, [x_input, ctx], [grad_qkv, grad_attended])
    attn_grad = reduce_grad(attn_parts)

    grad_pre = (
        visual_mask
        * inverse_std
        * bn_gain
        * (grad_bn_both - total_shift / total_count - normed_pre * (total_gain / total_count))
    ).astype(BF16)
    project_grad = reduce_grad(outer(project_grad_offs, n_blocks, [maps], [grad_pre]))
    grad_maps = dot_nt(grad_pre, project_half)

    all_tokens = n_batch * TLEN
    rate_attention = 1.5 / math.sqrt(D * all_tokens)
    rate_matrix = 0.6 / math.sqrt(D * all_tokens)
    rate_vector = 0.12 / math.sqrt(all_tokens)
    ffn_grad = jnp.concatenate([up_grad, down_grad], axis=1)[None]
    ffn_new = nesterov(ffn_weight, ffn_moment, ffn_average, ffn_grad, rate_matrix)
    attn_new = nesterov(attn_weight, attn_moment, attn_average, attn_grad[None], rate_attention)
    width = vector_weight.shape[1]
    vector_grad = lax.dynamic_slice(sums[:12].reshape(-1), (me * width,), (width,))[None]
    vector_new = nesterov(vector_weight, vector_moment, vector_average, vector_grad, rate_vector)
    project_new = nesterov(
        project_weight, project_moment, project_average, project_grad, rate_matrix
    )
    width = shared_weight.shape[0]
    own_shared = lax.dynamic_slice(shared_grad, (me * width,), (width,))
    shared_new = nesterov(shared_weight, shared_moment, shared_average, own_shared, rate_vector)
    return (
        joined.reshape(1, TLEN, D),
        grad_input.reshape(1, 1, TLEN, D),
        grad_maps.reshape(1, TLEN, -1),
        attn_new[0],
        attn_new[1],
        attn_new[2],
        ffn_new[0],
        ffn_new[1],
        ffn_new[2],
        vector_new[0],
        vector_new[1],
        vector_new[2],
        project_new[0],
        project_new[1],
        project_new[2],
        shared_new[0],
        shared_new[1],
        shared_new[2],
    )


def solution(mesh):
    return jax.shard_map(
        on_device,
        mesh=mesh,
        in_specs=(
            P("batch", None, None),
            P("batch", None, "stream"),
            P("batch"),
            P("stream", "batch", None, None),
            P("batch", None, None),
            P("stream", "batch", None),
            P("stream", "batch", None),
            P("stream", "batch", None),
            P("stream", "batch", None),
            P("stream", "batch", None),
            P("stream", "batch", None),
            P("stream", "batch"),
            P("stream", "batch"),
            P("stream", "batch"),
            P(("stream", "batch"), None),
            P(("stream", "batch"), None),
            P(("stream", "batch"), None),
            P("batch"),
            P("batch"),
            P("batch"),
        ),
        out_specs=(
            P("batch", None, None),
            P("stream", "batch", None, None),
            P("batch", None, "stream"),
            P("stream", "batch", None),
            P("stream", "batch", None),
            P("stream", "batch", None),
            P("stream", "batch", None),
            P("stream", "batch", None),
            P("stream", "batch", None),
            P("stream", "batch"),
            P("stream", "batch"),
            P("stream", "batch"),
            P(("stream", "batch"), None),
            P(("stream", "batch"), None),
            P(("stream", "batch"), None),
            P("batch"),
            P("batch"),
            P("batch"),
        ),
        check_vma=False,
    )
```

```python
import functools
import math

import jax
import jax.numpy as jnp
import numpy as np
from jax import lax
from jax.experimental import pallas as pl
from jax.experimental.pallas import tpu as pltpu
from jax.sharding import PartitionSpec as P

D = 768
HEADS = 12
HEAD_DIM = 64
FF = 3072
TLEN = 512
BUCKETS = 32
PAIRS = HEADS // 2
ROWS = 128
SOFT = 128
STEPS = TLEN // ROWS
CHUNKS = FF // D

EPS = 1e-05
MOMENTUM = 0.9
AVERAGE = 0.95
SCALE = HEAD_DIM ** (-0.5)

BF16 = jnp.bfloat16
F32 = jnp.float32
ANY = pl.BlockSpec(memory_space=pl.ANY)
SMEM = pl.BlockSpec(memory_space=pltpu.SMEM)
VMEM = pl.BlockSpec(memory_space=pltpu.VMEM)
MIB = 1024 * 1024

CYCLE = ((0, 0), (1, 0), (2, 0), (3, 0), (3, 1), (2, 1), (1, 1), (0, 1))
CHIP = [z * 2 + y for z, y in CYCLE]
PLACE = [CHIP.index(k) for k in range(8)]


def cycle_perm(shift):
    return [
        (CHIP[r] * 2 + c, CHIP[(r + shift) % 8] * 2 + c) for r in range(8) for c in range(2)
    ]


def across(v):
    return lax.ppermute(v, "stream", [(0, 1), (1, 0)])


def swap(v, bit):
    n = lax.axis_size("batch")
    return lax.ppermute(v, "batch", [(i, i ^ bit) for i in range(n)])


def gather_shifts():
    return [0, -1, 1, -2, 2, -3, 3, -4]


def gather_sources():
    table = np.zeros((16, 16), np.int32)
    for b in range(16):
        place, core = PLACE[b // 2], b % 2
        for slot, shift in enumerate(gather_shifts()):
            chip = CHIP[(place + shift) % 8]
            table[b, slot] = chip * 2 + core
            table[b, 8 + slot] = chip * 2 + 1 - core
    return table


def scatter_targets():
    table = np.zeros((16, 16), np.int32)
    for b in range(16):
        place, core = PLACE[b // 2], b % 2
        for ahead in range(8):
            chip = CHIP[(place + ahead) % 8]
            table[b, ahead] = chip * 2 + core
            table[b, 8 + ahead] = chip * 2 + 1 - core
    return table


def ring_gather(block, split=0):
    up, down = cycle_perm(1), cycle_perm(-1)
    low = high = block
    own = [block]
    for _ in range(3):
        low = lax.ppermute(low, "batch", up)
        high = lax.ppermute(high, "batch", down)
        own += [low, high]
    if split:
        own.append(lax.ppermute(low[:, :split], "batch", up))
        own.append(lax.ppermute(high[:, split:], "batch", down))
    else:
        own.append(lax.ppermute(low, "batch", up))
    return own + [swap(v, 1) for v in own]


def ring_scatter(mine, theirs):
    up, down = cycle_perm(1), cycle_perm(-1)
    other = swap(theirs, 1)

    def term(j):
        return mine[j].astype(F32) + other[j].astype(F32)

    def passed(v, j):
        return (v.astype(F32) + term(j)).astype(BF16)

    low = lax.ppermute(term(4).astype(BF16), "batch", up)
    high = lax.ppermute(term(5).astype(BF16), "batch", down)
    steps = [[other], [low, high]]
    for ahead in (3, 2):
        low = lax.ppermute(passed(low, ahead), "batch", up)
        high = lax.ppermute(passed(high, 9 - ahead), "batch", down)
        steps.append([low, high])
    low = lax.ppermute(passed(low, 1), "batch", up)
    return low.astype(F32) + high.astype(F32) + term(0), steps


def reduce_grad(parts):
    if len(parts) == 1:
        total = lax.psum_scatter(parts[0][0], "batch", scatter_dimension=0, tiled=True)
        return total, [[]] * 4
    return ring_scatter(parts[0], parts[1])


def dot(left, right):
    return jnp.dot(left, right, preferred_element_type=F32)


def dot_nt(left, right):
    return lax.dot_general(left, right, (((1,), (1,)), ((), ())), preferred_element_type=F32)


def store_blocks(offs, src, parts, sems, extra=None, extra_sems=None):
    copies = []
    if len(parts) == 1:
        copies.append(pltpu.make_async_copy(src, parts[0].at[0], sems.at[0]))
    else:
        rows = src.shape[0] // 16
        for k in range(16):
            place = parts[k // 8].at[k % 8]
            at = pl.multiple_of(offs[k] * rows, 16)
            copies.append(
                pltpu.make_async_copy(src.at[pl.ds(at, rows), :], place.at[pl.ds(0, rows), :], sems.at[k])
            )
            if extra is not None:
                copies.append(
                    pltpu.make_async_copy(
                        extra.at[offs[k]], place.at[pl.ds(rows, 16), :], extra_sems.at[k]
                    )
                )
    for copy in copies:
        copy.start()
    return copies


def grad_shapes(n_blocks, rows, cols, extra=0):
    if n_blocks == 1:
        return [jax.ShapeDtypeStruct((1, rows, cols), BF16)]
    return [jax.ShapeDtypeStruct((8, rows // 16 + extra, cols), BF16)] * 2


def params(mib):
    return pltpu.CompilerParams(vmem_limit_bytes=mib * MIB)


def cost(micros):
    return pl.CostEstimate(flops=int(micros * 1e9), bytes_accessed=0, transcendentals=0)


def norm_rows(values):
    centre = values - jnp.mean(values, axis=-1, keepdims=True)
    inverse = lax.rsqrt(jnp.mean(centre * centre, axis=-1, keepdims=True) + EPS)
    return centre * inverse, inverse


def norm_back(upstream, normed, inverse, gain):
    scaled = upstream * gain
    return inverse * (
        scaled
        - jnp.mean(scaled, axis=-1, keepdims=True)
        - normed * jnp.mean(scaled * normed, axis=-1, keepdims=True)
    )


def half_mask(rows, half):
    lane = lax.broadcasted_iota(jnp.int32, (rows, 128), 1)
    return (lane < HEAD_DIM) if half == 0 else (lane >= HEAD_DIM)


def round_kernel(n_after, weight, *refs):
    refs[n_after][...] = weight[...].astype(BF16)


def rounded(weight, after):
    return pl.pallas_call(
        functools.partial(round_kernel, len(after)),
        out_shape=jax.ShapeDtypeStruct(weight.shape, BF16),
        in_specs=[VMEM] + [ANY] * len(after),
        out_specs=VMEM,
        compiler_params=params(60),
        cost_estimate=cost(1),
        name="round_weight",
    )(weight, *after)


def project_kernel(n_blocks, offs, maps, blocks, pre, whole, small, sems, small_sems):
    copies = []
    rows = whole.shape[0] // n_blocks
    for i in range(n_blocks):
        block = blocks.at[i]
        which = offs[i] if n_blocks > 1 else 0
        at = pl.multiple_of(which * rows, 16)
        copies.append(
            pltpu.make_async_copy(block.at[pl.ds(0, rows), :], whole.at[pl.ds(at, rows), :], sems.at[i])
        )
        copies.append(
            pltpu.make_async_copy(block.at[pl.ds(rows, 16), :], small.at[which], small_sems.at[i])
        )
    for copy in copies:
        copy.start()
    for copy in copies:
        copy.wait()
    for i in range(2):
        pick = pl.ds(i * (TLEN // 2), TLEN // 2)
        pre[pick, :] = dot(maps[pick, :], whole[...]).astype(BF16)


def project(offs, maps, blocks):
    n = blocks.shape[0]
    rows = blocks.shape[1] - 16
    channels = n * rows
    return pl.pallas_call(
        functools.partial(project_kernel, n),
        out_shape=[
            jax.ShapeDtypeStruct((TLEN, D), BF16),
            jax.ShapeDtypeStruct((channels, D), BF16),
            jax.ShapeDtypeStruct((n, 16, D), BF16),
        ],
        in_specs=[SMEM, VMEM, ANY],
        out_specs=[VMEM] * 3,
        scratch_shapes=[pltpu.SemaphoreType.DMA((n,)), pltpu.SemaphoreType.DMA((n,))],
        compiler_params=params(60),
        cost_estimate=cost(60),
        name="project_maps",
    )(offs, maps, blocks)


def bias_kernel(n_after, bucket, table, *refs):
    bias = refs[n_after]
    for t in range(TLEN // 128):
        lanes = slice(t * 128, (t + 1) * 128)
        which = bucket[:, lanes]
        for head in range(HEADS):
            row = jnp.broadcast_to(table[head : head + 1, :], which.shape)
            bias[head, :, lanes] = jnp.take_along_axis(row, which, axis=1).astype(BF16)


def spatial_bias(bucket, table, after):
    rows = 64
    return pl.pallas_call(
        functools.partial(bias_kernel, len(after)),
        grid=(TLEN // rows,),
        out_shape=jax.ShapeDtypeStruct((HEADS, TLEN, TLEN), BF16),
        in_specs=[
            pl.BlockSpec((rows, TLEN), lambda i: (i, 0)),
            pl.BlockSpec((16, 128), lambda i: (0, 0)),
        ]
        + [ANY] * len(after),
        out_specs=pl.BlockSpec((HEADS, rows, TLEN), lambda i: (0, i, 0)),
        compiler_params=params(60),
        cost_estimate=cost(60),
        name="spatial_bias",
    )(bucket, table, *after)


def attn_fwd_kernel(n_after, live, attn, bias, text, pre, bn, vec, *refs):
    qkv_out, probs, x_out, query_t, ctx, normed, inverse = refs[n_after : n_after + 7]
    weight, qkv, score_a, score_b, prob_a, prob_b, ctx_a, sems, in_sems, out_sems = refs[n_after + 7 :]
    loads = []
    for part in range(4):
        cols = pl.ds(part * D, D)
        loads.append(pltpu.make_async_copy(attn.at[:, cols], weight.at[:, cols], sems.at[part]))
        loads[-1].start()

    def bring(head):
        place = (prob_a, prob_b)[head % 2].at[head // 2]
        return pltpu.make_async_copy(bias.at[head], place, in_sems.at[head])

    for head in range(HEADS):
        bring(head).start()
    alive = lax.broadcasted_iota(jnp.int32, (TLEN, 1), 0) < live[0]
    visual = (pre[...] - bn[0:1, :]) * bn[1:2, :] * bn[2:3, :] + bn[3:4, :]
    x = jnp.where(live[1] == 1, text[...].astype(F32), jnp.where(alive, visual, 0.0))
    x_low = x.astype(BF16)
    x_out[...] = x_low
    exports = []
    for part in range(3):
        cols = slice(part * D, (part + 1) * D)
        loads[part].wait()
        value = dot(x_low, weight[:, cols])
        if part != 1:
            value = value + vec[part // 2 : part // 2 + 1, :]
        qkv[:, cols] = value.astype(BF16)
        exports.append(
            pltpu.make_async_copy(qkv.at[:, cols], qkv_out.at[:, cols], out_sems.at[HEADS + part])
        )
        exports[-1].start()

    def lanes(start, pair):
        return pl.ds(pl.multiple_of(start + pair * 128, 128), 128)

    def scores(pair, half, out):
        query = qkv[:, lanes(0, pair)] * SCALE
        query = jnp.where(half_mask(TLEN, half), query, jnp.zeros_like(query))
        out[...] = dot_nt(query, qkv[:, lanes(D, pair)])

    def softmax(score, prob, pair):
        key_valid = lax.broadcasted_iota(jnp.int32, (SOFT, TLEN), 1) < live[0]
        for i in range(TLEN // SOFT):
            rows = slice(i * SOFT, (i + 1) * SOFT)
            value = score[rows, :] + prob[pair, rows, :].astype(F32)
            value = jnp.where(key_valid, value, -1000000000.0)
            peak = jnp.max(value, axis=-1, keepdims=True)
            raised = jnp.exp(value - peak)
            total = jnp.sum(raised, axis=-1, keepdims=True)
            prob[pair, rows, :] = (raised * (1.0 / total)).astype(BF16)

    scores(0, 0, score_a)
    for head in range(HEADS):
        bring(head).wait()

    def step(pair, carry):
        values = qkv[:, lanes(2 * D, pair)]
        scores(pair, 1, score_b)
        softmax(score_a, prob_a, pair)
        scores(jnp.minimum(pair + 1, PAIRS - 1), 0, score_a)
        ctx_a[...] = dot(prob_a[pair], values)
        softmax(score_b, prob_b, pair)
        ctx_b = dot(prob_b[pair], values)
        ctx[:, lanes(0, pair)] = jnp.where(half_mask(TLEN, 0), ctx_a[...], ctx_b).astype(BF16)
        for half, prob in enumerate((prob_a, prob_b)):
            head = 2 * pair + half
            pltpu.make_async_copy(prob.at[pair], probs.at[head], out_sems.at[head]).start()
        return carry

    lax.fori_loop(0, PAIRS, step, 0)
    loads[3].wait()
    att = dot(ctx[...], weight[:, 3 * D :]) + vec[2:3, :]
    query_t[...] = (qkv[:, :D] * SCALE).T
    normal, inv = norm_rows(x + att)
    normed[...] = normal
    inverse[...] = jnp.broadcast_to(inv, (TLEN, 128))
    for copy in exports:
        copy.wait()
    for head in range(HEADS):
        prob = (prob_a, prob_b)[head % 2]
        pltpu.make_async_copy(prob.at[head // 2], probs.at[head], out_sems.at[head]).wait()


def attn_fwd(live, attn, bias, text, pre, bn, vec, after):
    return pl.pallas_call(
        functools.partial(attn_fwd_kernel, len(after)),
        out_shape=[
            jax.ShapeDtypeStruct((TLEN, 3 * D), BF16),
            jax.ShapeDtypeStruct((HEADS, TLEN, TLEN), BF16),
            jax.ShapeDtypeStruct((TLEN, D), BF16),
            jax.ShapeDtypeStruct((D, TLEN), BF16),
            jax.ShapeDtypeStruct((TLEN, D), BF16),
            jax.ShapeDtypeStruct((TLEN, D), F32),
            jax.ShapeDtypeStruct((TLEN, 128), F32),
        ],
        in_specs=[SMEM, ANY, ANY] + [VMEM] * 4 + [ANY] * len(after),
        out_specs=[ANY, ANY] + [VMEM] * 5,
        scratch_shapes=[
            pltpu.VMEM((D, 4 * D), BF16),
            pltpu.VMEM((TLEN, 3 * D), BF16),
            pltpu.VMEM((TLEN, TLEN), F32),
            pltpu.VMEM((TLEN, TLEN), F32),
            pltpu.VMEM((PAIRS, TLEN, TLEN), BF16),
            pltpu.VMEM((PAIRS, TLEN, TLEN), BF16),
            pltpu.VMEM((TLEN, 128), F32),
            pltpu.SemaphoreType.DMA((4,)),
            pltpu.SemaphoreType.DMA((HEADS,)),
            pltpu.SemaphoreType.DMA((HEADS + 3,)),
        ],
        compiler_params=params(60),
        cost_estimate=cost(15),
        name="attention_forward",
    )(live, attn, bias, text, pre, bn, vec, *after)


def load_ffn(offs, blocks, up, down, sems):
    first, second = [], []
    if len(blocks) == 1:
        first.append(pltpu.make_async_copy(blocks[0].at[:, pl.ds(0, FF)], up, sems.at[0]))
        second.append(pltpu.make_async_copy(blocks[0].at[:, pl.ds(FF, FF)], down, sems.at[1]))
        return first, second
    at = 0
    for slot in range(16):
        rows = pl.ds(pl.multiple_of(offs[slot] * 48, 16), 48)
        if slot % 8 < 7:
            left, right = blocks[at].at[:, pl.ds(0, FF)], blocks[at].at[:, pl.ds(FF, FF)]
            at += 1
        else:
            left, right = blocks[at], blocks[at + 1]
            at += 2
        first.append(pltpu.make_async_copy(left, up.at[rows, :], sems.at[2 * slot]))
        second.append(pltpu.make_async_copy(right, down.at[rows, :], sems.at[2 * slot + 1]))
    return first, second


def ffn_fwd_kernel(n_blocks, live, offs, normed, vec, joined_grad, *refs):
    blocks, refs = refs[:n_blocks], refs[n_blocks:]
    part, slope, result, grad_second, grad_low, grads = refs[:6]
    up, down, active, bend_out, sems, out_sems = refs[6:]
    loads = load_ffn(offs, blocks, up, down, sems)
    for copy in loads[0] + loads[1]:
        copy.start()
    sends = []
    first = normed[...] * vec[3:4, :] + vec[4:5, :]
    first_low = first.astype(BF16)
    for copy in loads[0]:
        copy.wait()
    units = dot(first_low, up[:, :D])
    total = first + vec[9:10, :]
    for k in range(CHUNKS):
        units = units + vec[5 + k : 6 + k, :]
        if k + 1 < CHUNKS:
            following = dot(first_low, up[:, (k + 1) * D : (k + 2) * D])
        square = units * units
        root = math.sqrt(2.0 / math.pi)
        bend = jnp.tanh(root * units * (1.0 + 0.044715 * square))
        half = 0.5 * (1.0 + bend)
        active[k] = (units * half).astype(BF16)
        bend_out[k] = (
            half + 0.5 * root * units * (1.0 - bend * bend) * (1.0 + 3.0 * 0.044715 * square)
        ).astype(BF16)
        sends.append(pltpu.make_async_copy(bend_out.at[k], slope.at[k], out_sems.at[k]))
        sends[-1].start()
        if k == 0:
            for copy in loads[1]:
                copy.wait()
        total = total + dot_nt(active[k], down[:, k * D : (k + 1) * D])
        if k + 1 < CHUNKS:
            units = following
    normal, inv = norm_rows(total)
    mask = lax.broadcasted_iota(jnp.int32, (TLEN, 1), 0) < live[0]
    upstream = jnp.where(mask, joined_grad[...].astype(F32), 0.0)
    second = norm_back(upstream, normal, inv, vec[10:11, :])
    second_low = second.astype(BF16)
    turned = second_low.T
    for k in range(CHUNKS):
        cols = pl.ds(k * D, D)
        up[:, k * D : (k + 1) * D] = dot(turned, active[k]).astype(BF16)
        sends.append(
            pltpu.make_async_copy(up.at[:, cols], part.at[0, :, cols], out_sems.at[CHUNKS + k])
        )
        sends[-1].start()
    result[...] = jnp.where(mask, normal * vec[10:11, :] + vec[11:12, :], 0.0).astype(BF16)
    grad_second[...] = second
    grad_low[...] = second_low
    grads[0:1, :] = jnp.sum(second_low.astype(F32), axis=0, keepdims=True)
    grads[1:2, :] = jnp.sum(upstream * normal, axis=0, keepdims=True)
    grads[2:3, :] = jnp.sum(upstream, axis=0, keepdims=True)
    for copy in sends:
        copy.wait()


def ffn_fwd(live, offs, blocks, normed, vec, joined_grad):
    n = len(blocks)
    out = pl.pallas_call(
        functools.partial(ffn_fwd_kernel, n),
        out_shape=[
            jax.ShapeDtypeStruct((1, D, FF), BF16),
            jax.ShapeDtypeStruct((CHUNKS, TLEN, D), BF16),
            jax.ShapeDtypeStruct((TLEN, D), BF16),
            jax.ShapeDtypeStruct((TLEN, D), F32),
            jax.ShapeDtypeStruct((TLEN, D), BF16),
            jax.ShapeDtypeStruct((8, D), F32),
        ],
        in_specs=[SMEM, SMEM, VMEM, VMEM, VMEM] + [ANY] * n,
        out_specs=[ANY, ANY] + [VMEM] * 4,
        scratch_shapes=[
            pltpu.VMEM((D, FF), BF16),
            pltpu.VMEM((D, FF), BF16),
            pltpu.VMEM((CHUNKS, TLEN, D), BF16),
            pltpu.VMEM((CHUNKS, TLEN, D), BF16),
            pltpu.SemaphoreType.DMA((32,)),
            pltpu.SemaphoreType.DMA((2 * CHUNKS,)),
        ],
        compiler_params=params(60),
        cost_estimate=cost(15),
        name="feed_forward",
    )(live, offs, normed, vec, joined_grad, *blocks)
    return out[0], out[1:]


def ffn_bwd_kernel(
    n_parts, n_blocks, places, offs, attn, normed, inverse, vec, slope, grad_second, grad_low, *refs
):
    blocks, refs = refs[:n_blocks], refs[n_blocks:]
    parts, refs = refs[:n_parts], refs[n_parts:]
    grad_residual, grad_attended, grads, grad_ctx, grad_ctx_t = refs[:5]
    up, down, total, grad, weight, sems, out_sems, weight_sems = refs[5:]
    loads = load_ffn(offs, blocks, up, down, sems)
    for copy in loads[1] + loads[0]:
        copy.start()
    last = pltpu.make_async_copy(attn.at[:, pl.ds(3 * D, D)], weight, weight_sems.at[0])
    last.start()
    first_low = (normed[...] * vec[3:4, :] + vec[4:5, :]).astype(BF16)
    turned = first_low.T
    total[...] = grad_second[...]
    for k in range(CHUNKS):
        cols = slice(k * D, (k + 1) * D)
        if k == 0:
            for copy in loads[1]:
                copy.wait()
        inner = (dot(grad_low[...], down[:, cols]) * slope[k].astype(F32)).astype(BF16)
        grads[k : k + 1, :] = jnp.sum(inner.astype(F32), axis=0, keepdims=True)
        if k == 0:
            for copy in loads[0]:
                copy.wait()
        total[...] += dot_nt(inner, up[:, cols])
        grad[:, k * D : (k + 1) * D] = dot(turned, inner).astype(BF16)
    upstream = total[...]
    grads[4:5, :] = jnp.sum(upstream * normed[...], axis=0, keepdims=True)
    grads[5:6, :] = jnp.sum(upstream, axis=0, keepdims=True)
    residual = norm_back(upstream, normed[...], inverse[:, 0:1], vec[3:4, :])
    grad_residual[...] = residual
    attended = residual.astype(BF16)
    grad_attended[...] = attended
    grads[6:7, :] = jnp.sum(attended.astype(F32), axis=0, keepdims=True)
    copies = store_blocks(places, grad, parts, out_sems)
    last.wait()
    back = dot_nt(attended, weight[...]).astype(BF16)
    grad_ctx[...] = back
    grad_ctx_t[...] = back.T
    for copy in copies:
        copy.wait()


def ffn_bwd(places, offs, blocks, attn, normed, inverse, vec, slope, grad_second, grad_low):
    n = len(blocks)
    parts = grad_shapes(n, D, FF)
    out = pl.pallas_call(
        functools.partial(ffn_bwd_kernel, len(parts), n),
        out_shape=parts
        + [
            jax.ShapeDtypeStruct((TLEN, D), F32),
            jax.ShapeDtypeStruct((TLEN, D), BF16),
            jax.ShapeDtypeStruct((8, D), F32),
            jax.ShapeDtypeStruct((TLEN, D), BF16),
            jax.ShapeDtypeStruct((D, TLEN), BF16),
        ],
        in_specs=[SMEM, SMEM, ANY] + [VMEM] * 6 + [ANY] * n,
        out_specs=[ANY] * len(parts) + [VMEM] * 5,
        scratch_shapes=[
            pltpu.VMEM((D, FF), BF16),
            pltpu.VMEM((D, FF), BF16),
            pltpu.VMEM((TLEN, D), F32),
            pltpu.VMEM((D, FF), BF16),
            pltpu.VMEM((D, D), BF16),
            pltpu.SemaphoreType.DMA((32,)),
            pltpu.SemaphoreType.DMA((16,)),
            pltpu.SemaphoreType.DMA((1,)),
        ],
        compiler_params=params(60),
        cost_estimate=cost(15),
        name="feed_forward_backward",
    )(places, offs, attn, normed, inverse, vec, slope, grad_second, grad_low, *blocks)
    return out[: len(parts)], out[len(parts) :]


def pairs_kernel(n_after, keys, values, back, context, back_t, query_t, probs, *refs):
    grad_query, grad_key_t, grad_value_t, grad_scores = refs[n_after:]
    total = jnp.zeros((TLEN, 128), F32)
    for half in range(2):
        mask = half_mask(TLEN, half)
        masked = jnp.where(mask, back[...], jnp.zeros_like(back[...]))
        prob = probs[half]
        slopes = dot_nt(masked, values[...])
        delta = jnp.sum(masked.astype(F32) * context[...].astype(F32), axis=-1, keepdims=True)
        slopes = (prob.astype(F32) * (slopes - delta)).astype(BF16)
        grad_scores[half] = slopes
        near = jnp.where(mask, keys[...], jnp.zeros_like(keys[...]))
        total = total + dot(slopes, near)
        lines = slice(half * HEAD_DIM, (half + 1) * HEAD_DIM)
        grad_key_t[lines, :] = dot(query_t[lines, :], slopes).astype(BF16)
        grad_value_t[lines, :] = dot(back_t[lines, :], prob).astype(BF16)
    grad_query[...] = (total * SCALE).astype(BF16)


def attn_bwd_pairs(first, count, qkv, grad_ctx, ctx, grad_ctx_t, query_t, probs, after):
    def cols(base):
        return pl.BlockSpec((TLEN, 128), lambda i: (0, base + i))

    def lines(base):
        return pl.BlockSpec((128, TLEN), lambda i: (base + i, 0))

    def heads(base):
        return pl.BlockSpec((2, TLEN, TLEN), lambda i: (base + i, 0, 0))

    return pl.pallas_call(
        functools.partial(pairs_kernel, len(after)),
        grid=(count,),
        out_shape=[
            jax.ShapeDtypeStruct((TLEN, 128 * count), BF16),
            jax.ShapeDtypeStruct((128 * count, TLEN), BF16),
            jax.ShapeDtypeStruct((128 * count, TLEN), BF16),
            jax.ShapeDtypeStruct((2 * count, TLEN, TLEN), BF16),
        ],
        in_specs=[
            cols(PAIRS + first),
            cols(2 * PAIRS + first),
            cols(first),
            cols(first),
            lines(first),
            lines(first),
            heads(first),
        ]
        + [ANY] * len(after),
        out_specs=[cols(0), lines(0), lines(0), heads(0)],
        compiler_params=params(60),
        cost_estimate=cost(1.5 * count),
        name="attention_backward",
    )(qkv, qkv, grad_ctx, ctx, grad_ctx_t, query_t, probs, *after)


def input_kernel(n_parts, n_after, live, attn, grads_two, grads_one, grad_residual, pre, bn, *refs):
    queries, refs = refs[:n_parts], refs[n_parts:]
    keys_t, refs = refs[:n_parts], refs[n_parts:]
    values_t, refs = refs[:n_parts], refs[n_parts + n_after :]
    grad_qkv, grad_input, grad_bn, sums, weight, sems = refs
    load = pltpu.make_async_copy(attn.at[:, pl.ds(0, 3 * D)], weight, sems.at[0])
    load.start()
    at = 0
    for query, key, value in zip(queries, keys_t, values_t):
        width = query.shape[1]
        grad_qkv[:, at : at + width] = query[...]
        grad_qkv[:, D + at : D + at + width] = key[...].T
        grad_qkv[:, 2 * D + at : 2 * D + at + width] = value[...].T
        at += width
    load.wait()
    total = grad_residual[...] + dot_nt(grad_qkv[...], weight[...])
    grad_input[...] = total
    alive = lax.broadcasted_iota(jnp.int32, (TLEN, 1), 0) < live[0]
    back = jnp.where(jnp.logical_and(alive, live[1] == 0), total, 0.0)
    grad_bn[...] = back.astype(BF16)
    normal = (pre[...] - bn[0:1, :]) * bn[1:2, :]
    sums[...] = jnp.zeros_like(sums)
    sums[0:1, :] = jnp.sum(grad_qkv[:, :D].astype(F32), axis=0, keepdims=True)
    sums[1:2, :] = jnp.sum(grad_qkv[:, 2 * D :].astype(F32), axis=0, keepdims=True)
    sums[2:3, :] = grads_one[6:7, :]
    sums[3:5, :] = grads_one[4:6, :]
    sums[5:9, :] = grads_one[0:4, :]
    sums[9:12, :] = grads_two[0:3, :]
    sums[12:13, :] = jnp.sum(back * normal, axis=0, keepdims=True)
    sums[13:14, :] = jnp.sum(back, axis=0, keepdims=True)


def attn_bwd_input(live, attn, grads_two, grads_one, grad_residual, pre, bn, queries, keys_t, values_t, after):
    parts = len(queries)
    return pl.pallas_call(
        functools.partial(input_kernel, parts, len(after)),
        out_shape=[
            jax.ShapeDtypeStruct((TLEN, 3 * D), BF16),
            jax.ShapeDtypeStruct((TLEN, D), F32),
            jax.ShapeDtypeStruct((TLEN, D), BF16),
            jax.ShapeDtypeStruct((16, D), F32),
        ],
        in_specs=[SMEM, ANY] + [VMEM] * (3 * parts + 5) + [ANY] * len(after),
        out_specs=[VMEM] * 4,
        scratch_shapes=[pltpu.VMEM((D, 3 * D), BF16), pltpu.SemaphoreType.DMA((1,))],
        compiler_params=params(60),
        cost_estimate=cost(8),
        name="input_gradient",
    )(live, attn, grads_two, grads_one, grad_residual, pre, bn, *queries, *keys_t, *values_t, *after)


def table_kernel(n_parts, n_after, bucket, *refs):
    parts, (grad_table, one_hot, total) = refs[:n_parts], refs[n_parts + n_after :]
    step = pl.program_id(0)

    @pl.when(step == 0)
    def _():
        total[...] = jnp.zeros_like(total)

    for group in range(ROWS // 16):
        lines = slice(group * 16, (group + 1) * 16)
        which = bucket[lines, :]
        for b in range(BUCKETS):
            one_hot[b * 16 : (b + 1) * 16, :] = jnp.where(which == b, 1.0, 0.0).astype(BF16)
        slopes = jnp.concatenate(
            [part[:, lines, :].reshape(part.shape[0] * 16, TLEN) for part in parts], axis=0
        )
        total[...] += dot_nt(one_hot[...], slopes)

    @pl.when(step == STEPS - 1)
    def _():
        line = lax.broadcasted_iota(jnp.int32, (BUCKETS * 16, HEADS * 16), 0) % 16
        lane = lax.broadcasted_iota(jnp.int32, (BUCKETS * 16, HEADS * 16), 1) % 16
        kept = jnp.where(line == lane, total[...], 0.0)
        grad_table[...] = jnp.sum(kept.reshape(BUCKETS, 16, HEADS * 16), axis=1)


def table_grad(bucket, parts, after):
    return pl.pallas_call(
        functools.partial(table_kernel, len(parts), len(after)),
        grid=(STEPS,),
        out_shape=jax.ShapeDtypeStruct((BUCKETS, HEADS * 16), F32),
        in_specs=[pl.BlockSpec((ROWS, TLEN), lambda i: (i, 0))]
        + [pl.BlockSpec((part.shape[0], ROWS, TLEN), lambda i: (0, i, 0)) for part in parts]
        + [ANY] * len(after),
        out_specs=pl.BlockSpec((BUCKETS, HEADS * 16), lambda i: (0, 0)),
        scratch_shapes=[
            pltpu.VMEM((BUCKETS * 16, TLEN), BF16),
            pltpu.VMEM((BUCKETS * 16, HEADS * 16), F32),
        ],
        compiler_params=params(60),
        cost_estimate=cost(7),
        name="table_gradient",
    )(bucket, *parts, *after)


def outer_kernel(n_parts, n_after, widths, offs, *refs):
    count = len(widths)
    lefts, rights, refs = refs[:count], refs[count : 2 * count], refs[2 * count + n_after :]
    parts, (grad, sems) = refs[:n_parts], refs[n_parts:]
    at = 0
    for left, right, width in zip(lefts, rights, widths):
        turned = left[...].astype(BF16).T
        for lo in range(0, width, D):
            grad[:, at + lo : at + lo + D] = dot(turned, right[:, lo : lo + D]).astype(BF16)
        at += width
    for copy in store_blocks(offs, grad, parts, sems):
        copy.wait()


def outer(offs, n_blocks, lefts, rights, after):
    widths = tuple(right.shape[1] for right in rights)
    rows = lefts[0].shape[1]
    parts = grad_shapes(n_blocks, rows, sum(widths))
    out = pl.pallas_call(
        functools.partial(outer_kernel, len(parts), len(after), widths),
        out_shape=parts,
        in_specs=[SMEM] + [VMEM] * (2 * len(widths)) + [ANY] * len(after),
        out_specs=[ANY] * len(parts),
        scratch_shapes=[
            pltpu.VMEM((rows, sum(widths)), BF16),
            pltpu.SemaphoreType.DMA((16,)),
        ],
        compiler_params=params(60),
        cost_estimate=cost(4.5),
        name="weight_gradient",
    )(offs, *lefts, *rights, *after)
    return list(out)


def project_grad_kernel(n_parts, n_after, live, places, maps, own, other, pre, bn, totals, extra, *refs):
    parts, refs = refs[n_after : n_after + n_parts], refs[n_after + n_parts :]
    grad_pre, grad, sems, extra_sems = refs
    alive = lax.broadcasted_iota(jnp.int32, (TLEN, 1), 0) < live[0]
    normal = (pre[...] - bn[0:1, :]) * bn[1:2, :]
    count = bn[4:5, :]
    back = own[...].astype(F32) + other[...].astype(F32)
    back = back - totals[1:2, :] / count - normal * (totals[0:1, :] / count)
    low = jnp.where(alive, back * (bn[1:2, :] * bn[2:3, :]), 0.0).astype(BF16)
    grad_pre[...] = low
    grad[...] = dot(maps[...].T, low).astype(BF16)
    copies = store_blocks(places, grad, parts, sems, extra, extra_sems)
    for copy in copies:
        copy.wait()


def project_gradient(live, places, n_blocks, maps, own, other, pre, bn, totals, extra, after):
    rows = maps.shape[1]
    parts = grad_shapes(n_blocks, rows, D, 16)
    out = pl.pallas_call(
        functools.partial(project_grad_kernel, len(parts), len(after)),
        out_shape=parts + [jax.ShapeDtypeStruct((TLEN, D), BF16)],
        in_specs=[SMEM, SMEM] + [VMEM] * 7 + [ANY] * len(after),
        out_specs=[ANY] * len(parts) + [VMEM],
        scratch_shapes=[
            pltpu.VMEM((rows, D), BF16),
            pltpu.SemaphoreType.DMA((16,)),
            pltpu.SemaphoreType.DMA((16,)),
        ],
        compiler_params=params(60),
        cost_estimate=cost(5),
        name="project_gradient",
    )(live, places, maps, own, other, pre, bn, totals, extra, *after)
    return out[:-1], out[-1]


def nesterov(weight, moment, average, gradient, rate):
    moment_new = MOMENTUM * moment + gradient
    weight_new = weight - rate * (gradient + MOMENTUM * moment_new)
    return (weight_new, moment_new, AVERAGE * average + (1.0 - AVERAGE) * weight_new)


def stats_kernel(n_after, live, own, other, *refs):
    pre, stats = refs[n_after:]
    total = (own[...].astype(F32) + other[...].astype(F32)).astype(BF16).astype(F32)
    pre[...] = total
    count = live[0].astype(F32)
    mask = lax.broadcasted_iota(jnp.int32, (TLEN, 1), 0) < live[0]
    mean = jnp.sum(jnp.where(mask, total, 0.0), axis=0, keepdims=True) / count
    centre = jnp.where(mask, total - mean, 0.0)
    stats[...] = jnp.concatenate(
        [
            mean,
            jnp.sum(centre * centre, axis=0, keepdims=True),
            jnp.full((6, D), count, F32),
        ],
        axis=0,
    )


def local_stats(live, own, other, after):
    return pl.pallas_call(
        functools.partial(stats_kernel, len(after)),
        out_shape=[
            jax.ShapeDtypeStruct((TLEN, D), F32),
            jax.ShapeDtypeStruct((8, D), F32),
        ],
        in_specs=[SMEM, VMEM, VMEM] + [ANY] * len(after),
        out_specs=[VMEM, VMEM],
        compiler_params=params(60),
        cost_estimate=cost(3),
        name="local_statistics",
    )(live, own, other, *after)


def merge_kernel(here, there, gains, out):
    n_here, n_there = here[2:3, :], there[2:3, :]
    total = n_here + n_there
    gap = there[0:1, :] - here[0:1, :]
    out[0:1, :] = (here[0:1, :] * n_here + there[0:1, :] * n_there) / total
    spread = here[1:2, :] + there[1:2, :] + gap * gap * (n_here * n_there / total)
    out[1:2, :] = spread
    out[2:8, :] = jnp.broadcast_to(total, (6, D))
    if gains is not None:
        out[1:2, :] = lax.rsqrt(spread / total + EPS)
        out[2:4, :] = gains[0:2, :]


def merge_stats(stats, gains, after):
    bit, n = 1, lax.axis_size("batch")
    while bit < n:
        last = 2 * bit == n
        ties = after.get(bit, [])
        operands = [stats, swap(stats, bit)] + ([gains] if last else [])

        def kernel(*refs, last=last):
            merge_kernel(refs[0], refs[1], refs[2] if last else None, refs[-1])

        stats = pl.pallas_call(
            kernel,
            out_shape=jax.ShapeDtypeStruct((8, D), F32),
            in_specs=[VMEM] * len(operands) + [ANY] * len(ties),
            out_specs=VMEM,
            cost_estimate=cost(0.5),
            name="merge_statistics",
        )(*operands, *ties)
        bit *= 2
    return stats


def add_kernel(here, there, *refs):
    refs[-1][...] = here[...] + there[...]


def sum_small(values, after):
    bit = 1
    while bit < lax.axis_size("batch"):
        ties = after.get(bit, [])
        values = pl.pallas_call(
            add_kernel,
            out_shape=jax.ShapeDtypeStruct(values.shape, F32),
            in_specs=[VMEM] * 2 + [ANY] * len(ties),
            out_specs=VMEM,
            cost_estimate=cost(0.5),
            name="sum_small",
        )(values, swap(values, bit), *ties)
        bit *= 2
    return values


def on_device(
    text_embed,
    visual_maps,
    visual_bucket,
    rel_bucket,
    joined_grad,
    attn_weight,
    attn_moment,
    attn_average,
    ffn_weight,
    ffn_moment,
    ffn_average,
    vector_weight,
    vector_moment,
    vector_average,
    project_weight,
    project_moment,
    project_average,
    shared_weight,
    shared_moment,
    shared_average,
):
    n_batch = lax.axis_size("batch")
    me = lax.axis_index("batch")
    ringed = n_batch == 16
    is_text = lax.axis_index("stream") == 0
    maps = visual_maps.reshape(TLEN, -1)

    small = jnp.zeros((16, D), BF16)
    small = small.at[0, : vector_weight.shape[1]].set(vector_weight[0].astype(BF16))
    small = small.at[1, : shared_weight.shape[0]].set(shared_weight.astype(BF16))
    attn_low = rounded(attn_weight[0], [])
    attn_full = lax.all_gather(attn_low, "batch", axis=0, tiled=True)
    packed = jnp.concatenate([project_weight.astype(BF16), small], axis=0)
    if ringed:
        sources = jnp.asarray(gather_sources())[me]
        targets = jnp.asarray(scatter_targets())[me]
        project_blocks = ring_gather(packed)
        ffn_low = rounded(ffn_weight[0], project_blocks[5:7])
        ffn_blocks = ring_gather(ffn_low, FF)
        n_blocks = 16
    else:
        sources = jnp.zeros((1,), jnp.int32)
        targets = jnp.zeros((1,), jnp.int32)
        rows = lax.all_gather(project_weight.astype(BF16), "batch", axis=0, tiled=True)
        project_blocks = [jnp.concatenate([rows, jnp.zeros((16, D), BF16)], axis=0)]
        ffn_low = rounded(ffn_weight[0], [])
        ffn_blocks = [lax.all_gather(ffn_low, "batch", axis=0, tiled=True)]
        n_blocks = 1

    partial_pre, project_half, small_all = project(sources, maps, jnp.stack(project_blocks))
    if not ringed:
        small_all = lax.all_gather(small, "batch", axis=0, tiled=False)
    other_pre = across(partial_pre)
    vector_rows = small_all[:, 0, : vector_weight.shape[1]].reshape(12, D).astype(F32)
    vec = jnp.concatenate([vector_rows, jnp.zeros((4, D), F32)], axis=0)
    shared_full = small_all[:, 1, : shared_weight.shape[0]].reshape(-1).astype(F32)
    table = jnp.zeros((16, 128), F32)
    table = table.at[:HEADS, :BUCKETS].set(
        shared_full[: BUCKETS * HEADS].reshape(BUCKETS, HEADS).T
    )
    gains = shared_full[BUCKETS * HEADS :].reshape(2, D)

    bucket = rel_bucket.reshape(TLEN, TLEN)
    bias = spatial_bias(bucket, table, ffn_blocks[1:3] if ringed else [])
    visual_len = ((visual_bucket + 1) * (TLEN // 2)).astype(jnp.int32)
    pre, stats = local_stats(visual_len, partial_pre, other_pre, [bias])
    bn = merge_stats(stats, gains, {2: ffn_blocks[3:5]} if ringed else {})
    text = is_text.astype(jnp.int32)
    live = jnp.stack([jnp.where(is_text, TLEN, visual_len[0]), text])
    visual_live = jnp.stack([visual_len[0], text])

    qkv, probs, x_low, query_t, ctx, normed, inverse = attn_fwd(
        live,
        attn_full,
        bias,
        text_embed.reshape(TLEN, D),
        pre,
        bn,
        vec,
        ffn_blocks[5:7] if ringed else [],
    )
    down_part, (slope, result, grad_second, grad_low, grads_two) = ffn_fwd(
        live, sources, ffn_blocks, normed, vec, joined_grad.reshape(TLEN, D)
    )
    joined = result + across(result)
    down_sum, _ = reduce_grad([down_part])
    up_parts, (grad_residual, grad_attended, grads_one, grad_ctx, grad_ctx_t) = ffn_bwd(
        targets,
        sources,
        ffn_blocks,
        attn_full,
        normed,
        inverse,
        vec,
        slope,
        grad_second,
        grad_low,
    )
    up_grad, up_steps = reduce_grad(up_parts)
    pieces = []
    for i in range(2):
        pieces.append(
            attn_bwd_pairs(
                3 * i, 3, qkv, grad_ctx, ctx, grad_ctx_t, query_t, probs, up_steps[0] if i else []
            )
        )
    queries, keys_t, values_t, score_grads = zip(*pieces)
    grad_qkv, grad_input, grad_bn, sums = attn_bwd_input(
        visual_live,
        attn_full,
        grads_two,
        grads_one,
        grad_residual,
        pre,
        bn,
        queries,
        keys_t,
        values_t,
        up_steps[1],
    )

    grad_bn_other = across(grad_bn)
    attn_parts = outer(targets, n_blocks, [x_low, ctx], [grad_qkv, grad_attended], [])
    attn_grad, attn_steps = reduce_grad(attn_parts)
    grad_table = table_grad(bucket, score_grads, [attn_parts[0]])
    sums = sum_small(
        sums,
        {
            1: [attn_parts[0]],
            2: [grad_table],
            8: [grad_bn_other],
        },
    )
    shared_sums = sums[8:]
    shared_sums = (shared_sums + across(shared_sums))[4:6]
    all_tokens = n_batch * TLEN
    rate_attention = 1.5 / math.sqrt(D * all_tokens)
    rate_matrix = 0.6 / math.sqrt(D * all_tokens)
    rate_vector = 0.12 / math.sqrt(all_tokens)
    width = vector_weight.shape[1]
    vector_grad = lax.dynamic_slice(sums[:12].reshape(-1), (me * width,), (width,))[None]
    vector_new = nesterov(vector_weight, vector_moment, vector_average, vector_grad, rate_vector)
    table_row = jnp.sum(grad_table.reshape(BUCKETS, HEADS, 16), axis=-1).reshape(1, -1)
    table_row = table_row + across(table_row)
    width = shared_weight.shape[0]
    padded = jnp.pad(table_row[0], (0, n_batch * width - BUCKETS * HEADS))
    if ringed:
        extra = jnp.zeros((16, 16, D), BF16)
        extra = extra.at[:, 0, :width].set(padded.reshape(16, width).astype(BF16))
    else:
        extra = jnp.zeros((1, 16, D), BF16)
    project_parts, grad_pre = project_gradient(
        visual_live,
        targets,
        n_blocks,
        maps,
        grad_bn,
        grad_bn_other,
        pre,
        bn,
        shared_sums,
        extra,
        [down_sum] + list(vector_new),
    )
    project_sum, _ = reduce_grad(project_parts)
    grad_maps = dot_nt(grad_pre, project_half)
    if ringed:
        rows = project_weight.shape[0]
        project_grad, own_table = project_sum[:rows], project_sum[rows, :width]
    else:
        project_grad = project_sum
        own_table = lax.dynamic_slice(lax.psum(padded, "batch"), (me * width,), (width,))
    own_shared = own_table + lax.dynamic_slice(
        jnp.concatenate([jnp.zeros((BUCKETS * HEADS,), F32), shared_sums.reshape(-1)]),
        (me * width,),
        (width,),
    )

    ffn_grad = jnp.concatenate([up_grad.astype(F32), down_sum.astype(F32)], axis=1)[None]
    ffn_new = nesterov(ffn_weight, ffn_moment, ffn_average, ffn_grad, rate_matrix)
    attn_new = nesterov(attn_weight, attn_moment, attn_average, attn_grad.astype(F32)[None], rate_attention)
    project_new = nesterov(
        project_weight, project_moment, project_average, project_grad.astype(F32), rate_matrix
    )
    shared_new = nesterov(shared_weight, shared_moment, shared_average, own_shared, rate_vector)
    return (
        joined.reshape(1, TLEN, D),
        grad_input.reshape(1, 1, TLEN, D),
        grad_maps.reshape(1, TLEN, -1),
        attn_new[0],
        attn_new[1],
        attn_new[2],
        ffn_new[0],
        ffn_new[1],
        ffn_new[2],
        vector_new[0],
        vector_new[1],
        vector_new[2],
        project_new[0],
        project_new[1],
        project_new[2],
        shared_new[0],
        shared_new[1],
        shared_new[2],
    )


def solution(mesh):
    return jax.shard_map(
        on_device,
        mesh=mesh,
        in_specs=(
            P("batch", None, None),
            P("batch", None, "stream"),
            P("batch"),
            P("stream", "batch", None, None),
            P("batch", None, None),
            P("stream", "batch", None),
            P("stream", "batch", None),
            P("stream", "batch", None),
            P("stream", "batch", None),
            P("stream", "batch", None),
            P("stream", "batch", None),
            P("stream", "batch"),
            P("stream", "batch"),
            P("stream", "batch"),
            P(("stream", "batch"), None),
            P(("stream", "batch"), None),
            P(("stream", "batch"), None),
            P("batch"),
            P("batch"),
            P("batch"),
        ),
        out_specs=(
            P("batch", None, None),
            P("stream", "batch", None, None),
            P("batch", None, "stream"),
            P("stream", "batch", None),
            P("stream", "batch", None),
            P("stream", "batch", None),
            P("stream", "batch", None),
            P("stream", "batch", None),
            P("stream", "batch", None),
            P("stream", "batch"),
            P("stream", "batch"),
            P("stream", "batch"),
            P(("stream", "batch"), None),
            P(("stream", "batch"), None),
            P(("stream", "batch"), None),
            P("batch"),
            P("batch"),
            P("batch"),
        ),
        check_vma=False,
    )
```

```python
import functools
import math

import jax
import jax.numpy as jnp
import numpy as np
from jax import lax
from jax.experimental import pallas as pl
from jax.experimental.pallas import tpu as pltpu
from jax.sharding import PartitionSpec as P

D = 768
HEADS = 12
HEAD_DIM = 64
FF = 3072
TLEN = 512
BUCKETS = 32
PAIRS = HEADS // 2
ROWS = 128
SOFT = 128
STEPS = TLEN // ROWS
CHUNKS = FF // D

EPS = 1e-05
MOMENTUM = 0.9
AVERAGE = 0.95
SCALE = HEAD_DIM ** (-0.5)

BF16 = jnp.bfloat16
F32 = jnp.float32
ANY = pl.BlockSpec(memory_space=pl.ANY)
SMEM = pl.BlockSpec(memory_space=pltpu.SMEM)
VMEM = pl.BlockSpec(memory_space=pltpu.VMEM)
MIB = 1024 * 1024

CYCLE = ((0, 0), (1, 0), (2, 0), (3, 0), (3, 1), (2, 1), (1, 1), (0, 1))
CHIP = [z * 2 + y for z, y in CYCLE]
PLACE = [CHIP.index(k) for k in range(8)]


def cycle_perm(shift):
    return [
        (CHIP[r] * 2 + c, CHIP[(r + shift) % 8] * 2 + c) for r in range(8) for c in range(2)
    ]


def across(v):
    return lax.ppermute(v, "stream", [(0, 1), (1, 0)])


def swap(v, bit):
    n = lax.axis_size("batch")
    return lax.ppermute(v, "batch", [(i, i ^ bit) for i in range(n)])


def gather_shifts():
    return [0, -1, 1, -2, 2, -3, 3, -4]


def gather_sources():
    table = np.zeros((16, 16), np.int32)
    for b in range(16):
        place, core = PLACE[b // 2], b % 2
        for slot, shift in enumerate(gather_shifts()):
            chip = CHIP[(place + shift) % 8]
            table[b, slot] = chip * 2 + core
            table[b, 8 + slot] = chip * 2 + 1 - core
    return table


def scatter_targets():
    table = np.zeros((16, 16), np.int32)
    for b in range(16):
        place, core = PLACE[b // 2], b % 2
        for ahead in range(8):
            chip = CHIP[(place + ahead) % 8]
            table[b, ahead] = chip * 2 + core
            table[b, 8 + ahead] = chip * 2 + 1 - core
    return table


def ring_gather(block, split=0):
    up, down = cycle_perm(1), cycle_perm(-1)
    low = high = block
    own = [block]
    for _ in range(3):
        low = lax.ppermute(low, "batch", up)
        high = lax.ppermute(high, "batch", down)
        own += [low, high]
    if split:
        own.append(lax.ppermute(low[:, :split], "batch", up))
        own.append(lax.ppermute(high[:, split:], "batch", down))
    else:
        own.append(lax.ppermute(low, "batch", up))
    return own + [swap(v, 1) for v in own]


def ring_scatter(mine, theirs):
    up, down = cycle_perm(1), cycle_perm(-1)
    other = swap(theirs, 1)

    def term(j):
        return mine[j].astype(F32) + other[j].astype(F32)

    def passed(v, j):
        return (v.astype(F32) + term(j)).astype(BF16)

    first = [term(4).astype(BF16), term(5).astype(BF16)]
    low = lax.ppermute(first[0], "batch", up)
    high = lax.ppermute(first[1], "batch", down)
    for ahead in (3, 2):
        low = lax.ppermute(passed(low, ahead), "batch", up)
        high = lax.ppermute(passed(high, 9 - ahead), "batch", down)
    low = lax.ppermute(passed(low, 1), "batch", up)
    return low.astype(F32) + high.astype(F32) + term(0), first


def reduce_grad(parts):
    if len(parts) == 1:
        total = lax.psum_scatter(parts[0][0], "batch", scatter_dimension=0, tiled=True)
        return total.astype(F32), []
    return ring_scatter(*parts)


def dot(left, right):
    return jnp.dot(left, right, preferred_element_type=F32)


def dot_nt(left, right):
    return lax.dot_general(left, right, (((1,), (1,)), ((), ())), preferred_element_type=F32)


def store_blocks(offs, src, parts, sems):
    copies = []
    if len(parts) == 1:
        copies.append(pltpu.make_async_copy(src, parts[0].at[0], sems.at[0]))
    else:
        rows = src.shape[0] // 16
        for k in range(16):
            at = pl.multiple_of(offs[k] * rows, 16)
            place = parts[k // 8].at[k % 8]
            copies.append(pltpu.make_async_copy(src.at[pl.ds(at, rows), :], place, sems.at[k]))
    for copy in copies:
        copy.start()
    return copies


def grad_shapes(n_blocks, rows, cols):
    if n_blocks == 1:
        return [jax.ShapeDtypeStruct((1, rows, cols), BF16)]
    return [jax.ShapeDtypeStruct((8, rows // 16, cols), BF16)] * 2


def params(mib):
    return pltpu.CompilerParams(vmem_limit_bytes=mib * MIB)


def cost(micros):
    return pl.CostEstimate(flops=int(micros * 1e9), bytes_accessed=0, transcendentals=0)


def norm_rows(values):
    centre = values - jnp.mean(values, axis=-1, keepdims=True)
    inverse = lax.rsqrt(jnp.mean(centre * centre, axis=-1, keepdims=True) + EPS)
    return centre * inverse, inverse


def norm_back(upstream, normed, inverse, gain):
    scaled = upstream * gain
    return inverse * (
        scaled
        - jnp.mean(scaled, axis=-1, keepdims=True)
        - normed * jnp.mean(scaled * normed, axis=-1, keepdims=True)
    )


def half_mask(rows, half):
    lane = lax.broadcasted_iota(jnp.int32, (rows, 128), 1)
    return (lane < HEAD_DIM) if half == 0 else (lane >= HEAD_DIM)


def round_kernel(n_after, weight, *refs):
    refs[n_after][...] = weight[...].astype(BF16)


def rounded(weight, after):
    return pl.pallas_call(
        functools.partial(round_kernel, len(after)),
        out_shape=jax.ShapeDtypeStruct(weight.shape, BF16),
        in_specs=[VMEM] + [ANY] * len(after),
        out_specs=VMEM,
        compiler_params=params(60),
        cost_estimate=cost(1),
        name="round_weight",
    )(weight, *after)


def project_kernel(n_blocks, offs, maps, blocks, pre, whole, small, sems, small_sems):
    copies = []
    rows = whole.shape[0] // n_blocks
    for i in range(n_blocks):
        block = blocks.at[i]
        which = offs[i] if n_blocks > 1 else 0
        at = pl.multiple_of(which * rows, 16)
        copies.append(
            pltpu.make_async_copy(block.at[pl.ds(0, rows), :], whole.at[pl.ds(at, rows), :], sems.at[i])
        )
        copies.append(
            pltpu.make_async_copy(block.at[pl.ds(rows, 16), :], small.at[which], small_sems.at[i])
        )
    for copy in copies:
        copy.start()
    for copy in copies:
        copy.wait()
    for i in range(2):
        pick = pl.ds(i * (TLEN // 2), TLEN // 2)
        pre[pick, :] = dot(maps[pick, :], whole[...]).astype(BF16)


def project(offs, maps, blocks):
    n = blocks.shape[0]
    rows = blocks.shape[1] - 16
    channels = n * rows
    return pl.pallas_call(
        functools.partial(project_kernel, n),
        out_shape=[
            jax.ShapeDtypeStruct((TLEN, D), BF16),
            jax.ShapeDtypeStruct((channels, D), BF16),
            jax.ShapeDtypeStruct((n, 16, D), BF16),
        ],
        in_specs=[SMEM, VMEM, ANY],
        out_specs=[VMEM] * 3,
        scratch_shapes=[pltpu.SemaphoreType.DMA((n,)), pltpu.SemaphoreType.DMA((n,))],
        compiler_params=params(60),
        cost_estimate=cost(60),
        name="project_maps",
    )(offs, maps, blocks)


def bias_kernel(n_after, bucket, table, *refs):
    bias = refs[n_after]
    for t in range(TLEN // 128):
        lanes = slice(t * 128, (t + 1) * 128)
        which = bucket[:, lanes]
        for head in range(HEADS):
            row = jnp.broadcast_to(table[head : head + 1, :], which.shape)
            bias[head, :, lanes] = jnp.take_along_axis(row, which, axis=1).astype(BF16)


def spatial_bias(bucket, table, after):
    rows = 64
    return pl.pallas_call(
        functools.partial(bias_kernel, len(after)),
        grid=(TLEN // rows,),
        out_shape=jax.ShapeDtypeStruct((HEADS, TLEN, TLEN), BF16),
        in_specs=[
            pl.BlockSpec((rows, TLEN), lambda i: (i, 0)),
            pl.BlockSpec((16, 128), lambda i: (0, 0)),
        ]
        + [ANY] * len(after),
        out_specs=pl.BlockSpec((HEADS, rows, TLEN), lambda i: (0, i, 0)),
        compiler_params=params(60),
        cost_estimate=cost(5),
        name="spatial_bias",
    )(bucket, table, *after)


def attn_fwd_kernel(n_after, live, attn, bias, text, pre, bn, vec, *refs):
    qkv_out, probs, x_out, query_t, ctx, normed, inverse = refs[n_after : n_after + 7]
    weight, qkv, score_a, score_b, prob_a, prob_b, ctx_a, sems, in_sems, out_sems = refs[n_after + 7 :]
    loads = []
    for part in range(4):
        cols = pl.ds(part * D, D)
        loads.append(pltpu.make_async_copy(attn.at[:, cols], weight.at[:, cols], sems.at[part]))
        loads[-1].start()

    def bring(head):
        place = (prob_a, prob_b)[head % 2].at[head // 2]
        return pltpu.make_async_copy(bias.at[head], place, in_sems.at[head])

    for head in range(HEADS):
        bring(head).start()
    alive = lax.broadcasted_iota(jnp.int32, (TLEN, 1), 0) < live[0]
    visual = (pre[...] - bn[0:1, :]) * bn[1:2, :] * bn[2:3, :] + bn[3:4, :]
    x = jnp.where(live[1] == 1, text[...].astype(F32), jnp.where(alive, visual, 0.0))
    x_low = x.astype(BF16)
    x_out[...] = x_low
    exports = []
    for part in range(3):
        cols = slice(part * D, (part + 1) * D)
        loads[part].wait()
        value = dot(x_low, weight[:, cols])
        if part != 1:
            value = value + vec[part // 2 : part // 2 + 1, :]
        qkv[:, cols] = value.astype(BF16)
        exports.append(
            pltpu.make_async_copy(qkv.at[:, cols], qkv_out.at[:, cols], out_sems.at[HEADS + part])
        )
        exports[-1].start()

    def lanes(start, pair):
        return pl.ds(pl.multiple_of(start + pair * 128, 128), 128)

    def scores(pair, half, out):
        query = qkv[:, lanes(0, pair)] * SCALE
        query = jnp.where(half_mask(TLEN, half), query, jnp.zeros_like(query))
        out[...] = dot_nt(query, qkv[:, lanes(D, pair)])

    def softmax(score, prob, pair):
        key_valid = lax.broadcasted_iota(jnp.int32, (SOFT, TLEN), 1) < live[0]
        for i in range(TLEN // SOFT):
            rows = slice(i * SOFT, (i + 1) * SOFT)
            value = score[rows, :] + prob[pair, rows, :].astype(F32)
            value = jnp.where(key_valid, value, -1000000000.0)
            peak = jnp.max(value, axis=-1, keepdims=True)
            raised = jnp.exp(value - peak)
            total = jnp.sum(raised, axis=-1, keepdims=True)
            prob[pair, rows, :] = (raised * (1.0 / total)).astype(BF16)

    scores(0, 0, score_a)
    for head in range(HEADS):
        bring(head).wait()

    def step(pair, carry):
        values = qkv[:, lanes(2 * D, pair)]
        scores(pair, 1, score_b)
        softmax(score_a, prob_a, pair)
        scores(jnp.minimum(pair + 1, PAIRS - 1), 0, score_a)
        ctx_a[...] = dot(prob_a[pair], values)
        softmax(score_b, prob_b, pair)
        ctx_b = dot(prob_b[pair], values)
        ctx[:, lanes(0, pair)] = jnp.where(half_mask(TLEN, 0), ctx_a[...], ctx_b).astype(BF16)
        for half, prob in enumerate((prob_a, prob_b)):
            head = 2 * pair + half
            pltpu.make_async_copy(prob.at[pair], probs.at[head], out_sems.at[head]).start()
        return carry

    lax.fori_loop(0, PAIRS, step, 0)
    loads[3].wait()
    att = dot(ctx[...], weight[:, 3 * D :]) + vec[2:3, :]
    query_t[...] = (qkv[:, :D] * SCALE).T
    normal, inv = norm_rows(x + att)
    normed[...] = normal
    inverse[...] = jnp.broadcast_to(inv, (TLEN, 128))
    for copy in exports:
        copy.wait()
    for head in range(HEADS):
        prob = (prob_a, prob_b)[head % 2]
        pltpu.make_async_copy(prob.at[head // 2], probs.at[head], out_sems.at[head]).wait()


def attn_fwd(live, attn, bias, text, pre, bn, vec, after):
    return pl.pallas_call(
        functools.partial(attn_fwd_kernel, len(after)),
        out_shape=[
            jax.ShapeDtypeStruct((TLEN, 3 * D), BF16),
            jax.ShapeDtypeStruct((HEADS, TLEN, TLEN), BF16),
            jax.ShapeDtypeStruct((TLEN, D), BF16),
            jax.ShapeDtypeStruct((D, TLEN), BF16),
            jax.ShapeDtypeStruct((TLEN, D), BF16),
            jax.ShapeDtypeStruct((TLEN, D), F32),
            jax.ShapeDtypeStruct((TLEN, 128), F32),
        ],
        in_specs=[SMEM, ANY, ANY] + [VMEM] * 4 + [ANY] * len(after),
        out_specs=[ANY, ANY] + [VMEM] * 5,
        scratch_shapes=[
            pltpu.VMEM((D, 4 * D), BF16),
            pltpu.VMEM((TLEN, 3 * D), BF16),
            pltpu.VMEM((TLEN, TLEN), F32),
            pltpu.VMEM((TLEN, TLEN), F32),
            pltpu.VMEM((PAIRS, TLEN, TLEN), BF16),
            pltpu.VMEM((PAIRS, TLEN, TLEN), BF16),
            pltpu.VMEM((TLEN, 128), F32),
            pltpu.SemaphoreType.DMA((4,)),
            pltpu.SemaphoreType.DMA((HEADS,)),
            pltpu.SemaphoreType.DMA((HEADS + 3,)),
        ],
        compiler_params=params(60),
        cost_estimate=cost(15),
        name="attention_forward",
    )(live, attn, bias, text, pre, bn, vec, *after)


def load_ffn(offs, blocks, up, down, sems):
    first, second = [], []
    if len(blocks) == 1:
        first.append(pltpu.make_async_copy(blocks[0].at[:, pl.ds(0, FF)], up, sems.at[0]))
        second.append(pltpu.make_async_copy(blocks[0].at[:, pl.ds(FF, FF)], down, sems.at[1]))
        return first, second
    at = 0
    for slot in range(16):
        rows = pl.ds(pl.multiple_of(offs[slot] * 48, 16), 48)
        if slot % 8 < 7:
            left, right = blocks[at].at[:, pl.ds(0, FF)], blocks[at].at[:, pl.ds(FF, FF)]
            at += 1
        else:
            left, right = blocks[at], blocks[at + 1]
            at += 2
        first.append(pltpu.make_async_copy(left, up.at[rows, :], sems.at[2 * slot]))
        second.append(pltpu.make_async_copy(right, down.at[rows, :], sems.at[2 * slot + 1]))
    return first, second


def ffn_kernel(n_blocks, live, offs, attn, normed, inverse, vec, joined_grad, *refs):
    blocks, refs = refs[:n_blocks], refs[n_blocks:]
    part, refs = refs[0], refs[1:]
    result, grad_residual, grad_attended, grad_ctx, grad_ctx_t, grads = refs[:6]
    up, down, active, slope, grad, total, weight, sems, last_sems, out_sems = refs[6:]
    loads = load_ffn(offs, blocks, up, down, sems)
    for copy in loads[0] + loads[1]:
        copy.start()
    last = pltpu.make_async_copy(attn.at[:, pl.ds(3 * D, D)], weight, last_sems.at[0])
    last.start()
    first = normed[...] * vec[3:4, :] + vec[4:5, :]
    first_low = first.astype(BF16)
    for copy in loads[0]:
        copy.wait()
    units = dot(first_low, up[:, :D])
    total[...] = first + vec[9:10, :]
    for k in range(CHUNKS):
        units = units + vec[5 + k : 6 + k, :]
        if k + 1 < CHUNKS:
            following = dot(first_low, up[:, (k + 1) * D : (k + 2) * D])
        square = units * units
        root = math.sqrt(2.0 / math.pi)
        bend = jnp.tanh(root * units * (1.0 + 0.044715 * square))
        half = 0.5 * (1.0 + bend)
        active[k] = (units * half).astype(BF16)
        slope[k] = (
            half + 0.5 * root * units * (1.0 - bend * bend) * (1.0 + 3.0 * 0.044715 * square)
        ).astype(BF16)
        if k == 0:
            for copy in loads[1]:
                copy.wait()
        total[...] += dot_nt(active[k], down[:, k * D : (k + 1) * D])
        if k + 1 < CHUNKS:
            units = following
    normal, inv = norm_rows(total[...])
    mask = lax.broadcasted_iota(jnp.int32, (TLEN, 1), 0) < live[0]
    result[...] = jnp.where(mask, normal * vec[10:11, :] + vec[11:12, :], 0.0).astype(BF16)
    upstream = jnp.where(mask, joined_grad[...].astype(F32), 0.0)
    second = norm_back(upstream, normal, inv, vec[10:11, :])
    second_low = second.astype(BF16)
    total[...] = second
    grads[9:10, :] = jnp.sum(second_low.astype(F32), axis=0, keepdims=True)
    grads[10:11, :] = jnp.sum(upstream * normal, axis=0, keepdims=True)
    grads[11:12, :] = jnp.sum(upstream, axis=0, keepdims=True)
    turned = second_low.T
    for k in range(CHUNKS):
        cols = slice(FF + k * D, FF + (k + 1) * D)
        grad[:, cols] = dot(turned, active[k]).astype(BF16)
    cols = pl.ds(FF, FF)
    copies = [pltpu.make_async_copy(grad.at[:, cols], part.at[:, cols], out_sems.at[0])]
    copies[0].start()
    turned = first_low.T
    for k in range(CHUNKS):
        cols = slice(k * D, (k + 1) * D)
        inner = (dot(second_low, down[:, cols]) * slope[k].astype(F32)).astype(BF16)
        grads[5 + k : 6 + k, :] = jnp.sum(inner.astype(F32), axis=0, keepdims=True)
        total[...] += dot_nt(inner, up[:, cols])
        grad[:, cols] = dot(turned, inner).astype(BF16)
    cols = pl.ds(0, FF)
    copies.append(pltpu.make_async_copy(grad.at[:, cols], part.at[:, cols], out_sems.at[1]))
    copies[-1].start()
    upstream = total[...]
    grads[3:4, :] = jnp.sum(upstream * normed[...], axis=0, keepdims=True)
    grads[4:5, :] = jnp.sum(upstream, axis=0, keepdims=True)
    residual = norm_back(upstream, normed[...], inverse[:, 0:1], vec[3:4, :])
    grad_residual[...] = residual
    attended = residual.astype(BF16)
    grad_attended[...] = attended
    grads[2:3, :] = jnp.sum(attended.astype(F32), axis=0, keepdims=True)
    grads[0:2, :] = jnp.zeros((2, D), F32)
    grads[12:16, :] = jnp.zeros((4, D), F32)
    last.wait()
    back = dot_nt(attended, weight[...]).astype(BF16)
    grad_ctx[...] = back
    grad_ctx_t[...] = back.T
    for copy in copies:
        copy.wait()


def feed_forward(live, offs, blocks, attn, normed, inverse, vec, joined_grad):
    n = len(blocks)
    out = pl.pallas_call(
        functools.partial(ffn_kernel, n),
        out_shape=[
            jax.ShapeDtypeStruct((D, 2 * FF), BF16),
            jax.ShapeDtypeStruct((TLEN, D), BF16),
            jax.ShapeDtypeStruct((TLEN, D), F32),
            jax.ShapeDtypeStruct((TLEN, D), BF16),
            jax.ShapeDtypeStruct((TLEN, D), BF16),
            jax.ShapeDtypeStruct((D, TLEN), BF16),
            jax.ShapeDtypeStruct((16, D), F32),
        ],
        in_specs=[SMEM, SMEM, ANY] + [VMEM] * 4 + [ANY] * n,
        out_specs=[ANY] + [VMEM] * 6,
        scratch_shapes=[
            pltpu.VMEM((D, FF), BF16),
            pltpu.VMEM((D, FF), BF16),
            pltpu.VMEM((CHUNKS, TLEN, D), BF16),
            pltpu.VMEM((CHUNKS, TLEN, D), BF16),
            pltpu.VMEM((D, 2 * FF), BF16),
            pltpu.VMEM((TLEN, D), F32),
            pltpu.VMEM((D, D), BF16),
            pltpu.SemaphoreType.DMA((32,)),
            pltpu.SemaphoreType.DMA((1,)),
            pltpu.SemaphoreType.DMA((2,)),
        ],
        compiler_params=params(60),
        cost_estimate=cost(30),
        name="feed_forward",
    )(live, offs, attn, normed, inverse, vec, joined_grad, *blocks)
    return out


def pairs_kernel(n_after, keys, values, back, context, back_t, query_t, probs, *refs):
    grad_query, grad_key_t, grad_value_t, grad_scores = refs[n_after:]
    total = jnp.zeros((TLEN, 128), F32)
    for half in range(2):
        mask = half_mask(TLEN, half)
        masked = jnp.where(mask, back[...], jnp.zeros_like(back[...]))
        prob = probs[half]
        slopes = dot_nt(masked, values[...])
        delta = jnp.sum(masked.astype(F32) * context[...].astype(F32), axis=-1, keepdims=True)
        slopes = (prob.astype(F32) * (slopes - delta)).astype(BF16)
        grad_scores[half] = slopes
        near = jnp.where(mask, keys[...], jnp.zeros_like(keys[...]))
        total = total + dot(slopes, near)
        lines = slice(half * HEAD_DIM, (half + 1) * HEAD_DIM)
        grad_key_t[lines, :] = dot(query_t[lines, :], slopes).astype(BF16)
        grad_value_t[lines, :] = dot(back_t[lines, :], prob).astype(BF16)
    grad_query[...] = (total * SCALE).astype(BF16)


def attn_bwd_pairs(first, count, qkv, grad_ctx, ctx, grad_ctx_t, query_t, probs, after):
    def cols(base):
        return pl.BlockSpec((TLEN, 128), lambda i: (0, base + i))

    def lines(base):
        return pl.BlockSpec((128, TLEN), lambda i: (base + i, 0))

    def heads(base):
        return pl.BlockSpec((2, TLEN, TLEN), lambda i: (base + i, 0, 0))

    return pl.pallas_call(
        functools.partial(pairs_kernel, len(after)),
        grid=(count,),
        out_shape=[
            jax.ShapeDtypeStruct((TLEN, 128 * count), BF16),
            jax.ShapeDtypeStruct((128 * count, TLEN), BF16),
            jax.ShapeDtypeStruct((128 * count, TLEN), BF16),
            jax.ShapeDtypeStruct((2 * count, TLEN, TLEN), BF16),
        ],
        in_specs=[
            cols(PAIRS + first),
            cols(2 * PAIRS + first),
            cols(first),
            cols(first),
            lines(first),
            lines(first),
            heads(first),
        ]
        + [ANY] * len(after),
        out_specs=[cols(0), lines(0), lines(0), heads(0)],
        compiler_params=params(60),
        cost_estimate=cost(5),
        name="attention_backward",
    )(qkv, qkv, grad_ctx, ctx, grad_ctx_t, query_t, probs, *after)


def input_kernel(n_parts, n_after, live, attn, grads, grad_residual, pre, bn, *refs):
    queries, refs = refs[:n_parts], refs[n_parts:]
    keys_t, refs = refs[:n_parts], refs[n_parts:]
    values_t, refs = refs[:n_parts], refs[n_parts + n_after :]
    grad_qkv, grad_input, grad_bn, sums, weight, sems = refs
    load = pltpu.make_async_copy(attn.at[:, pl.ds(0, 3 * D)], weight, sems.at[0])
    load.start()
    at = 0
    for query, key, value in zip(queries, keys_t, values_t):
        width = query.shape[1]
        grad_qkv[:, at : at + width] = query[...]
        grad_qkv[:, D + at : D + at + width] = key[...].T
        grad_qkv[:, 2 * D + at : 2 * D + at + width] = value[...].T
        at += width
    load.wait()
    total = grad_residual[...] + dot_nt(grad_qkv[...], weight[...])
    grad_input[...] = total
    alive = lax.broadcasted_iota(jnp.int32, (TLEN, 1), 0) < live[0]
    back = jnp.where(jnp.logical_and(alive, live[1] == 0), total, 0.0)
    grad_bn[...] = back.astype(BF16)
    normal = (pre[...] - bn[0:1, :]) * bn[1:2, :]
    sums[...] = grads[...]
    sums[0:1, :] = jnp.sum(grad_qkv[:, :D].astype(F32), axis=0, keepdims=True)
    sums[1:2, :] = jnp.sum(grad_qkv[:, 2 * D :].astype(F32), axis=0, keepdims=True)
    sums[12:13, :] = jnp.sum(back * normal, axis=0, keepdims=True)
    sums[13:14, :] = jnp.sum(back, axis=0, keepdims=True)


def attn_bwd_input(live, attn, grads, grad_residual, pre, bn, queries, keys_t, values_t, after):
    parts = len(queries)
    return pl.pallas_call(
        functools.partial(input_kernel, parts, len(after)),
        out_shape=[
            jax.ShapeDtypeStruct((TLEN, 3 * D), BF16),
            jax.ShapeDtypeStruct((TLEN, D), F32),
            jax.ShapeDtypeStruct((TLEN, D), BF16),
            jax.ShapeDtypeStruct((16, D), F32),
        ],
        in_specs=[SMEM, ANY] + [VMEM] * (3 * parts + 4) + [ANY] * len(after),
        out_specs=[VMEM] * 4,
        scratch_shapes=[pltpu.VMEM((D, 3 * D), BF16), pltpu.SemaphoreType.DMA((1,))],
        compiler_params=params(60),
        cost_estimate=cost(5),
        name="input_gradient",
    )(live, attn, grads, grad_residual, pre, bn, *queries, *keys_t, *values_t, *after)


def table_kernel(n_parts, n_after, bucket, sums, *refs):
    parts, (out, one_hot, total) = refs[:n_parts], refs[n_parts + n_after :]
    step = pl.program_id(0)

    @pl.when(step == 0)
    def _():
        total[...] = jnp.zeros_like(total)

    for group in range(ROWS // 16):
        lines = slice(group * 16, (group + 1) * 16)
        which = bucket[lines, :]
        for b in range(BUCKETS):
            one_hot[b * 16 : (b + 1) * 16, :] = jnp.where(which == b, 1.0, 0.0).astype(BF16)
        slopes = jnp.concatenate(
            [part[:, lines, :].reshape(part.shape[0] * 16, TLEN) for part in parts], axis=0
        )
        total[...] += dot_nt(one_hot[...], slopes)

    @pl.when(step == STEPS - 1)
    def _():
        line = lax.broadcasted_iota(jnp.int32, (BUCKETS * 16, HEADS * 16), 0) % 16
        lane = lax.broadcasted_iota(jnp.int32, (BUCKETS * 16, HEADS * 16), 1) % 16
        kept = jnp.where(line == lane, total[...], 0.0)
        kept = jnp.sum(kept.reshape(BUCKETS, 16, HEADS * 16), axis=1)
        shape = (HEADS * 16, BUCKETS * HEADS)
        head = lax.broadcasted_iota(jnp.int32, shape, 0) // 16
        pick = lax.broadcasted_iota(jnp.int32, shape, 1) % HEADS
        spread = jnp.dot(
            kept,
            jnp.where(head == pick, 1.0, 0.0),
            precision=lax.Precision.HIGHEST,
            preferred_element_type=F32,
        )
        shape = (BUCKETS, BUCKETS * HEADS)
        own = lax.broadcasted_iota(jnp.int32, shape, 1) // HEADS
        spread = jnp.where(own == lax.broadcasted_iota(jnp.int32, shape, 0), spread, 0.0)
        out[...] = sums[...]
        out[14:15, : BUCKETS * HEADS] = jnp.sum(spread, axis=0, keepdims=True)


def table_grad(bucket, sums, parts, after):
    return pl.pallas_call(
        functools.partial(table_kernel, len(parts), len(after)),
        grid=(STEPS,),
        out_shape=jax.ShapeDtypeStruct((16, D), F32),
        in_specs=[
            pl.BlockSpec((ROWS, TLEN), lambda i: (i, 0)),
            pl.BlockSpec((16, D), lambda i: (0, 0)),
        ]
        + [pl.BlockSpec((part.shape[0], ROWS, TLEN), lambda i: (0, i, 0)) for part in parts]
        + [ANY] * len(after),
        out_specs=pl.BlockSpec((16, D), lambda i: (0, 0)),
        scratch_shapes=[
            pltpu.VMEM((BUCKETS * 16, TLEN), BF16),
            pltpu.VMEM((BUCKETS * 16, HEADS * 16), F32),
        ],
        compiler_params=params(60),
        cost_estimate=cost(5),
        name="table_gradient",
    )(bucket, sums, *parts, *after)


def outer_kernel(n_parts, n_after, widths, offs, *refs):
    count = len(widths)
    lefts, rights, refs = refs[:count], refs[count : 2 * count], refs[2 * count + n_after :]
    parts, (grad, sems) = refs[:n_parts], refs[n_parts:]
    at = 0
    for left, right, width in zip(lefts, rights, widths):
        turned = left[...].astype(BF16).T
        for lo in range(0, width, D):
            grad[:, at + lo : at + lo + D] = dot(turned, right[:, lo : lo + D]).astype(BF16)
        at += width
    for copy in store_blocks(offs, grad, parts, sems):
        copy.wait()


def outer(offs, n_blocks, lefts, rights, after):
    widths = tuple(right.shape[1] for right in rights)
    rows = lefts[0].shape[1]
    parts = grad_shapes(n_blocks, rows, sum(widths))
    return pl.pallas_call(
        functools.partial(outer_kernel, len(parts), len(after), widths),
        out_shape=parts,
        in_specs=[SMEM] + [VMEM] * (2 * len(widths)) + [ANY] * len(after),
        out_specs=[ANY] * len(parts),
        scratch_shapes=[
            pltpu.VMEM((rows, sum(widths)), BF16),
            pltpu.SemaphoreType.DMA((16,)),
        ],
        compiler_params=params(60),
        cost_estimate=cost(5),
        name="weight_gradient",
    )(offs, *lefts, *rights, *after)


def project_grad_kernel(n_parts, n_after, live, places, maps, own, other, pre, bn, totals, *refs):
    parts, refs = refs[n_after : n_after + n_parts], refs[n_after + n_parts :]
    grad_pre, grad, sems = refs
    alive = lax.broadcasted_iota(jnp.int32, (TLEN, 1), 0) < live[0]
    normal = (pre[...] - bn[0:1, :]) * bn[1:2, :]
    count = bn[4:5, :]
    back = own[...].astype(F32) + other[...].astype(F32)
    back = back - totals[1:2, :] / count - normal * (totals[0:1, :] / count)
    low = jnp.where(alive, back * (bn[1:2, :] * bn[2:3, :]), 0.0).astype(BF16)
    grad_pre[...] = low
    grad[...] = dot(maps[...].T, low).astype(BF16)
    for copy in store_blocks(places, grad, parts, sems):
        copy.wait()


def project_gradient(live, places, n_blocks, maps, own, other, pre, bn, totals, after):
    rows = maps.shape[1]
    parts = grad_shapes(n_blocks, rows, D)
    out = pl.pallas_call(
        functools.partial(project_grad_kernel, len(parts), len(after)),
        out_shape=parts + [jax.ShapeDtypeStruct((TLEN, D), BF16)],
        in_specs=[SMEM, SMEM] + [VMEM] * 6 + [ANY] * len(after),
        out_specs=[ANY] * len(parts) + [VMEM],
        scratch_shapes=[
            pltpu.VMEM((rows, D), BF16),
            pltpu.SemaphoreType.DMA((16,)),
        ],
        compiler_params=params(60),
        cost_estimate=cost(5),
        name="project_gradient",
    )(live, places, maps, own, other, pre, bn, totals, *after)
    return out[:-1], out[-1]


def nesterov(weight, moment, average, gradient, rate):
    moment_new = MOMENTUM * moment + gradient
    weight_new = weight - rate * (gradient + MOMENTUM * moment_new)
    return (weight_new, moment_new, AVERAGE * average + (1.0 - AVERAGE) * weight_new)


def stats_kernel(n_after, live, own, other, *refs):
    pre, stats = refs[n_after:]
    total = (own[...].astype(F32) + other[...].astype(F32)).astype(BF16).astype(F32)
    pre[...] = total
    count = live[0].astype(F32)
    mask = lax.broadcasted_iota(jnp.int32, (TLEN, 1), 0) < live[0]
    mean = jnp.sum(jnp.where(mask, total, 0.0), axis=0, keepdims=True) / count
    centre = jnp.where(mask, total - mean, 0.0)
    stats[...] = jnp.concatenate(
        [
            mean,
            jnp.sum(centre * centre, axis=0, keepdims=True),
            jnp.full((6, D), count, F32),
        ],
        axis=0,
    )


def local_stats(live, own, other, after):
    return pl.pallas_call(
        functools.partial(stats_kernel, len(after)),
        out_shape=[
            jax.ShapeDtypeStruct((TLEN, D), F32),
            jax.ShapeDtypeStruct((8, D), F32),
        ],
        in_specs=[SMEM, VMEM, VMEM] + [ANY] * len(after),
        out_specs=[VMEM, VMEM],
        compiler_params=params(60),
        cost_estimate=cost(40),
        name="local_statistics",
    )(live, own, other, *after)


def exchange_steps():
    bit, n = 1, lax.axis_size("batch")
    while bit < n:
        partners = [bit] if 2 * bit == n else [bit, 2 * bit, 3 * bit]
        bit *= 2 * len(partners) if len(partners) == 1 else 4
        yield partners, bit >= n


def merge_kernel(count, last, *refs):
    parts, out = refs[:count], refs[-1]
    total = parts[0][2:3, :]
    mean = parts[0][0:1, :] * total
    for part in parts[1:]:
        total = total + part[2:3, :]
        mean = mean + part[0:1, :] * part[2:3, :]
    mean = mean / total
    spread = jnp.zeros_like(mean)
    for part in parts:
        gap = part[0:1, :] - mean
        spread = spread + part[1:2, :] + gap * gap * part[2:3, :]
    out[0:1, :] = mean
    out[1:2, :] = spread
    out[2:8, :] = jnp.broadcast_to(total, (6, D))
    if last:
        out[1:2, :] = lax.rsqrt(spread / total + EPS)
        out[2:4, :] = refs[count][0:2, :]


def merge_stats(stats, gains, after):
    for partners, last in exchange_steps():
        parts = [stats] + [swap(stats, bit) for bit in partners]
        operands = parts + ([gains] if last else [])
        stats = pl.pallas_call(
            functools.partial(merge_kernel, len(parts), last),
            out_shape=jax.ShapeDtypeStruct((8, D), F32),
            in_specs=[VMEM] * len(operands) + [ANY] * len(after),
            out_specs=VMEM,
            cost_estimate=cost(15),
            name="merge_statistics",
        )(*operands, *after)
        after = []
    return stats


def add_kernel(count, *refs):
    total = refs[0][...]
    for part in refs[1:count]:
        total = total + part[...]
    refs[-1][...] = total


def sum_small(values, after, begin=0, end=None):
    for step, (partners, _) in enumerate(list(exchange_steps())[begin:end]):
        parts = [values] + [swap(values, bit) for bit in partners]
        ties = after[step] if step < len(after) else []
        values = pl.pallas_call(
            functools.partial(add_kernel, len(parts)),
            out_shape=jax.ShapeDtypeStruct(values.shape, F32),
            in_specs=[VMEM] * len(parts) + [ANY] * len(ties),
            out_specs=VMEM,
            cost_estimate=cost(0.5),
            name="sum_small",
        )(*parts, *ties)
    return values


def on_device(
    text_embed,
    visual_maps,
    visual_bucket,
    rel_bucket,
    joined_grad,
    attn_weight,
    attn_moment,
    attn_average,
    ffn_weight,
    ffn_moment,
    ffn_average,
    vector_weight,
    vector_moment,
    vector_average,
    project_weight,
    project_moment,
    project_average,
    shared_weight,
    shared_moment,
    shared_average,
):
    n_batch = lax.axis_size("batch")
    me = lax.axis_index("batch")
    ringed = n_batch == 16
    is_text = lax.axis_index("stream") == 0
    maps = visual_maps.reshape(TLEN, -1)

    small = jnp.zeros((16, D), BF16)
    small = small.at[0, : vector_weight.shape[1]].set(vector_weight[0].astype(BF16))
    small = small.at[1, : shared_weight.shape[0]].set(shared_weight.astype(BF16))
    attn_low = rounded(attn_weight[0], [])
    attn_full = lax.all_gather(attn_low, "batch", axis=0, tiled=True)
    packed = jnp.concatenate([project_weight.astype(BF16), small], axis=0)
    if ringed:
        sources = jnp.asarray(gather_sources())[me]
        targets = jnp.asarray(scatter_targets())[me]
        project_blocks = ring_gather(packed)
        ffn_low = rounded(ffn_weight[0], project_blocks[5:7])
        ffn_blocks = ring_gather(ffn_low, FF)
        n_blocks = 16
    else:
        sources = jnp.zeros((1,), jnp.int32)
        targets = jnp.zeros((1,), jnp.int32)
        rows = lax.all_gather(project_weight.astype(BF16), "batch", axis=0, tiled=True)
        project_blocks = [jnp.concatenate([rows, jnp.zeros((16, D), BF16)], axis=0)]
        ffn_low = rounded(ffn_weight[0], [])
        ffn_blocks = [lax.all_gather(ffn_low, "batch", axis=0, tiled=True)]
        n_blocks = 1

    partial_pre, project_half, small_all = project(sources, maps, jnp.stack(project_blocks))
    if not ringed:
        small_all = lax.all_gather(small, "batch", axis=0, tiled=False)
    other_pre = across(partial_pre)
    vector_rows = small_all[:, 0, : vector_weight.shape[1]].reshape(12, D).astype(F32)
    vec = jnp.concatenate([vector_rows, jnp.zeros((4, D), F32)], axis=0)
    shared_full = small_all[:, 1, : shared_weight.shape[0]].reshape(-1).astype(F32)
    table = jnp.zeros((16, 128), F32)
    table = table.at[:HEADS, :BUCKETS].set(
        shared_full[: BUCKETS * HEADS].reshape(BUCKETS, HEADS).T
    )
    gains = shared_full[BUCKETS * HEADS :].reshape(2, D)

    bucket = rel_bucket.reshape(TLEN, TLEN)
    bias = spatial_bias(bucket, table, [])
    visual_len = ((visual_bucket + 1) * (TLEN // 2)).astype(jnp.int32)
    pre, stats = local_stats(
        visual_len, partial_pre, other_pre, [bias] + (ffn_blocks[1:3] if ringed else [])
    )
    bn = merge_stats(stats, gains, ffn_blocks[3:5] if ringed else [])
    text = is_text.astype(jnp.int32)
    live = jnp.stack([jnp.where(is_text, TLEN, visual_len[0]), text])
    visual_live = jnp.stack([visual_len[0], text])

    qkv, probs, x_low, query_t, ctx, normed, inverse = attn_fwd(
        live,
        attn_full,
        bias,
        text_embed.reshape(TLEN, D),
        pre,
        bn,
        vec,
        ffn_blocks[5:7] if ringed else [],
    )
    ffn_part, result, grad_residual, grad_attended, grad_ctx, grad_ctx_t, grads = feed_forward(
        live,
        sources,
        ffn_blocks,
        attn_full,
        normed,
        inverse,
        vec,
        joined_grad.reshape(TLEN, D),
    )
    result_other = across(result)
    joined = result + result_other
    ffn_sum, _ = reduce_grad([ffn_part[None]])
    queries, keys_t, values_t, score_grads = (
        [piece]
        for piece in attn_bwd_pairs(0, PAIRS, qkv, grad_ctx, ctx, grad_ctx_t, query_t, probs, [])
    )
    grad_qkv, grad_input, grad_bn, sums = attn_bwd_input(
        visual_live,
        attn_full,
        grads,
        grad_residual,
        pre,
        bn,
        queries,
        keys_t,
        values_t,
        [result_other],
    )

    grad_bn_other = across(grad_bn)
    sums = table_grad(bucket, sums, score_grads, [])
    attn_parts = outer(
        targets,
        n_blocks,
        [x_low, ctx],
        [grad_qkv, grad_attended],
        [],
    )
    attn_sum, sent = reduce_grad(attn_parts)
    sums = sum_small(sums, [[attn_parts[0]], sent])
    shared_sums = sums[8:]
    shared_sums = (shared_sums + across(shared_sums))[4:7]
    project_parts, grad_pre = project_gradient(
        visual_live,
        targets,
        n_blocks,
        maps,
        grad_bn,
        grad_bn_other,
        pre,
        bn,
        shared_sums[:2],
        [],
    )
    project_grad, _ = reduce_grad(project_parts)
    ffn_grad, attn_grad = ffn_sum[None], attn_sum[None]
    grad_maps = dot_nt(grad_pre, project_half)
    width = shared_weight.shape[0]
    own_shared = lax.dynamic_slice(
        jnp.concatenate([shared_sums[2, : BUCKETS * HEADS], shared_sums[0], shared_sums[1]]),
        (me * width,),
        (width,),
    )

    all_tokens = n_batch * TLEN
    rate_attention = 1.5 / math.sqrt(D * all_tokens)
    rate_matrix = 0.6 / math.sqrt(D * all_tokens)
    rate_vector = 0.12 / math.sqrt(all_tokens)
    width = vector_weight.shape[1]
    vector_grad = lax.dynamic_slice(sums[:12].reshape(-1), (me * width,), (width,))[None]
    vector_new = nesterov(vector_weight, vector_moment, vector_average, vector_grad, rate_vector)
    ffn_new = nesterov(ffn_weight, ffn_moment, ffn_average, ffn_grad, rate_matrix)
    attn_new = nesterov(attn_weight, attn_moment, attn_average, attn_grad, rate_attention)
    project_new = nesterov(
        project_weight, project_moment, project_average, project_grad, rate_matrix
    )
    shared_new = nesterov(shared_weight, shared_moment, shared_average, own_shared, rate_vector)
    return (
        joined.reshape(1, TLEN, D),
        grad_input.reshape(1, 1, TLEN, D),
        grad_maps.reshape(1, TLEN, -1),
        attn_new[0],
        attn_new[1],
        attn_new[2],
        ffn_new[0],
        ffn_new[1],
        ffn_new[2],
        vector_new[0],
        vector_new[1],
        vector_new[2],
        project_new[0],
        project_new[1],
        project_new[2],
        shared_new[0],
        shared_new[1],
        shared_new[2],
    )


def solution(mesh):
    return jax.shard_map(
        on_device,
        mesh=mesh,
        in_specs=(
            P("batch", None, None),
            P("batch", None, "stream"),
            P("batch"),
            P("stream", "batch", None, None),
            P("batch", None, None),
            P("stream", "batch", None),
            P("stream", "batch", None),
            P("stream", "batch", None),
            P("stream", "batch", None),
            P("stream", "batch", None),
            P("stream", "batch", None),
            P("stream", "batch"),
            P("stream", "batch"),
            P("stream", "batch"),
            P(("stream", "batch"), None),
            P(("stream", "batch"), None),
            P(("stream", "batch"), None),
            P("batch"),
            P("batch"),
            P("batch"),
        ),
        out_specs=(
            P("batch", None, None),
            P("stream", "batch", None, None),
            P("batch", None, "stream"),
            P("stream", "batch", None),
            P("stream", "batch", None),
            P("stream", "batch", None),
            P("stream", "batch", None),
            P("stream", "batch", None),
            P("stream", "batch", None),
            P("stream", "batch"),
            P("stream", "batch"),
            P("stream", "batch"),
            P(("stream", "batch"), None),
            P(("stream", "batch"), None),
            P(("stream", "batch"), None),
            P("batch"),
            P("batch"),
            P("batch"),
        ),
        check_vma=False,
    )
```

```python
import functools
import math

import jax
import jax.numpy as jnp
import numpy as np
from jax import lax
from jax.experimental import pallas as pl
from jax.experimental.pallas import tpu as pltpu
from jax.sharding import PartitionSpec as P

D = 768
HEADS = 12
HEAD_DIM = 64
FF = 3072
TLEN = 512
BUCKETS = 32
PAIRS = HEADS // 2
ROWS = 128
SOFT = 128
STEPS = TLEN // ROWS
CHUNKS = FF // D

EPS = 1e-05
MOMENTUM = 0.9
AVERAGE = 0.95
SCALE = HEAD_DIM ** (-0.5)

BF16 = jnp.bfloat16
F32 = jnp.float32
ANY = pl.BlockSpec(memory_space=pl.ANY)
SMEM = pl.BlockSpec(memory_space=pltpu.SMEM)
VMEM = pl.BlockSpec(memory_space=pltpu.VMEM)
MIB = 1024 * 1024

CYCLE = ((0, 0), (1, 0), (2, 0), (3, 0), (3, 1), (2, 1), (1, 1), (0, 1))
CHIP = [z * 2 + y for z, y in CYCLE]
PLACE = [CHIP.index(k) for k in range(8)]


def cycle_perm(shift):
    return [
        (CHIP[r] * 2 + c, CHIP[(r + shift) % 8] * 2 + c) for r in range(8) for c in range(2)
    ]


def across(v):
    return lax.ppermute(v, "stream", [(0, 1), (1, 0)])


def swap(v, bit):
    n = lax.axis_size("batch")
    return lax.ppermute(v, "batch", [(i, i ^ bit) for i in range(n)])


def gather_shifts():
    return [0, -1, 1, -2, 2, -3, 3, -4]


def gather_sources():
    table = np.zeros((16, 16), np.int32)
    for b in range(16):
        place, core = PLACE[b // 2], b % 2
        for slot, shift in enumerate(gather_shifts()):
            chip = CHIP[(place + shift) % 8]
            table[b, slot] = chip * 2 + core
            table[b, 8 + slot] = chip * 2 + 1 - core
    return table


def scatter_targets():
    table = np.zeros((16, 16), np.int32)
    for b in range(16):
        place, core = PLACE[b // 2], b % 2
        for ahead in range(8):
            chip = CHIP[(place + ahead) % 8]
            table[b, ahead] = chip * 2 + core
            table[b, 8 + ahead] = chip * 2 + 1 - core
    return table


def tie(values, after):
    return pl.pallas_call(
        lambda *refs: None,
        out_shape=[jax.ShapeDtypeStruct(value.shape, value.dtype) for value in values],
        in_specs=[ANY] * (len(values) + len(after)),
        out_specs=[ANY] * len(values),
        input_output_aliases={i: i for i in range(len(values))},
        compiler_params=params(1),
        cost_estimate=cost(0),
        name="tie",
    )(*values, *after)


def ring_gather(block, split=0):
    up, down = cycle_perm(1), cycle_perm(-1)
    low = high = block
    own = [block]
    for _ in range(3):
        low = lax.ppermute(low, "batch", up)
        high = lax.ppermute(high, "batch", down)
        own += [low, high]
    if split:
        own.append(lax.ppermute(low[:, :split], "batch", up))
        own.append(lax.ppermute(high[:, split:], "batch", down))
    else:
        own.append(lax.ppermute(low, "batch", up))
    return own


def swapped(blocks):
    return [swap(v, 1) for v in blocks]


class RingSum:
    def __init__(self, parts):
        self.mine, self.other = parts[0], swap(parts[1], 1)
        self.low, self.high = self.term(4).astype(BF16), self.term(5).astype(BF16)
        self.ahead = 4

    def term(self, j):
        return self.mine[j].astype(F32) + self.other[j].astype(F32)

    def step(self, after=()):
        low = lax.ppermute(self.low, "batch", cycle_perm(1))
        high = lax.ppermute(self.high, "batch", cycle_perm(-1))
        if after:
            low, high = tie([low, high], list(after))
        self.ahead -= 1
        self.low = (low.astype(F32) + self.term(self.ahead)).astype(BF16)
        if self.ahead > 1:
            self.high = (high.astype(F32) + self.term(9 - self.ahead)).astype(BF16)
        else:
            self.high = high
        return [self.low]

    def finish(self):
        low = lax.ppermute(self.low, "batch", cycle_perm(1))
        return low.astype(F32) + self.high.astype(F32) + self.term(0)


def scatter_sum(whole):
    return lax.psum_scatter(whole, "batch", scatter_dimension=0, tiled=True).astype(F32)


def dot(left, right):
    return jnp.dot(left, right, preferred_element_type=F32)


def dot_nt(left, right):
    return lax.dot_general(left, right, (((1,), (1,)), ((), ())), preferred_element_type=F32)


def store_blocks(offs, src, parts, sems):
    copies = []
    if len(parts) == 1:
        copies.append(pltpu.make_async_copy(src, parts[0].at[0], sems.at[0]))
    else:
        rows = src.shape[0] // 16
        for k in range(16):
            at = pl.multiple_of(offs[k] * rows, 16)
            place = parts[k // 8].at[k % 8]
            copies.append(pltpu.make_async_copy(src.at[pl.ds(at, rows), :], place, sems.at[k]))
    for copy in copies:
        copy.start()
    return copies


def grad_shapes(n_blocks, rows, cols):
    if n_blocks == 1:
        return [jax.ShapeDtypeStruct((1, rows, cols), BF16)]
    return [jax.ShapeDtypeStruct((8, rows // 16, cols), BF16)] * 2


def params(mib):
    return pltpu.CompilerParams(vmem_limit_bytes=mib * MIB)


def cost(micros):
    return pl.CostEstimate(flops=int(micros * 1e9), bytes_accessed=0, transcendentals=0)


def norm_rows(values):
    centre = values - jnp.mean(values, axis=-1, keepdims=True)
    inverse = lax.rsqrt(jnp.mean(centre * centre, axis=-1, keepdims=True) + EPS)
    return centre * inverse, inverse


def norm_back(upstream, normed, inverse, gain):
    scaled = upstream * gain
    return inverse * (
        scaled
        - jnp.mean(scaled, axis=-1, keepdims=True)
        - normed * jnp.mean(scaled * normed, axis=-1, keepdims=True)
    )


def half_mask(rows, half):
    lane = lax.broadcasted_iota(jnp.int32, (rows, 128), 1)
    return (lane < HEAD_DIM) if half == 0 else (lane >= HEAD_DIM)


def round_kernel(n_after, weight, *refs):
    refs[n_after][...] = weight[...].astype(BF16)


def rounded(weight, after):
    return pl.pallas_call(
        functools.partial(round_kernel, len(after)),
        out_shape=jax.ShapeDtypeStruct(weight.shape, BF16),
        in_specs=[VMEM] + [ANY] * len(after),
        out_specs=VMEM,
        compiler_params=params(60),
        cost_estimate=cost(1),
        name="round_weight",
    )(weight, *after)


def project_kernel(n_blocks, offs, maps, blocks, pre, whole, small, sems, small_sems):
    copies = []
    rows = whole.shape[0] // n_blocks
    for i in range(n_blocks):
        block = blocks.at[i]
        which = offs[i] if n_blocks > 1 else 0
        at = pl.multiple_of(which * rows, 16)
        copies.append(
            pltpu.make_async_copy(block.at[pl.ds(0, rows), :], whole.at[pl.ds(at, rows), :], sems.at[i])
        )
        copies.append(
            pltpu.make_async_copy(block.at[pl.ds(rows, 16), :], small.at[which], small_sems.at[i])
        )
    for copy in copies:
        copy.start()
    for copy in copies:
        copy.wait()
    for i in range(2):
        pick = pl.ds(i * (TLEN // 2), TLEN // 2)
        pre[pick, :] = dot(maps[pick, :], whole[...]).astype(BF16)


def project(offs, maps, blocks):
    n = blocks.shape[0]
    rows = blocks.shape[1] - 16
    channels = n * rows
    return pl.pallas_call(
        functools.partial(project_kernel, n),
        out_shape=[
            jax.ShapeDtypeStruct((TLEN, D), BF16),
            jax.ShapeDtypeStruct((channels, D), BF16),
            jax.ShapeDtypeStruct((n, 16, D), BF16),
        ],
        in_specs=[SMEM, VMEM, ANY],
        out_specs=[VMEM] * 3,
        scratch_shapes=[pltpu.SemaphoreType.DMA((n,)), pltpu.SemaphoreType.DMA((n,))],
        compiler_params=params(60),
        cost_estimate=cost(60),
        name="project_maps",
    )(offs, maps, blocks)


def bias_kernel(n_after, bucket, table, *refs):
    bias = refs[n_after]
    for t in range(TLEN // 128):
        lanes = slice(t * 128, (t + 1) * 128)
        which = bucket[:, lanes]
        for head in range(HEADS):
            row = jnp.broadcast_to(table[head : head + 1, :], which.shape)
            bias[head, :, lanes] = jnp.take_along_axis(row, which, axis=1).astype(BF16)


def spatial_bias(bucket, table, after):
    rows = 64
    return pl.pallas_call(
        functools.partial(bias_kernel, len(after)),
        grid=(TLEN // rows,),
        out_shape=jax.ShapeDtypeStruct((HEADS, TLEN, TLEN), BF16),
        in_specs=[
            pl.BlockSpec((rows, TLEN), lambda i: (i, 0)),
            pl.BlockSpec((16, 128), lambda i: (0, 0)),
        ]
        + [ANY] * len(after),
        out_specs=pl.BlockSpec((HEADS, rows, TLEN), lambda i: (0, i, 0)),
        compiler_params=params(60),
        cost_estimate=cost(5),
        name="spatial_bias",
    )(bucket, table, *after)


def attn_fwd_kernel(n_after, live, attn, bias, text, pre, bn, vec, *refs):
    qkv_out, probs, x_out, query_t, ctx, normed, inverse = refs[n_after : n_after + 7]
    weight, qkv, score_a, score_b, prob_a, prob_b, ctx_a, sems, in_sems, out_sems = refs[n_after + 7 :]
    loads = []
    for part in range(4):
        cols = pl.ds(part * D, D)
        loads.append(pltpu.make_async_copy(attn.at[:, cols], weight.at[:, cols], sems.at[part]))
        loads[-1].start()

    def bring(head):
        place = (prob_a, prob_b)[head % 2].at[head // 2]
        return pltpu.make_async_copy(bias.at[head], place, in_sems.at[head])

    for head in range(HEADS):
        bring(head).start()
    alive = lax.broadcasted_iota(jnp.int32, (TLEN, 1), 0) < live[0]
    visual = (pre[...] - bn[0:1, :]) * bn[1:2, :] * bn[2:3, :] + bn[3:4, :]
    x = jnp.where(live[1] == 1, text[...].astype(F32), jnp.where(alive, visual, 0.0))
    x_low = x.astype(BF16)
    x_out[...] = x_low
    exports = []
    for part in range(3):
        cols = slice(part * D, (part + 1) * D)
        loads[part].wait()
        value = dot(x_low, weight[:, cols])
        if part != 1:
            value = value + vec[part // 2 : part // 2 + 1, :]
        qkv[:, cols] = value.astype(BF16)
        exports.append(
            pltpu.make_async_copy(qkv.at[:, cols], qkv_out.at[:, cols], out_sems.at[HEADS + part])
        )
        exports[-1].start()

    def lanes(start, pair):
        return pl.ds(pl.multiple_of(start + pair * 128, 128), 128)

    def scores(pair, half, out):
        query = qkv[:, lanes(0, pair)] * SCALE
        query = jnp.where(half_mask(TLEN, half), query, jnp.zeros_like(query))
        out[...] = dot_nt(query, qkv[:, lanes(D, pair)])

    def softmax(score, prob, pair):
        key_valid = lax.broadcasted_iota(jnp.int32, (SOFT, TLEN), 1) < live[0]
        for i in range(TLEN // SOFT):
            rows = slice(i * SOFT, (i + 1) * SOFT)
            value = score[rows, :] + prob[pair, rows, :].astype(F32)
            value = jnp.where(key_valid, value, -1000000000.0)
            peak = jnp.max(value, axis=-1, keepdims=True)
            raised = jnp.exp(value - peak)
            total = jnp.sum(raised, axis=-1, keepdims=True)
            prob[pair, rows, :] = (raised * (1.0 / total)).astype(BF16)

    scores(0, 0, score_a)
    for head in range(HEADS):
        bring(head).wait()

    def step(pair, carry):
        values = qkv[:, lanes(2 * D, pair)]
        scores(pair, 1, score_b)
        softmax(score_a, prob_a, pair)
        scores(jnp.minimum(pair + 1, PAIRS - 1), 0, score_a)
        ctx_a[...] = dot(prob_a[pair], values)
        softmax(score_b, prob_b, pair)
        ctx_b = dot(prob_b[pair], values)
        ctx[:, lanes(0, pair)] = jnp.where(half_mask(TLEN, 0), ctx_a[...], ctx_b).astype(BF16)
        for half, prob in enumerate((prob_a, prob_b)):
            head = 2 * pair + half
            pltpu.make_async_copy(prob.at[pair], probs.at[head], out_sems.at[head]).start()
        return carry

    lax.fori_loop(0, PAIRS, step, 0)
    loads[3].wait()
    att = dot(ctx[...], weight[:, 3 * D :]) + vec[2:3, :]
    query_t[...] = (qkv[:, :D] * SCALE).T
    normal, inv = norm_rows(x + att)
    normed[...] = normal
    inverse[...] = jnp.broadcast_to(inv, (TLEN, 128))
    for copy in exports:
        copy.wait()
    for head in range(HEADS):
        prob = (prob_a, prob_b)[head % 2]
        pltpu.make_async_copy(prob.at[head // 2], probs.at[head], out_sems.at[head]).wait()


def attn_fwd(live, attn, bias, text, pre, bn, vec, after):
    return pl.pallas_call(
        functools.partial(attn_fwd_kernel, len(after)),
        out_shape=[
            jax.ShapeDtypeStruct((TLEN, 3 * D), BF16),
            jax.ShapeDtypeStruct((HEADS, TLEN, TLEN), BF16),
            jax.ShapeDtypeStruct((TLEN, D), BF16),
            jax.ShapeDtypeStruct((D, TLEN), BF16),
            jax.ShapeDtypeStruct((TLEN, D), BF16),
            jax.ShapeDtypeStruct((TLEN, D), F32),
            jax.ShapeDtypeStruct((TLEN, 128), F32),
        ],
        in_specs=[SMEM, ANY, ANY] + [VMEM] * 4 + [ANY] * len(after),
        out_specs=[ANY, ANY] + [VMEM] * 5,
        scratch_shapes=[
            pltpu.VMEM((D, 4 * D), BF16),
            pltpu.VMEM((TLEN, 3 * D), BF16),
            pltpu.VMEM((TLEN, TLEN), F32),
            pltpu.VMEM((TLEN, TLEN), F32),
            pltpu.VMEM((PAIRS, TLEN, TLEN), BF16),
            pltpu.VMEM((PAIRS, TLEN, TLEN), BF16),
            pltpu.VMEM((TLEN, 128), F32),
            pltpu.SemaphoreType.DMA((4,)),
            pltpu.SemaphoreType.DMA((HEADS,)),
            pltpu.SemaphoreType.DMA((HEADS + 3,)),
        ],
        compiler_params=params(60),
        cost_estimate=cost(15),
        name="attention_forward",
    )(live, attn, bias, text, pre, bn, vec, *after)


def load_ffn(offs, blocks, up, down, sems):
    first, second = [], []
    if len(blocks) == 1:
        first.append(pltpu.make_async_copy(blocks[0].at[:, pl.ds(0, FF)], up, sems.at[0]))
        second.append(pltpu.make_async_copy(blocks[0].at[:, pl.ds(FF, FF)], down, sems.at[1]))
        return first, second
    at = 0
    for slot in range(16):
        rows = pl.ds(pl.multiple_of(offs[slot] * 48, 16), 48)
        if slot % 8 < 7:
            left, right = blocks[at].at[:, pl.ds(0, FF)], blocks[at].at[:, pl.ds(FF, FF)]
            at += 1
        else:
            left, right = blocks[at], blocks[at + 1]
            at += 2
        first.append(pltpu.make_async_copy(left, up.at[rows, :], sems.at[2 * slot]))
        second.append(pltpu.make_async_copy(right, down.at[rows, :], sems.at[2 * slot + 1]))
    return first, second


def ffn_kernel(n_blocks, live, offs, attn, normed, inverse, vec, joined_grad, *refs):
    blocks, refs = refs[:n_blocks], refs[n_blocks:]
    part, refs = refs[0], refs[1:]
    result, grad_residual, grad_attended, grad_ctx, grad_ctx_t, grads = refs[:6]
    up, down, active, slope, grad, total, weight, sems, last_sems, out_sems = refs[6:]
    loads = load_ffn(offs, blocks, up, down, sems)
    for copy in loads[0] + loads[1]:
        copy.start()
    last = pltpu.make_async_copy(attn.at[:, pl.ds(3 * D, D)], weight, last_sems.at[0])
    last.start()
    first = normed[...] * vec[3:4, :] + vec[4:5, :]
    first_low = first.astype(BF16)
    for copy in loads[0]:
        copy.wait()
    units = dot(first_low, up[:, :D])
    total[...] = first + vec[9:10, :]
    for k in range(CHUNKS):
        units = units + vec[5 + k : 6 + k, :]
        if k + 1 < CHUNKS:
            following = dot(first_low, up[:, (k + 1) * D : (k + 2) * D])
        square = units * units
        root = math.sqrt(2.0 / math.pi)
        bend = jnp.tanh(root * units * (1.0 + 0.044715 * square))
        half = 0.5 * (1.0 + bend)
        active[k] = (units * half).astype(BF16)
        slope[k] = (
            half + 0.5 * root * units * (1.0 - bend * bend) * (1.0 + 3.0 * 0.044715 * square)
        ).astype(BF16)
        if k == 0:
            for copy in loads[1]:
                copy.wait()
        total[...] += dot_nt(active[k], down[:, k * D : (k + 1) * D])
        if k + 1 < CHUNKS:
            units = following
    normal, inv = norm_rows(total[...])
    mask = lax.broadcasted_iota(jnp.int32, (TLEN, 1), 0) < live[0]
    result[...] = jnp.where(mask, normal * vec[10:11, :] + vec[11:12, :], 0.0).astype(BF16)
    upstream = jnp.where(mask, joined_grad[...].astype(F32), 0.0)
    second = norm_back(upstream, normal, inv, vec[10:11, :])
    second_low = second.astype(BF16)
    total[...] = second
    grads[9:10, :] = jnp.sum(second_low.astype(F32), axis=0, keepdims=True)
    grads[10:11, :] = jnp.sum(upstream * normal, axis=0, keepdims=True)
    grads[11:12, :] = jnp.sum(upstream, axis=0, keepdims=True)
    turned = second_low.T
    for k in range(CHUNKS):
        cols = slice(FF + k * D, FF + (k + 1) * D)
        grad[:, cols] = dot(turned, active[k]).astype(BF16)
    cols = pl.ds(FF, FF)
    copies = [pltpu.make_async_copy(grad.at[:, cols], part.at[:, cols], out_sems.at[0])]
    copies[0].start()
    turned = first_low.T
    for k in range(CHUNKS):
        cols = slice(k * D, (k + 1) * D)
        inner = (dot(second_low, down[:, cols]) * slope[k].astype(F32)).astype(BF16)
        grads[5 + k : 6 + k, :] = jnp.sum(inner.astype(F32), axis=0, keepdims=True)
        total[...] += dot_nt(inner, up[:, cols])
        grad[:, cols] = dot(turned, inner).astype(BF16)
    cols = pl.ds(0, FF)
    copies.append(pltpu.make_async_copy(grad.at[:, cols], part.at[:, cols], out_sems.at[1]))
    copies[-1].start()
    upstream = total[...]
    grads[3:4, :] = jnp.sum(upstream * normed[...], axis=0, keepdims=True)
    grads[4:5, :] = jnp.sum(upstream, axis=0, keepdims=True)
    residual = norm_back(upstream, normed[...], inverse[:, 0:1], vec[3:4, :])
    grad_residual[...] = residual
    attended = residual.astype(BF16)
    grad_attended[...] = attended
    grads[2:3, :] = jnp.sum(attended.astype(F32), axis=0, keepdims=True)
    grads[0:2, :] = jnp.zeros((2, D), F32)
    grads[12:16, :] = jnp.zeros((4, D), F32)
    last.wait()
    back = dot_nt(attended, weight[...]).astype(BF16)
    grad_ctx[...] = back
    grad_ctx_t[...] = back.T
    for copy in copies:
        copy.wait()


def feed_forward(live, offs, blocks, attn, normed, inverse, vec, joined_grad):
    n = len(blocks)
    out = pl.pallas_call(
        functools.partial(ffn_kernel, n),
        out_shape=[
            jax.ShapeDtypeStruct((D, 2 * FF), BF16),
            jax.ShapeDtypeStruct((TLEN, D), BF16),
            jax.ShapeDtypeStruct((TLEN, D), F32),
            jax.ShapeDtypeStruct((TLEN, D), BF16),
            jax.ShapeDtypeStruct((TLEN, D), BF16),
            jax.ShapeDtypeStruct((D, TLEN), BF16),
            jax.ShapeDtypeStruct((16, D), F32),
        ],
        in_specs=[SMEM, SMEM, ANY] + [VMEM] * 4 + [ANY] * n,
        out_specs=[ANY] + [VMEM] * 6,
        scratch_shapes=[
            pltpu.VMEM((D, FF), BF16),
            pltpu.VMEM((D, FF), BF16),
            pltpu.VMEM((CHUNKS, TLEN, D), BF16),
            pltpu.VMEM((CHUNKS, TLEN, D), BF16),
            pltpu.VMEM((D, 2 * FF), BF16),
            pltpu.VMEM((TLEN, D), F32),
            pltpu.VMEM((D, D), BF16),
            pltpu.SemaphoreType.DMA((32,)),
            pltpu.SemaphoreType.DMA((1,)),
            pltpu.SemaphoreType.DMA((2,)),
        ],
        compiler_params=params(60),
        cost_estimate=cost(30),
        name="feed_forward",
    )(live, offs, attn, normed, inverse, vec, joined_grad, *blocks)
    return out


def pairs_kernel(n_after, keys, values, back, context, back_t, query_t, probs, *refs):
    grad_query, grad_key_t, grad_value_t, grad_scores = refs[n_after:]
    total = jnp.zeros((TLEN, 128), F32)
    for half in range(2):
        mask = half_mask(TLEN, half)
        masked = jnp.where(mask, back[...], jnp.zeros_like(back[...]))
        prob = probs[half]
        slopes = dot_nt(masked, values[...])
        delta = jnp.sum(masked.astype(F32) * context[...].astype(F32), axis=-1, keepdims=True)
        slopes = (prob.astype(F32) * (slopes - delta)).astype(BF16)
        grad_scores[half] = slopes
        near = jnp.where(mask, keys[...], jnp.zeros_like(keys[...]))
        total = total + dot(slopes, near)
        lines = slice(half * HEAD_DIM, (half + 1) * HEAD_DIM)
        grad_key_t[lines, :] = dot(query_t[lines, :], slopes).astype(BF16)
        grad_value_t[lines, :] = dot(back_t[lines, :], prob).astype(BF16)
    grad_query[...] = (total * SCALE).astype(BF16)


def attn_bwd_pairs(first, count, qkv, grad_ctx, ctx, grad_ctx_t, query_t, probs, after):
    def cols(base):
        return pl.BlockSpec((TLEN, 128), lambda i: (0, base + i))

    def lines(base):
        return pl.BlockSpec((128, TLEN), lambda i: (base + i, 0))

    def heads(base):
        return pl.BlockSpec((2, TLEN, TLEN), lambda i: (base + i, 0, 0))

    return pl.pallas_call(
        functools.partial(pairs_kernel, len(after)),
        grid=(count,),
        out_shape=[
            jax.ShapeDtypeStruct((TLEN, 128 * count), BF16),
            jax.ShapeDtypeStruct((128 * count, TLEN), BF16),
            jax.ShapeDtypeStruct((128 * count, TLEN), BF16),
            jax.ShapeDtypeStruct((2 * count, TLEN, TLEN), BF16),
        ],
        in_specs=[
            cols(PAIRS + first),
            cols(2 * PAIRS + first),
            cols(first),
            cols(first),
            lines(first),
            lines(first),
            heads(first),
        ]
        + [ANY] * len(after),
        out_specs=[cols(0), lines(0), lines(0), heads(0)],
        compiler_params=params(60),
        cost_estimate=cost(5),
        name="attention_backward",
    )(qkv, qkv, grad_ctx, ctx, grad_ctx_t, query_t, probs, *after)


def input_kernel(n_parts, n_after, live, attn, grads, grad_residual, pre, bn, *refs):
    queries, refs = refs[:n_parts], refs[n_parts:]
    keys_t, refs = refs[:n_parts], refs[n_parts:]
    values_t, refs = refs[:n_parts], refs[n_parts + n_after :]
    grad_qkv, grad_input, grad_bn, sums, weight, sems = refs
    load = pltpu.make_async_copy(attn.at[:, pl.ds(0, 3 * D)], weight, sems.at[0])
    load.start()
    at = 0
    for query, key, value in zip(queries, keys_t, values_t):
        width = query.shape[1]
        grad_qkv[:, at : at + width] = query[...]
        grad_qkv[:, D + at : D + at + width] = key[...].T
        grad_qkv[:, 2 * D + at : 2 * D + at + width] = value[...].T
        at += width
    load.wait()
    total = grad_residual[...] + dot_nt(grad_qkv[...], weight[...])
    grad_input[...] = total
    alive = lax.broadcasted_iota(jnp.int32, (TLEN, 1), 0) < live[0]
    back = jnp.where(jnp.logical_and(alive, live[1] == 0), total, 0.0)
    grad_bn[...] = back.astype(BF16)
    normal = (pre[...] - bn[0:1, :]) * bn[1:2, :]
    sums[...] = grads[...]
    sums[0:1, :] = jnp.sum(grad_qkv[:, :D].astype(F32), axis=0, keepdims=True)
    sums[1:2, :] = jnp.sum(grad_qkv[:, 2 * D :].astype(F32), axis=0, keepdims=True)
    sums[12:13, :] = jnp.sum(back * normal, axis=0, keepdims=True)
    sums[13:14, :] = jnp.sum(back, axis=0, keepdims=True)


def attn_bwd_input(live, attn, grads, grad_residual, pre, bn, queries, keys_t, values_t, after):
    parts = len(queries)
    return pl.pallas_call(
        functools.partial(input_kernel, parts, len(after)),
        out_shape=[
            jax.ShapeDtypeStruct((TLEN, 3 * D), BF16),
            jax.ShapeDtypeStruct((TLEN, D), F32),
            jax.ShapeDtypeStruct((TLEN, D), BF16),
            jax.ShapeDtypeStruct((16, D), F32),
        ],
        in_specs=[SMEM, ANY] + [VMEM] * (3 * parts + 4) + [ANY] * len(after),
        out_specs=[VMEM] * 4,
        scratch_shapes=[pltpu.VMEM((D, 3 * D), BF16), pltpu.SemaphoreType.DMA((1,))],
        compiler_params=params(60),
        cost_estimate=cost(5),
        name="input_gradient",
    )(live, attn, grads, grad_residual, pre, bn, *queries, *keys_t, *values_t, *after)


def table_kernel(n_parts, n_after, bucket, sums, *refs):
    parts, (out, one_hot, total) = refs[:n_parts], refs[n_parts + n_after :]
    step = pl.program_id(0)

    @pl.when(step == 0)
    def _():
        total[...] = jnp.zeros_like(total)

    for group in range(ROWS // 16):
        lines = slice(group * 16, (group + 1) * 16)
        which = bucket[lines, :]
        for b in range(BUCKETS):
            one_hot[b * 16 : (b + 1) * 16, :] = jnp.where(which == b, 1.0, 0.0).astype(BF16)
        slopes = jnp.concatenate(
            [part[:, lines, :].reshape(part.shape[0] * 16, TLEN) for part in parts], axis=0
        )
        total[...] += dot_nt(one_hot[...], slopes)

    @pl.when(step == STEPS - 1)
    def _():
        line = lax.broadcasted_iota(jnp.int32, (BUCKETS * 16, HEADS * 16), 0) % 16
        lane = lax.broadcasted_iota(jnp.int32, (BUCKETS * 16, HEADS * 16), 1) % 16
        kept = jnp.where(line == lane, total[...], 0.0)
        kept = jnp.sum(kept.reshape(BUCKETS, 16, HEADS * 16), axis=1)
        shape = (HEADS * 16, BUCKETS * HEADS)
        head = lax.broadcasted_iota(jnp.int32, shape, 0) // 16
        pick = lax.broadcasted_iota(jnp.int32, shape, 1) % HEADS
        spread = jnp.dot(
            kept,
            jnp.where(head == pick, 1.0, 0.0),
            precision=lax.Precision.HIGHEST,
            preferred_element_type=F32,
        )
        shape = (BUCKETS, BUCKETS * HEADS)
        own = lax.broadcasted_iota(jnp.int32, shape, 1) // HEADS
        spread = jnp.where(own == lax.broadcasted_iota(jnp.int32, shape, 0), spread, 0.0)
        out[...] = sums[...]
        out[14:15, : BUCKETS * HEADS] = jnp.sum(spread, axis=0, keepdims=True)


def table_grad(bucket, sums, parts, after):
    return pl.pallas_call(
        functools.partial(table_kernel, len(parts), len(after)),
        grid=(STEPS,),
        out_shape=jax.ShapeDtypeStruct((16, D), F32),
        in_specs=[
            pl.BlockSpec((ROWS, TLEN), lambda i: (i, 0)),
            pl.BlockSpec((16, D), lambda i: (0, 0)),
        ]
        + [pl.BlockSpec((part.shape[0], ROWS, TLEN), lambda i: (0, i, 0)) for part in parts]
        + [ANY] * len(after),
        out_specs=pl.BlockSpec((16, D), lambda i: (0, 0)),
        scratch_shapes=[
            pltpu.VMEM((BUCKETS * 16, TLEN), BF16),
            pltpu.VMEM((BUCKETS * 16, HEADS * 16), F32),
        ],
        compiler_params=params(60),
        cost_estimate=cost(5),
        name="table_gradient",
    )(bucket, sums, *parts, *after)


def outer_kernel(n_parts, n_after, widths, offs, *refs):
    count = len(widths)
    lefts, rights, refs = refs[:count], refs[count : 2 * count], refs[2 * count + n_after :]
    parts, (grad, sems) = refs[:n_parts], refs[n_parts:]
    at = 0
    for left, right, width in zip(lefts, rights, widths):
        turned = left[...].astype(BF16).T
        for lo in range(0, width, D):
            grad[:, at + lo : at + lo + D] = dot(turned, right[:, lo : lo + D]).astype(BF16)
        at += width
    for copy in store_blocks(offs, grad, parts, sems):
        copy.wait()


def outer(offs, n_blocks, lefts, rights, after):
    widths = tuple(right.shape[1] for right in rights)
    rows = lefts[0].shape[1]
    parts = grad_shapes(n_blocks, rows, sum(widths))
    return pl.pallas_call(
        functools.partial(outer_kernel, len(parts), len(after), widths),
        out_shape=parts,
        in_specs=[SMEM] + [VMEM] * (2 * len(widths)) + [ANY] * len(after),
        out_specs=[ANY] * len(parts),
        scratch_shapes=[
            pltpu.VMEM((rows, sum(widths)), BF16),
            pltpu.SemaphoreType.DMA((16,)),
        ],
        compiler_params=params(60),
        cost_estimate=cost(5),
        name="weight_gradient",
    )(offs, *lefts, *rights, *after)


def project_grad_kernel(n_parts, n_after, live, places, maps, own, other, pre, bn, totals, *refs):
    parts, refs = refs[n_after : n_after + n_parts], refs[n_after + n_parts :]
    grad_pre, grad, sems = refs
    alive = lax.broadcasted_iota(jnp.int32, (TLEN, 1), 0) < live[0]
    normal = (pre[...] - bn[0:1, :]) * bn[1:2, :]
    count = bn[4:5, :]
    back = own[...].astype(F32) + other[...].astype(F32)
    back = back - totals[1:2, :] / count - normal * (totals[0:1, :] / count)
    low = jnp.where(alive, back * (bn[1:2, :] * bn[2:3, :]), 0.0).astype(BF16)
    grad_pre[...] = low
    grad[...] = dot(maps[...].T, low).astype(BF16)
    for copy in store_blocks(places, grad, parts, sems):
        copy.wait()


def project_gradient(live, places, n_blocks, maps, own, other, pre, bn, totals, after):
    rows = maps.shape[1]
    parts = grad_shapes(n_blocks, rows, D)
    out = pl.pallas_call(
        functools.partial(project_grad_kernel, len(parts), len(after)),
        out_shape=parts + [jax.ShapeDtypeStruct((TLEN, D), BF16)],
        in_specs=[SMEM, SMEM] + [VMEM] * 6 + [ANY] * len(after),
        out_specs=[ANY] * len(parts) + [VMEM],
        scratch_shapes=[
            pltpu.VMEM((rows, D), BF16),
            pltpu.SemaphoreType.DMA((16,)),
        ],
        compiler_params=params(60),
        cost_estimate=cost(5),
        name="project_gradient",
    )(live, places, maps, own, other, pre, bn, totals, *after)
    return out[:-1], out[-1]


def maps_kernel(n_after, grad_pre, weight, *refs):
    refs[n_after][...] = dot_nt(grad_pre[...], weight[...])


def maps_gradient(grad_pre, weight, after):
    return pl.pallas_call(
        functools.partial(maps_kernel, len(after)),
        out_shape=jax.ShapeDtypeStruct((TLEN, weight.shape[0]), F32),
        in_specs=[VMEM] * 2 + [ANY] * len(after),
        out_specs=VMEM,
        compiler_params=params(60),
        cost_estimate=cost(1),
        name="maps_gradient",
    )(grad_pre, weight, *after)


def nesterov(weight, moment, average, gradient, rate):
    moment_new = MOMENTUM * moment + gradient
    weight_new = weight - rate * (gradient + MOMENTUM * moment_new)
    return (weight_new, moment_new, AVERAGE * average + (1.0 - AVERAGE) * weight_new)


def stats_kernel(n_after, live, own, other, *refs):
    pre, stats = refs[n_after:]
    total = (own[...].astype(F32) + other[...].astype(F32)).astype(BF16).astype(F32)
    pre[...] = total
    count = live[0].astype(F32)
    mask = lax.broadcasted_iota(jnp.int32, (TLEN, 1), 0) < live[0]
    mean = jnp.sum(jnp.where(mask, total, 0.0), axis=0, keepdims=True) / count
    centre = jnp.where(mask, total - mean, 0.0)
    stats[...] = jnp.concatenate(
        [
            mean,
            jnp.sum(centre * centre, axis=0, keepdims=True),
            jnp.full((6, D), count, F32),
        ],
        axis=0,
    )


def local_stats(live, own, other, after):
    return pl.pallas_call(
        functools.partial(stats_kernel, len(after)),
        out_shape=[
            jax.ShapeDtypeStruct((TLEN, D), F32),
            jax.ShapeDtypeStruct((8, D), F32),
        ],
        in_specs=[SMEM, VMEM, VMEM] + [ANY] * len(after),
        out_specs=[VMEM, VMEM],
        compiler_params=params(60),
        cost_estimate=cost(40),
        name="local_statistics",
    )(live, own, other, *after)


def exchange_steps():
    bit, n = 1, lax.axis_size("batch")
    while bit < n:
        partners = [bit] if 2 * bit == n else [bit, 2 * bit, 3 * bit]
        bit *= 2 * len(partners) if len(partners) == 1 else 4
        yield partners, bit >= n


def merge_kernel(count, last, *refs):
    parts, out = refs[:count], refs[-1]
    total = parts[0][2:3, :]
    mean = parts[0][0:1, :] * total
    for part in parts[1:]:
        total = total + part[2:3, :]
        mean = mean + part[0:1, :] * part[2:3, :]
    mean = mean / total
    spread = jnp.zeros_like(mean)
    for part in parts:
        gap = part[0:1, :] - mean
        spread = spread + part[1:2, :] + gap * gap * part[2:3, :]
    out[0:1, :] = mean
    out[1:2, :] = spread
    out[2:8, :] = jnp.broadcast_to(total, (6, D))
    if last:
        out[1:2, :] = lax.rsqrt(spread / total + EPS)
        out[2:4, :] = refs[count][0:2, :]


def merge_stats(stats, gains, after):
    for partners, last in exchange_steps():
        parts = [stats] + [swap(stats, bit) for bit in partners]
        operands = parts + ([gains] if last else [])
        stats = pl.pallas_call(
            functools.partial(merge_kernel, len(parts), last),
            out_shape=jax.ShapeDtypeStruct((8, D), F32),
            in_specs=[VMEM] * len(operands) + [ANY] * len(after),
            out_specs=VMEM,
            cost_estimate=cost(15),
            name="merge_statistics",
        )(*operands, *after)
        after = []
    return stats


def add_kernel(count, *refs):
    total = refs[0][...]
    for part in refs[1:count]:
        total = total + part[...]
    refs[-1][...] = total


def sum_small(values, after, begin=0, end=None):
    for step, (partners, _) in enumerate(list(exchange_steps())[begin:end]):
        parts = [values] + [swap(values, bit) for bit in partners]
        ties = after[step] if step < len(after) else []
        values = pl.pallas_call(
            functools.partial(add_kernel, len(parts)),
            out_shape=jax.ShapeDtypeStruct(values.shape, F32),
            in_specs=[VMEM] * len(parts) + [ANY] * len(ties),
            out_specs=VMEM,
            cost_estimate=cost(0.5),
            name="sum_small",
        )(*parts, *ties)
    return values


def on_device(
    text_embed,
    visual_maps,
    visual_bucket,
    rel_bucket,
    joined_grad,
    attn_weight,
    attn_moment,
    attn_average,
    ffn_weight,
    ffn_moment,
    ffn_average,
    vector_weight,
    vector_moment,
    vector_average,
    project_weight,
    project_moment,
    project_average,
    shared_weight,
    shared_moment,
    shared_average,
):
    n_batch = lax.axis_size("batch")
    me = lax.axis_index("batch")
    ringed = n_batch == 16
    is_text = lax.axis_index("stream") == 0
    maps = visual_maps.reshape(TLEN, -1)

    small = jnp.zeros((16, D), BF16)
    small = small.at[0, : vector_weight.shape[1]].set(vector_weight[0].astype(BF16))
    small = small.at[1, : shared_weight.shape[0]].set(shared_weight.astype(BF16))
    attn_low = rounded(attn_weight[0], [])
    attn_full = lax.all_gather(attn_low, "batch", axis=0, tiled=True)
    packed = jnp.concatenate([project_weight.astype(BF16), small], axis=0)
    if ringed:
        sources = jnp.asarray(gather_sources())[me]
        targets = jnp.asarray(scatter_targets())[me]
        project_blocks = ring_gather(packed)
        project_blocks += swapped(project_blocks)
        ffn_low = rounded(ffn_weight[0], project_blocks[5:7])
        ffn_blocks = ring_gather(ffn_low, FF)
        ffn_other = swapped(ffn_blocks[:7])
        n_blocks = 16
    else:
        sources = jnp.zeros((1,), jnp.int32)
        targets = jnp.zeros((1,), jnp.int32)
        rows = lax.all_gather(project_weight.astype(BF16), "batch", axis=0, tiled=True)
        project_blocks = [jnp.concatenate([rows, jnp.zeros((16, D), BF16)], axis=0)]
        ffn_low = rounded(ffn_weight[0], [])
        ffn_blocks = [lax.all_gather(ffn_low, "batch", axis=0, tiled=True)]
        n_blocks = 1

    partial_pre, project_half, small_all = project(sources, maps, jnp.stack(project_blocks))
    if not ringed:
        small_all = lax.all_gather(small, "batch", axis=0, tiled=False)
    other_pre = across(partial_pre)
    vector_rows = small_all[:, 0, : vector_weight.shape[1]].reshape(12, D).astype(F32)
    vec = jnp.concatenate([vector_rows, jnp.zeros((4, D), F32)], axis=0)
    shared_full = small_all[:, 1, : shared_weight.shape[0]].reshape(-1).astype(F32)
    table = jnp.zeros((16, 128), F32)
    table = table.at[:HEADS, :BUCKETS].set(
        shared_full[: BUCKETS * HEADS].reshape(BUCKETS, HEADS).T
    )
    gains = shared_full[BUCKETS * HEADS :].reshape(2, D)

    bucket = rel_bucket.reshape(TLEN, TLEN)
    bias = spatial_bias(bucket, table, [])
    visual_len = ((visual_bucket + 1) * (TLEN // 2)).astype(jnp.int32)
    pre, stats = local_stats(
        visual_len, partial_pre, other_pre, [bias] + (ffn_blocks[1:3] if ringed else [])
    )
    bn = merge_stats(stats, gains, ffn_blocks[3:5] if ringed else [])
    text = is_text.astype(jnp.int32)
    live = jnp.stack([jnp.where(is_text, TLEN, visual_len[0]), text])
    visual_live = jnp.stack([visual_len[0], text])

    qkv, probs, x_low, query_t, ctx, normed, inverse = attn_fwd(
        live,
        attn_full,
        bias,
        text_embed.reshape(TLEN, D),
        pre,
        bn,
        vec,
        ffn_blocks[5:7] + ffn_other if ringed else [],
    )
    if ringed:
        ffn_last = list(tie(ffn_blocks[7:], [normed]))
        ffn_blocks = ffn_blocks[:7] + ffn_last + ffn_other + swapped(ffn_last)
    ffn_part, result, grad_residual, grad_attended, grad_ctx, grad_ctx_t, grads = feed_forward(
        live,
        sources,
        ffn_blocks,
        attn_full,
        normed,
        inverse,
        vec,
        joined_grad.reshape(TLEN, D),
    )
    ffn_sum = scatter_sum(ffn_part)
    queries, keys_t, values_t, score_grads = (
        [piece]
        for piece in attn_bwd_pairs(0, PAIRS, qkv, grad_ctx, ctx, grad_ctx_t, query_t, probs, [])
    )
    grad_qkv, grad_input, grad_bn, sums = attn_bwd_input(
        visual_live,
        attn_full,
        grads,
        grad_residual,
        pre,
        bn,
        queries,
        keys_t,
        values_t,
        [],
    )

    grad_bn_other = across(grad_bn)
    sums = table_grad(bucket, sums, score_grads, [])
    attn_parts = outer(
        targets,
        n_blocks,
        [x_low, ctx],
        [grad_qkv, grad_attended],
        [],
    )
    if ringed:
        attn_ring = RingSum(attn_parts)
        sent = [attn_ring.low, attn_ring.high]
    else:
        sent = []
    sums = sum_small(sums, [[attn_parts[0]], sent])
    shared_sums = sums[8:]
    shared_sums = (shared_sums + across(shared_sums))[4:7]
    project_parts, grad_pre = project_gradient(
        visual_live,
        targets,
        n_blocks,
        maps,
        grad_bn,
        grad_bn_other,
        pre,
        bn,
        shared_sums[:2],
        [],
    )
    if ringed:
        project_ring = RingSum(project_parts)
        sent = [project_ring.low, project_ring.high]
        attn_ring.step()
        attn_ring.step(sent)
        project_ring.step()
        later = project_ring.step()
        attn_ring.step(later)
        project_ring.step()
        attn_sum, project_grad = attn_ring.finish(), project_ring.finish()
    else:
        attn_sum, project_grad = scatter_sum(attn_parts[0][0]), scatter_sum(project_parts[0][0])
        sent = []
    ffn_grad, attn_grad = ffn_sum[None], attn_sum[None]
    (result,) = tie([result], sent or [grad_pre])
    joined = result + across(result)
    grad_maps = maps_gradient(grad_pre, project_half, sent)
    width = shared_weight.shape[0]
    own_shared = lax.dynamic_slice(
        jnp.concatenate([shared_sums[2, : BUCKETS * HEADS], shared_sums[0], shared_sums[1]]),
        (me * width,),
        (width,),
    )

    all_tokens = n_batch * TLEN
    rate_attention = 1.5 / math.sqrt(D * all_tokens)
    rate_matrix = 0.6 / math.sqrt(D * all_tokens)
    rate_vector = 0.12 / math.sqrt(all_tokens)
    width = vector_weight.shape[1]
    vector_grad = lax.dynamic_slice(sums[:12].reshape(-1), (me * width,), (width,))[None]
    vector_new = nesterov(vector_weight, vector_moment, vector_average, vector_grad, rate_vector)
    ffn_new = nesterov(ffn_weight, ffn_moment, ffn_average, ffn_grad, rate_matrix)
    attn_new = nesterov(attn_weight, attn_moment, attn_average, attn_grad, rate_attention)
    project_new = nesterov(
        project_weight, project_moment, project_average, project_grad, rate_matrix
    )
    shared_new = nesterov(shared_weight, shared_moment, shared_average, own_shared, rate_vector)
    return (
        joined.reshape(1, TLEN, D),
        grad_input.reshape(1, 1, TLEN, D),
        grad_maps.reshape(1, TLEN, -1),
        attn_new[0],
        attn_new[1],
        attn_new[2],
        ffn_new[0],
        ffn_new[1],
        ffn_new[2],
        vector_new[0],
        vector_new[1],
        vector_new[2],
        project_new[0],
        project_new[1],
        project_new[2],
        shared_new[0],
        shared_new[1],
        shared_new[2],
    )


def solution(mesh):
    return jax.shard_map(
        on_device,
        mesh=mesh,
        in_specs=(
            P("batch", None, None),
            P("batch", None, "stream"),
            P("batch"),
            P("stream", "batch", None, None),
            P("batch", None, None),
            P("stream", "batch", None),
            P("stream", "batch", None),
            P("stream", "batch", None),
            P("stream", "batch", None),
            P("stream", "batch", None),
            P("stream", "batch", None),
            P("stream", "batch"),
            P("stream", "batch"),
            P("stream", "batch"),
            P(("stream", "batch"), None),
            P(("stream", "batch"), None),
            P(("stream", "batch"), None),
            P("batch"),
            P("batch"),
            P("batch"),
        ),
        out_specs=(
            P("batch", None, None),
            P("stream", "batch", None, None),
            P("batch", None, "stream"),
            P("stream", "batch", None),
            P("stream", "batch", None),
            P("stream", "batch", None),
            P("stream", "batch", None),
            P("stream", "batch", None),
            P("stream", "batch", None),
            P("stream", "batch"),
            P("stream", "batch"),
            P("stream", "batch"),
            P(("stream", "batch"), None),
            P(("stream", "batch"), None),
            P(("stream", "batch"), None),
            P("batch"),
            P("batch"),
            P("batch"),
        ),
        check_vma=False,
    )
```

```python
import functools
import math

import jax
import jax.numpy as jnp
import numpy as np
from jax import lax
from jax.experimental import pallas as pl
from jax.experimental.pallas import tpu as pltpu
from jax.sharding import PartitionSpec as P

D = 768
HEADS = 12
HEAD_DIM = 64
FF = 3072
TLEN = 512
BUCKETS = 32
PAIRS = HEADS // 2
ROWS = 128
SOFT = 128
STEPS = TLEN // ROWS
CHUNKS = FF // D

EPS = 1e-05
MOMENTUM = 0.9
AVERAGE = 0.95
SCALE = HEAD_DIM ** (-0.5)

BF16 = jnp.bfloat16
F32 = jnp.float32
ANY = pl.BlockSpec(memory_space=pl.ANY)
SMEM = pl.BlockSpec(memory_space=pltpu.SMEM)
VMEM = pl.BlockSpec(memory_space=pltpu.VMEM)
MIB = 1024 * 1024

CYCLE = ((0, 0), (1, 0), (2, 0), (3, 0), (3, 1), (2, 1), (1, 1), (0, 1))
CHIP = [z * 2 + y for z, y in CYCLE]
PLACE = [CHIP.index(k) for k in range(8)]


def cycle_perm(shift):
    return [
        (CHIP[r] * 2 + c, CHIP[(r + shift) % 8] * 2 + c) for r in range(8) for c in range(2)
    ]


def across(v):
    return lax.ppermute(v, "stream", [(0, 1), (1, 0)])


def swap(v, bit):
    n = lax.axis_size("batch")
    return lax.ppermute(v, "batch", [(i, i ^ bit) for i in range(n)])


def gather_shifts():
    return [0, -1, 1, -2, 2, -3, 3, -4]


def gather_sources():
    table = np.zeros((16, 16), np.int32)
    for b in range(16):
        place, core = PLACE[b // 2], b % 2
        for slot, shift in enumerate(gather_shifts()):
            chip = CHIP[(place + shift) % 8]
            table[b, slot] = chip * 2 + core
            table[b, 8 + slot] = chip * 2 + 1 - core
    return table


def scatter_targets():
    table = np.zeros((16, 16), np.int32)
    for b in range(16):
        place, core = PLACE[b // 2], b % 2
        for ahead in range(8):
            chip = CHIP[(place + ahead) % 8]
            table[b, ahead] = chip * 2 + core
            table[b, 8 + ahead] = chip * 2 + 1 - core
    return table


def tie(values, after):
    return pl.pallas_call(
        lambda *refs: None,
        out_shape=[jax.ShapeDtypeStruct(value.shape, value.dtype) for value in values],
        in_specs=[ANY] * (len(values) + len(after)),
        out_specs=[ANY] * len(values),
        input_output_aliases={i: i for i in range(len(values))},
        compiler_params=params(1),
        cost_estimate=cost(0),
        name="tie",
    )(*values, *after)


def ring_gather(block, split=0):
    up, down = cycle_perm(1), cycle_perm(-1)
    low = high = block
    own = [block]
    for _ in range(3):
        low = lax.ppermute(low, "batch", up)
        high = lax.ppermute(high, "batch", down)
        own += [low, high]
    if split:
        own.append(lax.ppermute(low[:, :split], "batch", up))
        own.append(lax.ppermute(high[:, split:], "batch", down))
    else:
        own.append(lax.ppermute(low, "batch", up))
    return own


def swapped(blocks):
    return [swap(v, 1) for v in blocks]


class RingSum:
    def __init__(self, parts):
        self.mine, self.other = parts[0], swap(parts[1], 1)
        self.low, self.high = self.term(4).astype(BF16), self.term(5).astype(BF16)
        self.ahead = 4

    def term(self, j):
        return self.mine[j].astype(F32) + self.other[j].astype(F32)

    def step(self, after=()):
        low = lax.ppermute(self.low, "batch", cycle_perm(1))
        high = lax.ppermute(self.high, "batch", cycle_perm(-1))
        if after:
            low, high = tie([low, high], list(after))
        self.ahead -= 1
        self.low = (low.astype(F32) + self.term(self.ahead)).astype(BF16)
        if self.ahead > 1:
            self.high = (high.astype(F32) + self.term(9 - self.ahead)).astype(BF16)
        else:
            self.high = high
        return [self.low]

    def finish(self):
        low = lax.ppermute(self.low, "batch", cycle_perm(1))
        return low.astype(F32) + self.high.astype(F32) + self.term(0)


def scatter_sum(whole):
    return lax.psum_scatter(whole, "batch", scatter_dimension=0, tiled=True).astype(F32)


def dot(left, right):
    return jnp.dot(left, right, preferred_element_type=F32)


def dot_nt(left, right):
    return lax.dot_general(left, right, (((1,), (1,)), ((), ())), preferred_element_type=F32)


def store_blocks(offs, src, parts, sems):
    copies = []
    if len(parts) == 1:
        copies.append(pltpu.make_async_copy(src, parts[0].at[0], sems.at[0]))
    else:
        rows = src.shape[0] // 16
        for k in range(16):
            at = pl.multiple_of(offs[k] * rows, 16)
            place = parts[k // 8].at[k % 8]
            copies.append(pltpu.make_async_copy(src.at[pl.ds(at, rows), :], place, sems.at[k]))
    for copy in copies:
        copy.start()
    return copies


def grad_shapes(n_blocks, rows, cols):
    if n_blocks == 1:
        return [jax.ShapeDtypeStruct((1, rows, cols), BF16)]
    return [jax.ShapeDtypeStruct((8, rows // 16, cols), BF16)] * 2


def params(mib):
    return pltpu.CompilerParams(vmem_limit_bytes=mib * MIB)


def cost(micros):
    return pl.CostEstimate(flops=int(micros * 1e9), bytes_accessed=0, transcendentals=0)


def norm_rows(values):
    centre = values - jnp.mean(values, axis=-1, keepdims=True)
    inverse = lax.rsqrt(jnp.mean(centre * centre, axis=-1, keepdims=True) + EPS)
    return centre * inverse, inverse


def norm_back(upstream, normed, inverse, gain):
    scaled = upstream * gain
    return inverse * (
        scaled
        - jnp.mean(scaled, axis=-1, keepdims=True)
        - normed * jnp.mean(scaled * normed, axis=-1, keepdims=True)
    )


def half_mask(rows, half):
    lane = lax.broadcasted_iota(jnp.int32, (rows, 128), 1)
    return (lane < HEAD_DIM) if half == 0 else (lane >= HEAD_DIM)


def round_kernel(n_after, weight, *refs):
    refs[n_after][...] = weight[...].astype(BF16)


def rounded(weight, after):
    return pl.pallas_call(
        functools.partial(round_kernel, len(after)),
        out_shape=jax.ShapeDtypeStruct(weight.shape, BF16),
        in_specs=[VMEM] + [ANY] * len(after),
        out_specs=VMEM,
        compiler_params=params(60),
        cost_estimate=cost(1),
        name="round_weight",
    )(weight, *after)


def project_kernel(n_blocks, offs, maps, blocks, pre, whole, small, sems, small_sems):
    copies = []
    rows = whole.shape[0] // n_blocks
    for i in range(n_blocks):
        block = blocks.at[i]
        which = offs[i] if n_blocks > 1 else 0
        at = pl.multiple_of(which * rows, 16)
        copies.append(
            pltpu.make_async_copy(block.at[pl.ds(0, rows), :], whole.at[pl.ds(at, rows), :], sems.at[i])
        )
        copies.append(
            pltpu.make_async_copy(block.at[pl.ds(rows, 16), :], small.at[which], small_sems.at[i])
        )
    for copy in copies:
        copy.start()
    for copy in copies:
        copy.wait()
    for i in range(2):
        pick = pl.ds(i * (TLEN // 2), TLEN // 2)
        pre[pick, :] = dot(maps[pick, :], whole[...]).astype(BF16)


def project(offs, maps, blocks):
    n = blocks.shape[0]
    rows = blocks.shape[1] - 16
    channels = n * rows
    return pl.pallas_call(
        functools.partial(project_kernel, n),
        out_shape=[
            jax.ShapeDtypeStruct((TLEN, D), BF16),
            jax.ShapeDtypeStruct((channels, D), BF16),
            jax.ShapeDtypeStruct((n, 16, D), BF16),
        ],
        in_specs=[SMEM, VMEM, ANY],
        out_specs=[VMEM] * 3,
        scratch_shapes=[pltpu.SemaphoreType.DMA((n,)), pltpu.SemaphoreType.DMA((n,))],
        compiler_params=params(60),
        cost_estimate=cost(60),
        name="project_maps",
    )(offs, maps, blocks)


def bias_kernel(n_after, bucket, table, *refs):
    bias = refs[n_after]
    for t in range(TLEN // 128):
        lanes = slice(t * 128, (t + 1) * 128)
        which = bucket[:, lanes]
        for head in range(HEADS):
            row = jnp.broadcast_to(table[head : head + 1, :], which.shape)
            bias[head, :, lanes] = jnp.take_along_axis(row, which, axis=1).astype(BF16)


def spatial_bias(bucket, table, after):
    rows = 64
    return pl.pallas_call(
        functools.partial(bias_kernel, len(after)),
        grid=(TLEN // rows,),
        out_shape=jax.ShapeDtypeStruct((HEADS, TLEN, TLEN), BF16),
        in_specs=[
            pl.BlockSpec((rows, TLEN), lambda i: (i, 0)),
            pl.BlockSpec((16, 128), lambda i: (0, 0)),
        ]
        + [ANY] * len(after),
        out_specs=pl.BlockSpec((HEADS, rows, TLEN), lambda i: (0, i, 0)),
        compiler_params=params(60),
        cost_estimate=cost(5),
        name="spatial_bias",
    )(bucket, table, *after)


def attn_fwd_kernel(n_after, live, attn, bias, text, pre, bn, vec, *refs):
    qkv_out, probs, x_out, query_t, ctx, normed, inverse = refs[n_after : n_after + 7]
    weight, qkv, score_a, score_b, prob_a, prob_b, ctx_a, sems, in_sems, out_sems = refs[n_after + 7 :]
    loads = []
    for part in range(4):
        cols = pl.ds(part * D, D)
        loads.append(pltpu.make_async_copy(attn.at[:, cols], weight.at[:, cols], sems.at[part]))
        loads[-1].start()

    def bring(head):
        place = (prob_a, prob_b)[head % 2].at[head // 2]
        return pltpu.make_async_copy(bias.at[head], place, in_sems.at[head])

    for head in range(HEADS):
        bring(head).start()
    alive = lax.broadcasted_iota(jnp.int32, (TLEN, 1), 0) < live[0]
    visual = (pre[...] - bn[0:1, :]) * bn[1:2, :] * bn[2:3, :] + bn[3:4, :]
    x = jnp.where(live[1] == 1, text[...].astype(F32), jnp.where(alive, visual, 0.0))
    x_low = x.astype(BF16)
    x_out[...] = x_low
    exports = []
    for part in range(3):
        cols = slice(part * D, (part + 1) * D)
        loads[part].wait()
        value = dot(x_low, weight[:, cols])
        if part != 1:
            value = value + vec[part // 2 : part // 2 + 1, :]
        qkv[:, cols] = value.astype(BF16)
        exports.append(
            pltpu.make_async_copy(qkv.at[:, cols], qkv_out.at[:, cols], out_sems.at[HEADS + part])
        )
        exports[-1].start()

    def lanes(start, pair):
        return pl.ds(pl.multiple_of(start + pair * 128, 128), 128)

    def scores(pair, half, out):
        query = qkv[:, lanes(0, pair)] * SCALE
        query = jnp.where(half_mask(TLEN, half), query, jnp.zeros_like(query))
        out[...] = dot_nt(query, qkv[:, lanes(D, pair)])

    def softmax(score, prob, pair):
        key_valid = lax.broadcasted_iota(jnp.int32, (SOFT, TLEN), 1) < live[0]
        for i in range(TLEN // SOFT):
            rows = slice(i * SOFT, (i + 1) * SOFT)
            value = score[rows, :] + prob[pair, rows, :].astype(F32)
            value = jnp.where(key_valid, value, -1000000000.0)
            peak = jnp.max(value, axis=-1, keepdims=True)
            raised = jnp.exp(value - peak)
            total = jnp.sum(raised, axis=-1, keepdims=True)
            prob[pair, rows, :] = (raised * (1.0 / total)).astype(BF16)

    scores(0, 0, score_a)
    for head in range(HEADS):
        bring(head).wait()

    def step(pair, carry):
        values = qkv[:, lanes(2 * D, pair)]
        scores(pair, 1, score_b)
        softmax(score_a, prob_a, pair)
        scores(jnp.minimum(pair + 1, PAIRS - 1), 0, score_a)
        ctx_a[...] = dot(prob_a[pair], values)
        softmax(score_b, prob_b, pair)
        ctx_b = dot(prob_b[pair], values)
        ctx[:, lanes(0, pair)] = jnp.where(half_mask(TLEN, 0), ctx_a[...], ctx_b).astype(BF16)
        for half, prob in enumerate((prob_a, prob_b)):
            head = 2 * pair + half
            pltpu.make_async_copy(prob.at[pair], probs.at[head], out_sems.at[head]).start()
        return carry

    lax.fori_loop(0, PAIRS, step, 0)
    loads[3].wait()
    att = dot(ctx[...], weight[:, 3 * D :]) + vec[2:3, :]
    query_t[...] = (qkv[:, :D] * SCALE).T
    normal, inv = norm_rows(x + att)
    normed[...] = normal
    inverse[...] = jnp.broadcast_to(inv, (TLEN, 128))
    for copy in exports:
        copy.wait()
    for head in range(HEADS):
        prob = (prob_a, prob_b)[head % 2]
        pltpu.make_async_copy(prob.at[head // 2], probs.at[head], out_sems.at[head]).wait()


def attn_fwd(live, attn, bias, text, pre, bn, vec, after):
    return pl.pallas_call(
        functools.partial(attn_fwd_kernel, len(after)),
        out_shape=[
            jax.ShapeDtypeStruct((TLEN, 3 * D), BF16),
            jax.ShapeDtypeStruct((HEADS, TLEN, TLEN), BF16),
            jax.ShapeDtypeStruct((TLEN, D), BF16),
            jax.ShapeDtypeStruct((D, TLEN), BF16),
            jax.ShapeDtypeStruct((TLEN, D), BF16),
            jax.ShapeDtypeStruct((TLEN, D), F32),
            jax.ShapeDtypeStruct((TLEN, 128), F32),
        ],
        in_specs=[SMEM, ANY, ANY] + [VMEM] * 4 + [ANY] * len(after),
        out_specs=[ANY, ANY] + [VMEM] * 5,
        scratch_shapes=[
            pltpu.VMEM((D, 4 * D), BF16),
            pltpu.VMEM((TLEN, 3 * D), BF16),
            pltpu.VMEM((TLEN, TLEN), F32),
            pltpu.VMEM((TLEN, TLEN), F32),
            pltpu.VMEM((PAIRS, TLEN, TLEN), BF16),
            pltpu.VMEM((PAIRS, TLEN, TLEN), BF16),
            pltpu.VMEM((TLEN, 128), F32),
            pltpu.SemaphoreType.DMA((4,)),
            pltpu.SemaphoreType.DMA((HEADS,)),
            pltpu.SemaphoreType.DMA((HEADS + 3,)),
        ],
        compiler_params=params(60),
        cost_estimate=cost(15),
        name="attention_forward",
    )(live, attn, bias, text, pre, bn, vec, *after)


def load_ffn(offs, blocks, up, down, sems):
    first, second = [], []
    if len(blocks) == 1:
        first.append(pltpu.make_async_copy(blocks[0].at[:, pl.ds(0, FF)], up, sems.at[0]))
        second.append(pltpu.make_async_copy(blocks[0].at[:, pl.ds(FF, FF)], down, sems.at[1]))
        return first, second
    at = 0
    for slot in range(16):
        rows = pl.ds(pl.multiple_of(offs[slot] * 48, 16), 48)
        if slot % 8 < 7:
            left, right = blocks[at].at[:, pl.ds(0, FF)], blocks[at].at[:, pl.ds(FF, FF)]
            at += 1
        else:
            left, right = blocks[at], blocks[at + 1]
            at += 2
        first.append(pltpu.make_async_copy(left, up.at[rows, :], sems.at[2 * slot]))
        second.append(pltpu.make_async_copy(right, down.at[rows, :], sems.at[2 * slot + 1]))
    return first, second


def ffn_kernel(n_blocks, live, offs, attn, normed, inverse, vec, joined_grad, *refs):
    blocks, refs = refs[:n_blocks], refs[n_blocks:]
    part, refs = refs[0], refs[1:]
    result, grad_residual, grad_attended, grad_ctx, grad_ctx_t, grads = refs[:6]
    up, down, active, slope, grad, total, weight, sems, last_sems, out_sems = refs[6:]
    loads = load_ffn(offs, blocks, up, down, sems)
    for copy in loads[0] + loads[1]:
        copy.start()
    last = pltpu.make_async_copy(attn.at[:, pl.ds(3 * D, D)], weight, last_sems.at[0])
    last.start()
    first = normed[...] * vec[3:4, :] + vec[4:5, :]
    first_low = first.astype(BF16)
    for copy in loads[0]:
        copy.wait()
    units = dot(first_low, up[:, :D])
    total[...] = first + vec[9:10, :]
    for k in range(CHUNKS):
        units = units + vec[5 + k : 6 + k, :]
        if k + 1 < CHUNKS:
            following = dot(first_low, up[:, (k + 1) * D : (k + 2) * D])
        square = units * units
        root = math.sqrt(2.0 / math.pi)
        bend = jnp.tanh(root * units * (1.0 + 0.044715 * square))
        half = 0.5 * (1.0 + bend)
        active[k] = (units * half).astype(BF16)
        slope[k] = (
            half + 0.5 * root * units * (1.0 - bend * bend) * (1.0 + 3.0 * 0.044715 * square)
        ).astype(BF16)
        if k == 0:
            for copy in loads[1]:
                copy.wait()
        total[...] += dot_nt(active[k], down[:, k * D : (k + 1) * D])
        if k + 1 < CHUNKS:
            units = following
    normal, inv = norm_rows(total[...])
    mask = lax.broadcasted_iota(jnp.int32, (TLEN, 1), 0) < live[0]
    result[...] = jnp.where(mask, normal * vec[10:11, :] + vec[11:12, :], 0.0).astype(BF16)
    upstream = jnp.where(mask, joined_grad[...].astype(F32), 0.0)
    second = norm_back(upstream, normal, inv, vec[10:11, :])
    second_low = second.astype(BF16)
    total[...] = second
    grads[9:10, :] = jnp.sum(second_low.astype(F32), axis=0, keepdims=True)
    grads[10:11, :] = jnp.sum(upstream * normal, axis=0, keepdims=True)
    grads[11:12, :] = jnp.sum(upstream, axis=0, keepdims=True)
    turned = second_low.T
    for k in range(CHUNKS):
        cols = slice(FF + k * D, FF + (k + 1) * D)
        grad[:, cols] = dot(turned, active[k]).astype(BF16)
    cols = pl.ds(FF, FF)
    copies = [pltpu.make_async_copy(grad.at[:, cols], part.at[:, cols], out_sems.at[0])]
    copies[0].start()
    turned = first_low.T
    for k in range(CHUNKS):
        cols = slice(k * D, (k + 1) * D)
        inner = (dot(second_low, down[:, cols]) * slope[k].astype(F32)).astype(BF16)
        grads[5 + k : 6 + k, :] = jnp.sum(inner.astype(F32), axis=0, keepdims=True)
        total[...] += dot_nt(inner, up[:, cols])
        grad[:, cols] = dot(turned, inner).astype(BF16)
    cols = pl.ds(0, FF)
    copies.append(pltpu.make_async_copy(grad.at[:, cols], part.at[:, cols], out_sems.at[1]))
    copies[-1].start()
    upstream = total[...]
    grads[3:4, :] = jnp.sum(upstream * normed[...], axis=0, keepdims=True)
    grads[4:5, :] = jnp.sum(upstream, axis=0, keepdims=True)
    residual = norm_back(upstream, normed[...], inverse[:, 0:1], vec[3:4, :])
    grad_residual[...] = residual
    attended = residual.astype(BF16)
    grad_attended[...] = attended
    grads[2:3, :] = jnp.sum(attended.astype(F32), axis=0, keepdims=True)
    grads[0:2, :] = jnp.zeros((2, D), F32)
    grads[12:16, :] = jnp.zeros((4, D), F32)
    last.wait()
    back = dot_nt(attended, weight[...]).astype(BF16)
    grad_ctx[...] = back
    grad_ctx_t[...] = back.T
    for copy in copies:
        copy.wait()


def feed_forward(live, offs, blocks, attn, normed, inverse, vec, joined_grad):
    n = len(blocks)
    out = pl.pallas_call(
        functools.partial(ffn_kernel, n),
        out_shape=[
            jax.ShapeDtypeStruct((D, 2 * FF), BF16),
            jax.ShapeDtypeStruct((TLEN, D), BF16),
            jax.ShapeDtypeStruct((TLEN, D), F32),
            jax.ShapeDtypeStruct((TLEN, D), BF16),
            jax.ShapeDtypeStruct((TLEN, D), BF16),
            jax.ShapeDtypeStruct((D, TLEN), BF16),
            jax.ShapeDtypeStruct((16, D), F32),
        ],
        in_specs=[SMEM, SMEM, ANY] + [VMEM] * 4 + [ANY] * n,
        out_specs=[ANY] + [VMEM] * 6,
        scratch_shapes=[
            pltpu.VMEM((D, FF), BF16),
            pltpu.VMEM((D, FF), BF16),
            pltpu.VMEM((CHUNKS, TLEN, D), BF16),
            pltpu.VMEM((CHUNKS, TLEN, D), BF16),
            pltpu.VMEM((D, 2 * FF), BF16),
            pltpu.VMEM((TLEN, D), F32),
            pltpu.VMEM((D, D), BF16),
            pltpu.SemaphoreType.DMA((32,)),
            pltpu.SemaphoreType.DMA((1,)),
            pltpu.SemaphoreType.DMA((2,)),
        ],
        compiler_params=params(60),
        cost_estimate=cost(30),
        name="feed_forward",
    )(live, offs, attn, normed, inverse, vec, joined_grad, *blocks)
    return out


def pairs_kernel(n_after, keys, values, back, context, back_t, query_t, probs, *refs):
    grad_query, grad_key_t, grad_value_t, grad_scores = refs[n_after:]
    total = jnp.zeros((TLEN, 128), F32)
    for half in range(2):
        mask = half_mask(TLEN, half)
        masked = jnp.where(mask, back[...], jnp.zeros_like(back[...]))
        prob = probs[half]
        slopes = dot_nt(masked, values[...])
        delta = jnp.sum(masked.astype(F32) * context[...].astype(F32), axis=-1, keepdims=True)
        slopes = (prob.astype(F32) * (slopes - delta)).astype(BF16)
        grad_scores[half] = slopes
        near = jnp.where(mask, keys[...], jnp.zeros_like(keys[...]))
        total = total + dot(slopes, near)
        lines = slice(half * HEAD_DIM, (half + 1) * HEAD_DIM)
        grad_key_t[lines, :] = dot(query_t[lines, :], slopes).astype(BF16)
        grad_value_t[lines, :] = dot(back_t[lines, :], prob).astype(BF16)
    grad_query[...] = (total * SCALE).astype(BF16)


def attn_bwd_pairs(first, count, qkv, grad_ctx, ctx, grad_ctx_t, query_t, probs, after):
    def cols(base):
        return pl.BlockSpec((TLEN, 128), lambda i: (0, base + i))

    def lines(base):
        return pl.BlockSpec((128, TLEN), lambda i: (base + i, 0))

    def heads(base):
        return pl.BlockSpec((2, TLEN, TLEN), lambda i: (base + i, 0, 0))

    return pl.pallas_call(
        functools.partial(pairs_kernel, len(after)),
        grid=(count,),
        out_shape=[
            jax.ShapeDtypeStruct((TLEN, 128 * count), BF16),
            jax.ShapeDtypeStruct((128 * count, TLEN), BF16),
            jax.ShapeDtypeStruct((128 * count, TLEN), BF16),
            jax.ShapeDtypeStruct((2 * count, TLEN, TLEN), BF16),
        ],
        in_specs=[
            cols(PAIRS + first),
            cols(2 * PAIRS + first),
            cols(first),
            cols(first),
            lines(first),
            lines(first),
            heads(first),
        ]
        + [ANY] * len(after),
        out_specs=[cols(0), lines(0), lines(0), heads(0)],
        compiler_params=params(60),
        cost_estimate=cost(5),
        name="attention_backward",
    )(qkv, qkv, grad_ctx, ctx, grad_ctx_t, query_t, probs, *after)


def input_kernel(n_parts, n_after, live, attn, grads, grad_residual, pre, bn, *refs):
    queries, refs = refs[:n_parts], refs[n_parts:]
    keys_t, refs = refs[:n_parts], refs[n_parts:]
    values_t, refs = refs[:n_parts], refs[n_parts + n_after :]
    grad_qkv, grad_input, grad_bn, sums, weight, sems = refs
    load = pltpu.make_async_copy(attn.at[:, pl.ds(0, 3 * D)], weight, sems.at[0])
    load.start()
    at = 0
    for query, key, value in zip(queries, keys_t, values_t):
        width = query.shape[1]
        grad_qkv[:, at : at + width] = query[...]
        grad_qkv[:, D + at : D + at + width] = key[...].T
        grad_qkv[:, 2 * D + at : 2 * D + at + width] = value[...].T
        at += width
    load.wait()
    total = grad_residual[...] + dot_nt(grad_qkv[...], weight[...])
    grad_input[...] = total
    alive = lax.broadcasted_iota(jnp.int32, (TLEN, 1), 0) < live[0]
    back = jnp.where(jnp.logical_and(alive, live[1] == 0), total, 0.0)
    grad_bn[...] = back.astype(BF16)
    normal = (pre[...] - bn[0:1, :]) * bn[1:2, :]
    sums[...] = grads[...]
    sums[0:1, :] = jnp.sum(grad_qkv[:, :D].astype(F32), axis=0, keepdims=True)
    sums[1:2, :] = jnp.sum(grad_qkv[:, 2 * D :].astype(F32), axis=0, keepdims=True)
    sums[12:13, :] = jnp.sum(back * normal, axis=0, keepdims=True)
    sums[13:14, :] = jnp.sum(back, axis=0, keepdims=True)


def attn_bwd_input(live, attn, grads, grad_residual, pre, bn, queries, keys_t, values_t, after):
    parts = len(queries)
    return pl.pallas_call(
        functools.partial(input_kernel, parts, len(after)),
        out_shape=[
            jax.ShapeDtypeStruct((TLEN, 3 * D), BF16),
            jax.ShapeDtypeStruct((TLEN, D), F32),
            jax.ShapeDtypeStruct((TLEN, D), BF16),
            jax.ShapeDtypeStruct((16, D), F32),
        ],
        in_specs=[SMEM, ANY] + [VMEM] * (3 * parts + 4) + [ANY] * len(after),
        out_specs=[VMEM] * 4,
        scratch_shapes=[pltpu.VMEM((D, 3 * D), BF16), pltpu.SemaphoreType.DMA((1,))],
        compiler_params=params(60),
        cost_estimate=cost(5),
        name="input_gradient",
    )(live, attn, grads, grad_residual, pre, bn, *queries, *keys_t, *values_t, *after)


def table_kernel(n_parts, n_after, bucket, sums, *refs):
    parts, (out, one_hot, total) = refs[:n_parts], refs[n_parts + n_after :]
    step = pl.program_id(0)

    @pl.when(step == 0)
    def _():
        total[...] = jnp.zeros_like(total)

    for group in range(ROWS // 16):
        lines = slice(group * 16, (group + 1) * 16)
        which = bucket[lines, :]
        for b in range(BUCKETS):
            one_hot[b * 16 : (b + 1) * 16, :] = jnp.where(which == b, 1.0, 0.0).astype(BF16)
        slopes = jnp.concatenate(
            [part[:, lines, :].reshape(part.shape[0] * 16, TLEN) for part in parts], axis=0
        )
        total[...] += dot_nt(one_hot[...], slopes)

    @pl.when(step == STEPS - 1)
    def _():
        line = lax.broadcasted_iota(jnp.int32, (BUCKETS * 16, HEADS * 16), 0) % 16
        lane = lax.broadcasted_iota(jnp.int32, (BUCKETS * 16, HEADS * 16), 1) % 16
        kept = jnp.where(line == lane, total[...], 0.0)
        kept = jnp.sum(kept.reshape(BUCKETS, 16, HEADS * 16), axis=1)
        shape = (HEADS * 16, BUCKETS * HEADS)
        head = lax.broadcasted_iota(jnp.int32, shape, 0) // 16
        pick = lax.broadcasted_iota(jnp.int32, shape, 1) % HEADS
        spread = jnp.dot(
            kept,
            jnp.where(head == pick, 1.0, 0.0),
            precision=lax.Precision.HIGHEST,
            preferred_element_type=F32,
        )
        shape = (BUCKETS, BUCKETS * HEADS)
        own = lax.broadcasted_iota(jnp.int32, shape, 1) // HEADS
        spread = jnp.where(own == lax.broadcasted_iota(jnp.int32, shape, 0), spread, 0.0)
        out[...] = sums[...]
        out[14:15, : BUCKETS * HEADS] = jnp.sum(spread, axis=0, keepdims=True)


def table_grad(bucket, sums, parts, after):
    return pl.pallas_call(
        functools.partial(table_kernel, len(parts), len(after)),
        grid=(STEPS,),
        out_shape=jax.ShapeDtypeStruct((16, D), F32),
        in_specs=[
            pl.BlockSpec((ROWS, TLEN), lambda i: (i, 0)),
            pl.BlockSpec((16, D), lambda i: (0, 0)),
        ]
        + [pl.BlockSpec((part.shape[0], ROWS, TLEN), lambda i: (0, i, 0)) for part in parts]
        + [ANY] * len(after),
        out_specs=pl.BlockSpec((16, D), lambda i: (0, 0)),
        scratch_shapes=[
            pltpu.VMEM((BUCKETS * 16, TLEN), BF16),
            pltpu.VMEM((BUCKETS * 16, HEADS * 16), F32),
        ],
        compiler_params=params(60),
        cost_estimate=cost(5),
        name="table_gradient",
    )(bucket, sums, *parts, *after)


def outer_kernel(n_parts, n_after, widths, offs, *refs):
    count = len(widths)
    lefts, rights, refs = refs[:count], refs[count : 2 * count], refs[2 * count + n_after :]
    parts, (grad, sems) = refs[:n_parts], refs[n_parts:]
    at = 0
    for left, right, width in zip(lefts, rights, widths):
        turned = left[...].astype(BF16).T
        for lo in range(0, width, D):
            grad[:, at + lo : at + lo + D] = dot(turned, right[:, lo : lo + D]).astype(BF16)
        at += width
    for copy in store_blocks(offs, grad, parts, sems):
        copy.wait()


def outer(offs, n_blocks, lefts, rights, after):
    widths = tuple(right.shape[1] for right in rights)
    rows = lefts[0].shape[1]
    parts = grad_shapes(n_blocks, rows, sum(widths))
    return pl.pallas_call(
        functools.partial(outer_kernel, len(parts), len(after), widths),
        out_shape=parts,
        in_specs=[SMEM] + [VMEM] * (2 * len(widths)) + [ANY] * len(after),
        out_specs=[ANY] * len(parts),
        scratch_shapes=[
            pltpu.VMEM((rows, sum(widths)), BF16),
            pltpu.SemaphoreType.DMA((16,)),
        ],
        compiler_params=params(60),
        cost_estimate=cost(5),
        name="weight_gradient",
    )(offs, *lefts, *rights, *after)


def project_grad_kernel(n_parts, n_after, live, places, maps, own, other, pre, bn, totals, *refs):
    parts, refs = refs[n_after : n_after + n_parts], refs[n_after + n_parts :]
    grad_pre, grad, sems = refs
    alive = lax.broadcasted_iota(jnp.int32, (TLEN, 1), 0) < live[0]
    normal = (pre[...] - bn[0:1, :]) * bn[1:2, :]
    count = bn[4:5, :]
    back = own[...].astype(F32) + other[...].astype(F32)
    back = back - totals[1:2, :] / count - normal * (totals[0:1, :] / count)
    low = jnp.where(alive, back * (bn[1:2, :] * bn[2:3, :]), 0.0).astype(BF16)
    grad_pre[...] = low
    grad[...] = dot(maps[...].T, low).astype(BF16)
    for copy in store_blocks(places, grad, parts, sems):
        copy.wait()


def project_gradient(live, places, n_blocks, maps, own, other, pre, bn, totals, after):
    rows = maps.shape[1]
    parts = grad_shapes(n_blocks, rows, D)
    out = pl.pallas_call(
        functools.partial(project_grad_kernel, len(parts), len(after)),
        out_shape=parts + [jax.ShapeDtypeStruct((TLEN, D), BF16)],
        in_specs=[SMEM, SMEM] + [VMEM] * 6 + [ANY] * len(after),
        out_specs=[ANY] * len(parts) + [VMEM],
        scratch_shapes=[
            pltpu.VMEM((rows, D), BF16),
            pltpu.SemaphoreType.DMA((16,)),
        ],
        compiler_params=params(60),
        cost_estimate=cost(5),
        name="project_gradient",
    )(live, places, maps, own, other, pre, bn, totals, *after)
    return out[:-1], out[-1]


def maps_kernel(grad_pre, weight, result, other, grad_maps, joined):
    joined[...] = result[...] + other[...]
    grad_maps[...] = dot_nt(grad_pre[...], weight[...])


def maps_gradient(grad_pre, weight, result, other):
    return pl.pallas_call(
        maps_kernel,
        out_shape=[
            jax.ShapeDtypeStruct((TLEN, weight.shape[0]), F32),
            jax.ShapeDtypeStruct((TLEN, D), BF16),
        ],
        in_specs=[VMEM] * 4,
        out_specs=[VMEM] * 2,
        compiler_params=params(60),
        cost_estimate=cost(1),
        name="maps_gradient",
    )(grad_pre, weight, result, other)


def nesterov(weight, moment, average, gradient, rate):
    moment_new = MOMENTUM * moment + gradient
    weight_new = weight - rate * (gradient + MOMENTUM * moment_new)
    return (weight_new, moment_new, AVERAGE * average + (1.0 - AVERAGE) * weight_new)


def stats_kernel(n_after, live, own, other, *refs):
    pre, stats = refs[n_after:]
    total = (own[...].astype(F32) + other[...].astype(F32)).astype(BF16).astype(F32)
    pre[...] = total
    count = live[0].astype(F32)
    mask = lax.broadcasted_iota(jnp.int32, (TLEN, 1), 0) < live[0]
    mean = jnp.sum(jnp.where(mask, total, 0.0), axis=0, keepdims=True) / count
    centre = jnp.where(mask, total - mean, 0.0)
    stats[...] = jnp.concatenate(
        [
            mean,
            jnp.sum(centre * centre, axis=0, keepdims=True),
            jnp.full((6, D), count, F32),
        ],
        axis=0,
    )


def local_stats(live, own, other, after):
    return pl.pallas_call(
        functools.partial(stats_kernel, len(after)),
        out_shape=[
            jax.ShapeDtypeStruct((TLEN, D), F32),
            jax.ShapeDtypeStruct((8, D), F32),
        ],
        in_specs=[SMEM, VMEM, VMEM] + [ANY] * len(after),
        out_specs=[VMEM, VMEM],
        compiler_params=params(60),
        cost_estimate=cost(40),
        name="local_statistics",
    )(live, own, other, *after)


def exchange_steps():
    bit, n = 1, lax.axis_size("batch")
    while bit < n:
        partners = [bit] if 2 * bit == n else [bit, 2 * bit, 3 * bit]
        bit *= 2 * len(partners) if len(partners) == 1 else 4
        yield partners, bit >= n


def merge_kernel(count, last, *refs):
    parts, out = refs[:count], refs[-1]
    total = parts[0][2:3, :]
    mean = parts[0][0:1, :] * total
    for part in parts[1:]:
        total = total + part[2:3, :]
        mean = mean + part[0:1, :] * part[2:3, :]
    mean = mean / total
    spread = jnp.zeros_like(mean)
    for part in parts:
        gap = part[0:1, :] - mean
        spread = spread + part[1:2, :] + gap * gap * part[2:3, :]
    out[0:1, :] = mean
    out[1:2, :] = spread
    out[2:8, :] = jnp.broadcast_to(total, (6, D))
    if last:
        out[1:2, :] = lax.rsqrt(spread / total + EPS)
        out[2:4, :] = refs[count][0:2, :]


def merge_stats(stats, gains, after):
    for partners, last in exchange_steps():
        parts = [stats] + [swap(stats, bit) for bit in partners]
        operands = parts + ([gains] if last else [])
        stats = pl.pallas_call(
            functools.partial(merge_kernel, len(parts), last),
            out_shape=jax.ShapeDtypeStruct((8, D), F32),
            in_specs=[VMEM] * len(operands) + [ANY] * len(after),
            out_specs=VMEM,
            cost_estimate=cost(15),
            name="merge_statistics",
        )(*operands, *after)
        after = []
    return stats


def add_kernel(count, *refs):
    total = refs[0][...]
    for part in refs[1:count]:
        total = total + part[...]
    refs[-1][...] = total


def sum_small(values, after, begin=0, end=None):
    for step, (partners, _) in enumerate(list(exchange_steps())[begin:end]):
        parts = [values] + [swap(values, bit) for bit in partners]
        ties = after[step] if step < len(after) else []
        values = pl.pallas_call(
            functools.partial(add_kernel, len(parts)),
            out_shape=jax.ShapeDtypeStruct(values.shape, F32),
            in_specs=[VMEM] * len(parts) + [ANY] * len(ties),
            out_specs=VMEM,
            cost_estimate=cost(0.5),
            name="sum_small",
        )(*parts, *ties)
    return values


def on_device(
    text_embed,
    visual_maps,
    visual_bucket,
    rel_bucket,
    joined_grad,
    attn_weight,
    attn_moment,
    attn_average,
    ffn_weight,
    ffn_moment,
    ffn_average,
    vector_weight,
    vector_moment,
    vector_average,
    project_weight,
    project_moment,
    project_average,
    shared_weight,
    shared_moment,
    shared_average,
):
    n_batch = lax.axis_size("batch")
    me = lax.axis_index("batch")
    ringed = n_batch == 16
    is_text = lax.axis_index("stream") == 0
    maps = visual_maps.reshape(TLEN, -1)

    small = jnp.zeros((16, D), BF16)
    small = small.at[0, : vector_weight.shape[1]].set(vector_weight[0].astype(BF16))
    small = small.at[1, : shared_weight.shape[0]].set(shared_weight.astype(BF16))
    attn_low = rounded(attn_weight[0], [])
    attn_full = lax.all_gather(attn_low, "batch", axis=0, tiled=True)
    packed = jnp.concatenate([project_weight.astype(BF16), small], axis=0)
    if ringed:
        sources = jnp.asarray(gather_sources())[me]
        targets = jnp.asarray(scatter_targets())[me]
        project_blocks = ring_gather(packed)
        project_blocks += swapped(project_blocks)
        ffn_low = rounded(ffn_weight[0], project_blocks[5:7])
        ffn_blocks = ring_gather(ffn_low, FF)
        ffn_other = swapped(ffn_blocks[:7])
        n_blocks = 16
    else:
        sources = jnp.zeros((1,), jnp.int32)
        targets = jnp.zeros((1,), jnp.int32)
        rows = lax.all_gather(project_weight.astype(BF16), "batch", axis=0, tiled=True)
        project_blocks = [jnp.concatenate([rows, jnp.zeros((16, D), BF16)], axis=0)]
        ffn_low = rounded(ffn_weight[0], [])
        ffn_blocks = [lax.all_gather(ffn_low, "batch", axis=0, tiled=True)]
        n_blocks = 1

    partial_pre, project_half, small_all = project(sources, maps, jnp.stack(project_blocks))
    if not ringed:
        small_all = lax.all_gather(small, "batch", axis=0, tiled=False)
    other_pre = across(partial_pre)
    vector_rows = small_all[:, 0, : vector_weight.shape[1]].reshape(12, D).astype(F32)
    vec = jnp.concatenate([vector_rows, jnp.zeros((4, D), F32)], axis=0)
    shared_full = small_all[:, 1, : shared_weight.shape[0]].reshape(-1).astype(F32)
    table = jnp.zeros((16, 128), F32)
    table = table.at[:HEADS, :BUCKETS].set(
        shared_full[: BUCKETS * HEADS].reshape(BUCKETS, HEADS).T
    )
    gains = shared_full[BUCKETS * HEADS :].reshape(2, D)

    bucket = rel_bucket.reshape(TLEN, TLEN)
    bias = spatial_bias(bucket, table, [])
    visual_len = ((visual_bucket + 1) * (TLEN // 2)).astype(jnp.int32)
    pre, stats = local_stats(
        visual_len, partial_pre, other_pre, [bias] + (ffn_blocks[1:3] if ringed else [])
    )
    bn = merge_stats(stats, gains, ffn_blocks[3:5] if ringed else [])
    text = is_text.astype(jnp.int32)
    live = jnp.stack([jnp.where(is_text, TLEN, visual_len[0]), text])
    visual_live = jnp.stack([visual_len[0], text])

    qkv, probs, x_low, query_t, ctx, normed, inverse = attn_fwd(
        live,
        attn_full,
        bias,
        text_embed.reshape(TLEN, D),
        pre,
        bn,
        vec,
        ffn_blocks[5:7] + ffn_other if ringed else [],
    )
    if ringed:
        ffn_last = list(tie(ffn_blocks[7:], [normed]))
        ffn_blocks = ffn_blocks[:7] + ffn_last + ffn_other + swapped(ffn_last)
    ffn_part, result, grad_residual, grad_attended, grad_ctx, grad_ctx_t, grads = feed_forward(
        live,
        sources,
        ffn_blocks,
        attn_full,
        normed,
        inverse,
        vec,
        joined_grad.reshape(TLEN, D),
    )
    ffn_sum = scatter_sum(ffn_part)
    queries, keys_t, values_t, score_grads = (
        [piece]
        for piece in attn_bwd_pairs(0, PAIRS, qkv, grad_ctx, ctx, grad_ctx_t, query_t, probs, [])
    )
    grad_qkv, grad_input, grad_bn, sums = attn_bwd_input(
        visual_live,
        attn_full,
        grads,
        grad_residual,
        pre,
        bn,
        queries,
        keys_t,
        values_t,
        [],
    )

    grad_bn_other = across(grad_bn)
    sums = table_grad(bucket, sums, score_grads, [])
    attn_parts = outer(
        targets,
        n_blocks,
        [x_low, ctx],
        [grad_qkv, grad_attended],
        [],
    )
    if ringed:
        attn_ring = RingSum(attn_parts)
        sent = [attn_ring.low, attn_ring.high]
    else:
        sent = []
    sums = sum_small(sums, [[attn_parts[0]], sent])
    shared_sums = sums[8:]
    shared_sums = (shared_sums + across(shared_sums))[4:7]
    project_parts, grad_pre = project_gradient(
        visual_live,
        targets,
        n_blocks,
        maps,
        grad_bn,
        grad_bn_other,
        pre,
        bn,
        shared_sums[:2],
        [],
    )
    (result,) = tie([result], [grad_pre])
    result_other = across(result)
    if ringed:
        project_ring = RingSum(project_parts)
        sent = [project_ring.low, project_ring.high]
        attn_ring.step()
        attn_ring.step(sent)
        project_ring.step()
        later = project_ring.step()
        attn_ring.step(later + [result_other])
        project_ring.step()
        attn_sum, project_grad = attn_ring.finish(), project_ring.finish()
    else:
        attn_sum, project_grad = scatter_sum(attn_parts[0][0]), scatter_sum(project_parts[0][0])
        sent = []
    ffn_grad, attn_grad = ffn_sum[None], attn_sum[None]
    grad_maps, joined = maps_gradient(grad_pre, project_half, result, result_other)
    width = shared_weight.shape[0]
    own_shared = lax.dynamic_slice(
        jnp.concatenate([shared_sums[2, : BUCKETS * HEADS], shared_sums[0], shared_sums[1]]),
        (me * width,),
        (width,),
    )

    all_tokens = n_batch * TLEN
    rate_attention = 1.5 / math.sqrt(D * all_tokens)
    rate_matrix = 0.6 / math.sqrt(D * all_tokens)
    rate_vector = 0.12 / math.sqrt(all_tokens)
    width = vector_weight.shape[1]
    vector_grad = lax.dynamic_slice(sums[:12].reshape(-1), (me * width,), (width,))[None]
    vector_new = nesterov(vector_weight, vector_moment, vector_average, vector_grad, rate_vector)
    ffn_new = nesterov(ffn_weight, ffn_moment, ffn_average, ffn_grad, rate_matrix)
    attn_new = nesterov(attn_weight, attn_moment, attn_average, attn_grad, rate_attention)
    project_new = nesterov(
        project_weight, project_moment, project_average, project_grad, rate_matrix
    )
    shared_new = nesterov(shared_weight, shared_moment, shared_average, own_shared, rate_vector)
    return (
        joined.reshape(1, TLEN, D),
        grad_input.reshape(1, 1, TLEN, D),
        grad_maps.reshape(1, TLEN, -1),
        attn_new[0],
        attn_new[1],
        attn_new[2],
        ffn_new[0],
        ffn_new[1],
        ffn_new[2],
        vector_new[0],
        vector_new[1],
        vector_new[2],
        project_new[0],
        project_new[1],
        project_new[2],
        shared_new[0],
        shared_new[1],
        shared_new[2],
    )


def solution(mesh):
    return jax.shard_map(
        on_device,
        mesh=mesh,
        in_specs=(
            P("batch", None, None),
            P("batch", None, "stream"),
            P("batch"),
            P("stream", "batch", None, None),
            P("batch", None, None),
            P("stream", "batch", None),
            P("stream", "batch", None),
            P("stream", "batch", None),
            P("stream", "batch", None),
            P("stream", "batch", None),
            P("stream", "batch", None),
            P("stream", "batch"),
            P("stream", "batch"),
            P("stream", "batch"),
            P(("stream", "batch"), None),
            P(("stream", "batch"), None),
            P(("stream", "batch"), None),
            P("batch"),
            P("batch"),
            P("batch"),
        ),
        out_specs=(
            P("batch", None, None),
            P("stream", "batch", None, None),
            P("batch", None, "stream"),
            P("stream", "batch", None),
            P("stream", "batch", None),
            P("stream", "batch", None),
            P("stream", "batch", None),
            P("stream", "batch", None),
            P("stream", "batch", None),
            P("stream", "batch"),
            P("stream", "batch"),
            P("stream", "batch"),
            P(("stream", "batch"), None),
            P(("stream", "batch"), None),
            P(("stream", "batch"), None),
            P("batch"),
            P("batch"),
            P("batch"),
        ),
        check_vma=False,
    )
```

```python
import functools
import math

import jax
import jax.numpy as jnp
import numpy as np
from jax import lax
from jax.experimental import pallas as pl
from jax.experimental.pallas import tpu as pltpu
from jax.sharding import PartitionSpec as P

D = 768
HEADS = 12
HEAD_DIM = 64
FF = 3072
TLEN = 512
BUCKETS = 32
PAIRS = HEADS // 2
ROWS = 128
SOFT = 128
STEPS = TLEN // ROWS
CHUNKS = FF // D

EPS = 1e-05
MOMENTUM = 0.9
AVERAGE = 0.95
SCALE = HEAD_DIM ** (-0.5)

BF16 = jnp.bfloat16
F32 = jnp.float32
ANY = pl.BlockSpec(memory_space=pl.ANY)
SMEM = pl.BlockSpec(memory_space=pltpu.SMEM)
VMEM = pl.BlockSpec(memory_space=pltpu.VMEM)
MIB = 1024 * 1024

CYCLE = ((0, 0), (1, 0), (2, 0), (3, 0), (3, 1), (2, 1), (1, 1), (0, 1))
CHIP = [z * 2 + y for z, y in CYCLE]
PLACE = [CHIP.index(k) for k in range(8)]


def cycle_perm(shift):
    return [
        (CHIP[r] * 2 + c, CHIP[(r + shift) % 8] * 2 + c) for r in range(8) for c in range(2)
    ]


def across(v):
    return lax.ppermute(v, "stream", [(0, 1), (1, 0)])


def swap(v, bit):
    n = lax.axis_size("batch")
    return lax.ppermute(v, "batch", [(i, i ^ bit) for i in range(n)])


def gather_shifts():
    return [0, -1, 1, -2, 2, -3, 3, -4]


def gather_sources():
    table = np.zeros((16, 16), np.int32)
    for b in range(16):
        place, core = PLACE[b // 2], b % 2
        for slot, shift in enumerate(gather_shifts()):
            chip = CHIP[(place + shift) % 8]
            table[b, slot] = chip * 2 + core
            table[b, 8 + slot] = chip * 2 + 1 - core
    return table


def scatter_targets():
    table = np.zeros((16, 16), np.int32)
    for b in range(16):
        place, core = PLACE[b // 2], b % 2
        for ahead in range(8):
            chip = CHIP[(place + ahead) % 8]
            table[b, ahead] = chip * 2 + core
            table[b, 8 + ahead] = chip * 2 + 1 - core
    return table


def tie(values, after):
    return pl.pallas_call(
        lambda *refs: None,
        out_shape=[jax.ShapeDtypeStruct(value.shape, value.dtype) for value in values],
        in_specs=[ANY] * (len(values) + len(after)),
        out_specs=[ANY] * len(values),
        input_output_aliases={i: i for i in range(len(values))},
        compiler_params=params(1),
        cost_estimate=cost(0),
        name="tie",
    )(*values, *after)


def ring_gather(block, split=0):
    up, down = cycle_perm(1), cycle_perm(-1)
    low = high = block
    own = [block]
    for _ in range(3):
        low = lax.ppermute(low, "batch", up)
        high = lax.ppermute(high, "batch", down)
        own += [low, high]
    if split:
        own.append(lax.ppermute(low[:, :split], "batch", up))
        own.append(lax.ppermute(high[:, split:], "batch", down))
    else:
        own.append(lax.ppermute(low, "batch", up))
    return own


def swapped(blocks):
    return [swap(v, 1) for v in blocks]


class RingSum:
    def __init__(self, parts):
        self.mine, self.other = parts[0], swap(parts[1], 1)
        self.low, self.high = self.term(4).astype(BF16), self.term(5).astype(BF16)
        self.ahead = 4

    def term(self, j):
        return self.mine[j].astype(F32) + self.other[j].astype(F32)

    def step(self, after=()):
        low = lax.ppermute(self.low, "batch", cycle_perm(1))
        high = lax.ppermute(self.high, "batch", cycle_perm(-1))
        if after:
            low, high = tie([low, high], list(after))
        self.ahead -= 1
        self.low = (low.astype(F32) + self.term(self.ahead)).astype(BF16)
        if self.ahead > 1:
            self.high = (high.astype(F32) + self.term(9 - self.ahead)).astype(BF16)
        else:
            self.high = high
        return [self.low]

    def finish(self):
        low = lax.ppermute(self.low, "batch", cycle_perm(1))
        return low.astype(F32) + self.high.astype(F32) + self.term(0)


def scatter_sum(whole):
    return lax.psum_scatter(whole, "batch", scatter_dimension=0, tiled=True).astype(F32)


def dot(left, right):
    return jnp.dot(left, right, preferred_element_type=F32)


def dot_nt(left, right):
    return lax.dot_general(left, right, (((1,), (1,)), ((), ())), preferred_element_type=F32)


def store_blocks(offs, src, parts, sems):
    copies = []
    if len(parts) == 1:
        copies.append(pltpu.make_async_copy(src, parts[0].at[0], sems.at[0]))
    else:
        rows = src.shape[0] // 16
        for k in range(16):
            at = pl.multiple_of(offs[k] * rows, 16)
            place = parts[k // 8].at[k % 8]
            copies.append(pltpu.make_async_copy(src.at[pl.ds(at, rows), :], place, sems.at[k]))
    for copy in copies:
        copy.start()
    return copies


def grad_shapes(n_blocks, rows, cols):
    if n_blocks == 1:
        return [jax.ShapeDtypeStruct((1, rows, cols), BF16)]
    return [jax.ShapeDtypeStruct((8, rows // 16, cols), BF16)] * 2


def params(mib):
    return pltpu.CompilerParams(vmem_limit_bytes=mib * MIB)


def cost(micros):
    return pl.CostEstimate(flops=int(micros * 1e9), bytes_accessed=0, transcendentals=0)


def norm_rows(values):
    centre = values - jnp.mean(values, axis=-1, keepdims=True)
    inverse = lax.rsqrt(jnp.mean(centre * centre, axis=-1, keepdims=True) + EPS)
    return centre * inverse, inverse


def norm_back(upstream, normed, inverse, gain):
    scaled = upstream * gain
    return inverse * (
        scaled
        - jnp.mean(scaled, axis=-1, keepdims=True)
        - normed * jnp.mean(scaled * normed, axis=-1, keepdims=True)
    )


def half_mask(rows, half):
    lane = lax.broadcasted_iota(jnp.int32, (rows, 128), 1)
    return (lane < HEAD_DIM) if half == 0 else (lane >= HEAD_DIM)


def round_kernel(n_after, weight, *refs):
    refs[n_after][...] = weight[...].astype(BF16)


def rounded(weight, after):
    return pl.pallas_call(
        functools.partial(round_kernel, len(after)),
        out_shape=jax.ShapeDtypeStruct(weight.shape, BF16),
        in_specs=[VMEM] + [ANY] * len(after),
        out_specs=VMEM,
        compiler_params=params(60),
        cost_estimate=cost(1),
        name="round_weight",
    )(weight, *after)


def project_kernel(n_blocks, offs, maps, blocks, pre, whole, small, sems, small_sems):
    copies = []
    rows = whole.shape[0] // n_blocks
    for i in range(n_blocks):
        block = blocks.at[i]
        which = offs[i] if n_blocks > 1 else 0
        at = pl.multiple_of(which * rows, 16)
        copies.append(
            pltpu.make_async_copy(block.at[pl.ds(0, rows), :], whole.at[pl.ds(at, rows), :], sems.at[i])
        )
        copies.append(
            pltpu.make_async_copy(block.at[pl.ds(rows, 16), :], small.at[which], small_sems.at[i])
        )
    for copy in copies:
        copy.start()
    for copy in copies:
        copy.wait()
    for i in range(2):
        pick = pl.ds(i * (TLEN // 2), TLEN // 2)
        pre[pick, :] = dot(maps[pick, :], whole[...]).astype(BF16)


def project(offs, maps, blocks):
    n = blocks.shape[0]
    rows = blocks.shape[1] - 16
    channels = n * rows
    return pl.pallas_call(
        functools.partial(project_kernel, n),
        out_shape=[
            jax.ShapeDtypeStruct((TLEN, D), BF16),
            jax.ShapeDtypeStruct((channels, D), BF16),
            jax.ShapeDtypeStruct((n, 16, D), BF16),
        ],
        in_specs=[SMEM, VMEM, ANY],
        out_specs=[VMEM] * 3,
        scratch_shapes=[pltpu.SemaphoreType.DMA((n,)), pltpu.SemaphoreType.DMA((n,))],
        compiler_params=params(60),
        cost_estimate=cost(60),
        name="project_maps",
    )(offs, maps, blocks)


def bias_kernel(n_after, bucket, table, *refs):
    bias = refs[n_after]
    for t in range(TLEN // 128):
        lanes = slice(t * 128, (t + 1) * 128)
        which = bucket[:, lanes]
        for head in range(HEADS):
            row = jnp.broadcast_to(table[head : head + 1, :], which.shape)
            bias[head, :, lanes] = jnp.take_along_axis(row, which, axis=1).astype(BF16)


def spatial_bias(bucket, table, after):
    rows = 64
    return pl.pallas_call(
        functools.partial(bias_kernel, len(after)),
        grid=(TLEN // rows,),
        out_shape=jax.ShapeDtypeStruct((HEADS, TLEN, TLEN), BF16),
        in_specs=[
            pl.BlockSpec((rows, TLEN), lambda i: (i, 0)),
            pl.BlockSpec((16, 128), lambda i: (0, 0)),
        ]
        + [ANY] * len(after),
        out_specs=pl.BlockSpec((HEADS, rows, TLEN), lambda i: (0, i, 0)),
        compiler_params=params(60),
        cost_estimate=cost(5),
        name="spatial_bias",
    )(bucket, table, *after)


def attn_fwd_kernel(n_after, live, attn, bias, text, pre, bn, vec, *refs):
    qkv_out, probs, x_out, ctx, normed, inverse = refs[n_after : n_after + 6]
    weight, qkv, score_a, score_b, prob_a, prob_b, ctx_a, sems, in_sems, out_sems = refs[n_after + 6 :]
    loads = []
    for part in range(4):
        cols = pl.ds(part * D, D)
        loads.append(pltpu.make_async_copy(attn.at[:, cols], weight.at[:, cols], sems.at[part]))
        loads[-1].start()

    def bring(head):
        place = (prob_a, prob_b)[head % 2].at[head // 2]
        return pltpu.make_async_copy(bias.at[head], place, in_sems.at[head])

    for head in range(HEADS):
        bring(head).start()
    alive = lax.broadcasted_iota(jnp.int32, (TLEN, 1), 0) < live[0]
    visual = (pre[...] - bn[0:1, :]) * bn[1:2, :] * bn[2:3, :] + bn[3:4, :]
    x = jnp.where(live[1] == 1, text[...].astype(F32), jnp.where(alive, visual, 0.0))
    x_low = x.astype(BF16)
    x_out[...] = x_low
    exports = []
    for part in range(3):
        cols = slice(part * D, (part + 1) * D)
        loads[part].wait()
        value = dot(x_low, weight[:, cols])
        if part != 1:
            value = value + vec[part // 2 : part // 2 + 1, :]
        qkv[:, cols] = value.astype(BF16)
        exports.append(
            pltpu.make_async_copy(qkv.at[:, cols], qkv_out.at[:, cols], out_sems.at[HEADS + part])
        )
        exports[-1].start()

    def lanes(start, pair):
        return pl.ds(pl.multiple_of(start + pair * 128, 128), 128)

    def scores(pair, half, out):
        query = qkv[:, lanes(0, pair)] * SCALE
        query = jnp.where(half_mask(TLEN, half), query, jnp.zeros_like(query))
        out[...] = dot_nt(query, qkv[:, lanes(D, pair)])

    def softmax(score, prob, pair):
        key_valid = lax.broadcasted_iota(jnp.int32, (SOFT, TLEN), 1) < live[0]
        for i in range(TLEN // SOFT):
            rows = slice(i * SOFT, (i + 1) * SOFT)
            value = score[rows, :] + prob[pair, rows, :].astype(F32)
            value = jnp.where(key_valid, value, -1000000000.0)
            peak = jnp.max(value, axis=-1, keepdims=True)
            raised = jnp.exp(value - peak)
            total = jnp.sum(raised, axis=-1, keepdims=True)
            prob[pair, rows, :] = (raised * (1.0 / total)).astype(BF16)

    scores(0, 0, score_a)
    for head in range(HEADS):
        bring(head).wait()

    def step(pair, carry):
        values = qkv[:, lanes(2 * D, pair)]
        scores(pair, 1, score_b)
        softmax(score_a, prob_a, pair)
        scores(jnp.minimum(pair + 1, PAIRS - 1), 0, score_a)
        ctx_a[...] = dot(prob_a[pair], values)
        softmax(score_b, prob_b, pair)
        ctx_b = dot(prob_b[pair], values)
        ctx[:, lanes(0, pair)] = jnp.where(half_mask(TLEN, 0), ctx_a[...], ctx_b).astype(BF16)
        for half, prob in enumerate((prob_a, prob_b)):
            head = 2 * pair + half
            pltpu.make_async_copy(prob.at[pair], probs.at[head], out_sems.at[head]).start()
        return carry

    lax.fori_loop(0, PAIRS, step, 0)
    loads[3].wait()
    att = dot(ctx[...], weight[:, 3 * D :]) + vec[2:3, :]
    normal, inv = norm_rows(x + att)
    normed[...] = normal
    inverse[...] = jnp.broadcast_to(inv, (TLEN, 128))
    for copy in exports:
        copy.wait()
    for head in range(HEADS):
        prob = (prob_a, prob_b)[head % 2]
        pltpu.make_async_copy(prob.at[head // 2], probs.at[head], out_sems.at[head]).wait()


def attn_fwd(live, attn, bias, text, pre, bn, vec, after):
    return pl.pallas_call(
        functools.partial(attn_fwd_kernel, len(after)),
        out_shape=[
            jax.ShapeDtypeStruct((TLEN, 3 * D), BF16),
            jax.ShapeDtypeStruct((HEADS, TLEN, TLEN), BF16),
            jax.ShapeDtypeStruct((TLEN, D), BF16),
            jax.ShapeDtypeStruct((TLEN, D), BF16),
            jax.ShapeDtypeStruct((TLEN, D), F32),
            jax.ShapeDtypeStruct((TLEN, 128), F32),
        ],
        in_specs=[SMEM, ANY, ANY] + [VMEM] * 4 + [ANY] * len(after),
        out_specs=[ANY, ANY] + [VMEM] * 4,
        scratch_shapes=[
            pltpu.VMEM((D, 4 * D), BF16),
            pltpu.VMEM((TLEN, 3 * D), BF16),
            pltpu.VMEM((TLEN, TLEN), F32),
            pltpu.VMEM((TLEN, TLEN), F32),
            pltpu.VMEM((PAIRS, TLEN, TLEN), BF16),
            pltpu.VMEM((PAIRS, TLEN, TLEN), BF16),
            pltpu.VMEM((TLEN, 128), F32),
            pltpu.SemaphoreType.DMA((4,)),
            pltpu.SemaphoreType.DMA((HEADS,)),
            pltpu.SemaphoreType.DMA((HEADS + 3,)),
        ],
        compiler_params=params(60),
        cost_estimate=cost(15),
        name="attention_forward",
    )(live, attn, bias, text, pre, bn, vec, *after)


def load_ffn(offs, blocks, up, down, sems):
    first, second = [], []
    if len(blocks) == 1:
        first.append(pltpu.make_async_copy(blocks[0].at[:, pl.ds(0, FF)], up, sems.at[0]))
        second.append(pltpu.make_async_copy(blocks[0].at[:, pl.ds(FF, FF)], down, sems.at[1]))
        return first, second
    at = 0
    for slot in range(16):
        rows = pl.ds(pl.multiple_of(offs[slot] * 48, 16), 48)
        if slot % 8 < 7:
            left, right = blocks[at].at[:, pl.ds(0, FF)], blocks[at].at[:, pl.ds(FF, FF)]
            at += 1
        else:
            left, right = blocks[at], blocks[at + 1]
            at += 2
        first.append(pltpu.make_async_copy(left, up.at[rows, :], sems.at[2 * slot]))
        second.append(pltpu.make_async_copy(right, down.at[rows, :], sems.at[2 * slot + 1]))
    return first, second


def ffn_kernel(n_blocks, live, offs, attn, normed, inverse, vec, joined_grad, *refs):
    blocks, refs = refs[:n_blocks], refs[n_blocks:]
    part, refs = refs[0], refs[1:]
    result, grad_residual, grad_attended, grad_ctx, grad_ctx_t, grads = refs[:6]
    up, down, active, slope, grad, total, weight, sems, last_sems, out_sems = refs[6:]
    loads = load_ffn(offs, blocks, up, down, sems)
    for copy in loads[0] + loads[1]:
        copy.start()
    last = pltpu.make_async_copy(attn.at[:, pl.ds(3 * D, D)], weight, last_sems.at[0])
    last.start()
    first = normed[...] * vec[3:4, :] + vec[4:5, :]
    first_low = first.astype(BF16)
    for copy in loads[0]:
        copy.wait()
    units = dot(first_low, up[:, :D])
    total[...] = first + vec[9:10, :]
    for k in range(CHUNKS):
        units = units + vec[5 + k : 6 + k, :]
        if k + 1 < CHUNKS:
            following = dot(first_low, up[:, (k + 1) * D : (k + 2) * D])
        square = units * units
        root = math.sqrt(2.0 / math.pi)
        bend = jnp.tanh(root * units * (1.0 + 0.044715 * square))
        half = 0.5 * (1.0 + bend)
        active[k] = (units * half).astype(BF16)
        slope[k] = (
            half + 0.5 * root * units * (1.0 - bend * bend) * (1.0 + 3.0 * 0.044715 * square)
        ).astype(BF16)
        if k == 0:
            for copy in loads[1]:
                copy.wait()
        total[...] += dot_nt(active[k], down[:, k * D : (k + 1) * D])
        if k + 1 < CHUNKS:
            units = following
    normal, inv = norm_rows(total[...])
    mask = lax.broadcasted_iota(jnp.int32, (TLEN, 1), 0) < live[0]
    result[...] = jnp.where(mask, normal * vec[10:11, :] + vec[11:12, :], 0.0).astype(BF16)
    upstream = jnp.where(mask, joined_grad[...].astype(F32), 0.0)
    second = norm_back(upstream, normal, inv, vec[10:11, :])
    second_low = second.astype(BF16)
    total[...] = second
    grads[9:10, :] = jnp.sum(second_low.astype(F32), axis=0, keepdims=True)
    grads[10:11, :] = jnp.sum(upstream * normal, axis=0, keepdims=True)
    grads[11:12, :] = jnp.sum(upstream, axis=0, keepdims=True)
    turned = second_low.T
    for k in range(CHUNKS):
        cols = slice(FF + k * D, FF + (k + 1) * D)
        grad[:, cols] = dot(turned, active[k]).astype(BF16)
    cols = pl.ds(FF, FF)
    copies = [pltpu.make_async_copy(grad.at[:, cols], part.at[:, cols], out_sems.at[0])]
    copies[0].start()
    turned = first_low.T
    for k in range(CHUNKS):
        cols = slice(k * D, (k + 1) * D)
        inner = (dot(second_low, down[:, cols]) * slope[k].astype(F32)).astype(BF16)
        grads[5 + k : 6 + k, :] = jnp.sum(inner.astype(F32), axis=0, keepdims=True)
        total[...] += dot_nt(inner, up[:, cols])
        grad[:, cols] = dot(turned, inner).astype(BF16)
    cols = pl.ds(0, FF)
    copies.append(pltpu.make_async_copy(grad.at[:, cols], part.at[:, cols], out_sems.at[1]))
    copies[-1].start()
    upstream = total[...]
    grads[3:4, :] = jnp.sum(upstream * normed[...], axis=0, keepdims=True)
    grads[4:5, :] = jnp.sum(upstream, axis=0, keepdims=True)
    residual = norm_back(upstream, normed[...], inverse[:, 0:1], vec[3:4, :])
    grad_residual[...] = residual
    attended = residual.astype(BF16)
    grad_attended[...] = attended
    grads[2:3, :] = jnp.sum(attended.astype(F32), axis=0, keepdims=True)
    grads[0:2, :] = jnp.zeros((2, D), F32)
    grads[12:16, :] = jnp.zeros((4, D), F32)
    last.wait()
    back = dot_nt(attended, weight[...]).astype(BF16)
    grad_ctx[...] = back
    grad_ctx_t[...] = back.T
    for copy in copies:
        copy.wait()


def feed_forward(live, offs, blocks, attn, normed, inverse, vec, joined_grad):
    n = len(blocks)
    out = pl.pallas_call(
        functools.partial(ffn_kernel, n),
        out_shape=[
            jax.ShapeDtypeStruct((D, 2 * FF), BF16),
            jax.ShapeDtypeStruct((TLEN, D), BF16),
            jax.ShapeDtypeStruct((TLEN, D), F32),
            jax.ShapeDtypeStruct((TLEN, D), BF16),
            jax.ShapeDtypeStruct((TLEN, D), BF16),
            jax.ShapeDtypeStruct((D, TLEN), BF16),
            jax.ShapeDtypeStruct((16, D), F32),
        ],
        in_specs=[SMEM, SMEM, ANY] + [VMEM] * 4 + [ANY] * n,
        out_specs=[ANY] + [VMEM] * 6,
        scratch_shapes=[
            pltpu.VMEM((D, FF), BF16),
            pltpu.VMEM((D, FF), BF16),
            pltpu.VMEM((CHUNKS, TLEN, D), BF16),
            pltpu.VMEM((CHUNKS, TLEN, D), BF16),
            pltpu.VMEM((D, 2 * FF), BF16),
            pltpu.VMEM((TLEN, D), F32),
            pltpu.VMEM((D, D), BF16),
            pltpu.SemaphoreType.DMA((32,)),
            pltpu.SemaphoreType.DMA((1,)),
            pltpu.SemaphoreType.DMA((2,)),
        ],
        compiler_params=params(60),
        cost_estimate=cost(30),
        name="feed_forward",
    )(live, offs, attn, normed, inverse, vec, joined_grad, *blocks)
    return out


def pairs_kernel(n_after, queries, keys, values, back, context, back_t, probs, *refs):
    query_t = (queries[...] * SCALE).T
    grad_query, grad_key_t, grad_value_t, grad_scores = refs[n_after:]
    total = jnp.zeros((TLEN, 128), F32)
    for half in range(2):
        mask = half_mask(TLEN, half)
        masked = jnp.where(mask, back[...], jnp.zeros_like(back[...]))
        prob = probs[half]
        slopes = dot_nt(masked, values[...])
        delta = jnp.sum(masked.astype(F32) * context[...].astype(F32), axis=-1, keepdims=True)
        slopes = (prob.astype(F32) * (slopes - delta)).astype(BF16)
        grad_scores[half] = slopes
        near = jnp.where(mask, keys[...], jnp.zeros_like(keys[...]))
        total = total + dot(slopes, near)
        lines = slice(half * HEAD_DIM, (half + 1) * HEAD_DIM)
        grad_key_t[lines, :] = dot(query_t[lines, :], slopes).astype(BF16)
        grad_value_t[lines, :] = dot(back_t[lines, :], prob).astype(BF16)
    grad_query[...] = (total * SCALE).astype(BF16)


def attn_bwd_pairs(first, count, qkv, grad_ctx, ctx, grad_ctx_t, probs, after):
    def cols(base):
        return pl.BlockSpec((TLEN, 128), lambda i: (0, base + i))

    def lines(base):
        return pl.BlockSpec((128, TLEN), lambda i: (base + i, 0))

    def heads(base):
        return pl.BlockSpec((2, TLEN, TLEN), lambda i: (base + i, 0, 0))

    return pl.pallas_call(
        functools.partial(pairs_kernel, len(after)),
        grid=(count,),
        out_shape=[
            jax.ShapeDtypeStruct((TLEN, 128 * count), BF16),
            jax.ShapeDtypeStruct((128 * count, TLEN), BF16),
            jax.ShapeDtypeStruct((128 * count, TLEN), BF16),
            jax.ShapeDtypeStruct((2 * count, TLEN, TLEN), BF16),
        ],
        in_specs=[
            cols(first),
            cols(PAIRS + first),
            cols(2 * PAIRS + first),
            cols(first),
            cols(first),
            lines(first),
            heads(first),
        ]
        + [ANY] * len(after),
        out_specs=[cols(0), lines(0), lines(0), heads(0)],
        compiler_params=params(60),
        cost_estimate=cost(5),
        name="attention_backward",
    )(qkv, qkv, qkv, grad_ctx, ctx, grad_ctx_t, probs, *after)


def input_kernel(n_parts, n_after, live, attn, grads, grad_residual, pre, bn, *refs):
    queries, refs = refs[:n_parts], refs[n_parts:]
    keys_t, refs = refs[:n_parts], refs[n_parts:]
    values_t, refs = refs[:n_parts], refs[n_parts + n_after :]
    grad_qkv, grad_input, grad_bn, sums, weight, sems = refs
    load = pltpu.make_async_copy(attn.at[:, pl.ds(0, 3 * D)], weight, sems.at[0])
    load.start()
    at = 0
    for query, key, value in zip(queries, keys_t, values_t):
        width = query.shape[1]
        grad_qkv[:, at : at + width] = query[...]
        grad_qkv[:, D + at : D + at + width] = key[...].T
        grad_qkv[:, 2 * D + at : 2 * D + at + width] = value[...].T
        at += width
    load.wait()
    total = grad_residual[...] + dot_nt(grad_qkv[...], weight[...])
    grad_input[...] = total
    alive = lax.broadcasted_iota(jnp.int32, (TLEN, 1), 0) < live[0]
    back = jnp.where(jnp.logical_and(alive, live[1] == 0), total, 0.0)
    grad_bn[...] = back.astype(BF16)
    normal = (pre[...] - bn[0:1, :]) * bn[1:2, :]
    sums[...] = grads[...]
    sums[0:1, :] = jnp.sum(grad_qkv[:, :D].astype(F32), axis=0, keepdims=True)
    sums[1:2, :] = jnp.sum(grad_qkv[:, 2 * D :].astype(F32), axis=0, keepdims=True)
    sums[12:13, :] = jnp.sum(back * normal, axis=0, keepdims=True)
    sums[13:14, :] = jnp.sum(back, axis=0, keepdims=True)


def attn_bwd_input(live, attn, grads, grad_residual, pre, bn, queries, keys_t, values_t, after):
    parts = len(queries)
    return pl.pallas_call(
        functools.partial(input_kernel, parts, len(after)),
        out_shape=[
            jax.ShapeDtypeStruct((TLEN, 3 * D), BF16),
            jax.ShapeDtypeStruct((TLEN, D), F32),
            jax.ShapeDtypeStruct((TLEN, D), BF16),
            jax.ShapeDtypeStruct((16, D), F32),
        ],
        in_specs=[SMEM, ANY] + [VMEM] * (3 * parts + 4) + [ANY] * len(after),
        out_specs=[VMEM] * 4,
        scratch_shapes=[pltpu.VMEM((D, 3 * D), BF16), pltpu.SemaphoreType.DMA((1,))],
        compiler_params=params(60),
        cost_estimate=cost(5),
        name="input_gradient",
    )(live, attn, grads, grad_residual, pre, bn, *queries, *keys_t, *values_t, *after)


def table_kernel(n_parts, n_after, bucket, sums, *refs):
    parts, (out, one_hot, total) = refs[:n_parts], refs[n_parts + n_after :]
    step = pl.program_id(0)

    @pl.when(step == 0)
    def _():
        total[...] = jnp.zeros_like(total)

    for group in range(ROWS // 16):
        lines = slice(group * 16, (group + 1) * 16)
        which = bucket[lines, :]
        for b in range(BUCKETS):
            one_hot[b * 16 : (b + 1) * 16, :] = jnp.where(which == b, 1.0, 0.0).astype(BF16)
        slopes = jnp.concatenate(
            [part[:, lines, :].reshape(part.shape[0] * 16, TLEN) for part in parts], axis=0
        )
        total[...] += dot_nt(one_hot[...], slopes)

    @pl.when(step == STEPS - 1)
    def _():
        line = lax.broadcasted_iota(jnp.int32, (BUCKETS * 16, HEADS * 16), 0) % 16
        lane = lax.broadcasted_iota(jnp.int32, (BUCKETS * 16, HEADS * 16), 1) % 16
        kept = jnp.where(line == lane, total[...], 0.0)
        kept = jnp.sum(kept.reshape(BUCKETS, 16, HEADS * 16), axis=1)
        shape = (HEADS * 16, BUCKETS * HEADS)
        head = lax.broadcasted_iota(jnp.int32, shape, 0) // 16
        pick = lax.broadcasted_iota(jnp.int32, shape, 1) % HEADS
        spread = jnp.dot(
            kept,
            jnp.where(head == pick, 1.0, 0.0),
            precision=lax.Precision.HIGHEST,
            preferred_element_type=F32,
        )
        shape = (BUCKETS, BUCKETS * HEADS)
        own = lax.broadcasted_iota(jnp.int32, shape, 1) // HEADS
        spread = jnp.where(own == lax.broadcasted_iota(jnp.int32, shape, 0), spread, 0.0)
        out[...] = sums[...]
        out[14:15, : BUCKETS * HEADS] = jnp.sum(spread, axis=0, keepdims=True)


def table_grad(bucket, sums, parts, after):
    return pl.pallas_call(
        functools.partial(table_kernel, len(parts), len(after)),
        grid=(STEPS,),
        out_shape=jax.ShapeDtypeStruct((16, D), F32),
        in_specs=[
            pl.BlockSpec((ROWS, TLEN), lambda i: (i, 0)),
            pl.BlockSpec((16, D), lambda i: (0, 0)),
        ]
        + [pl.BlockSpec((part.shape[0], ROWS, TLEN), lambda i: (0, i, 0)) for part in parts]
        + [ANY] * len(after),
        out_specs=pl.BlockSpec((16, D), lambda i: (0, 0)),
        scratch_shapes=[
            pltpu.VMEM((BUCKETS * 16, TLEN), BF16),
            pltpu.VMEM((BUCKETS * 16, HEADS * 16), F32),
        ],
        compiler_params=params(60),
        cost_estimate=cost(5),
        name="table_gradient",
    )(bucket, sums, *parts, *after)


def outer_kernel(n_parts, n_after, widths, offs, *refs):
    count = len(widths)
    lefts, rights, refs = refs[:count], refs[count : 2 * count], refs[2 * count + n_after :]
    parts, (grad, sems) = refs[:n_parts], refs[n_parts:]
    at = 0
    for left, right, width in zip(lefts, rights, widths):
        turned = left[...].astype(BF16).T
        for lo in range(0, width, D):
            grad[:, at + lo : at + lo + D] = dot(turned, right[:, lo : lo + D]).astype(BF16)
        at += width
    for copy in store_blocks(offs, grad, parts, sems):
        copy.wait()


def outer(offs, n_blocks, lefts, rights, after):
    widths = tuple(right.shape[1] for right in rights)
    rows = lefts[0].shape[1]
    parts = grad_shapes(n_blocks, rows, sum(widths))
    return pl.pallas_call(
        functools.partial(outer_kernel, len(parts), len(after), widths),
        out_shape=parts,
        in_specs=[SMEM] + [VMEM] * (2 * len(widths)) + [ANY] * len(after),
        out_specs=[ANY] * len(parts),
        scratch_shapes=[
            pltpu.VMEM((rows, sum(widths)), BF16),
            pltpu.SemaphoreType.DMA((16,)),
        ],
        compiler_params=params(60),
        cost_estimate=cost(5),
        name="weight_gradient",
    )(offs, *lefts, *rights, *after)


def project_grad_kernel(n_parts, n_after, live, places, maps, own, other, pre, bn, totals, *refs):
    parts, refs = refs[n_after : n_after + n_parts], refs[n_after + n_parts :]
    grad_pre, grad, sems = refs
    alive = lax.broadcasted_iota(jnp.int32, (TLEN, 1), 0) < live[0]
    normal = (pre[...] - bn[0:1, :]) * bn[1:2, :]
    count = bn[4:5, :]
    back = own[...].astype(F32) + other[...].astype(F32)
    back = back - totals[1:2, :] / count - normal * (totals[0:1, :] / count)
    low = jnp.where(alive, back * (bn[1:2, :] * bn[2:3, :]), 0.0).astype(BF16)
    grad_pre[...] = low
    grad[...] = dot(maps[...].T, low).astype(BF16)
    for copy in store_blocks(places, grad, parts, sems):
        copy.wait()


def project_gradient(live, places, n_blocks, maps, own, other, pre, bn, totals, after):
    rows = maps.shape[1]
    parts = grad_shapes(n_blocks, rows, D)
    out = pl.pallas_call(
        functools.partial(project_grad_kernel, len(parts), len(after)),
        out_shape=parts + [jax.ShapeDtypeStruct((TLEN, D), BF16)],
        in_specs=[SMEM, SMEM] + [VMEM] * 6 + [ANY] * len(after),
        out_specs=[ANY] * len(parts) + [VMEM],
        scratch_shapes=[
            pltpu.VMEM((rows, D), BF16),
            pltpu.SemaphoreType.DMA((16,)),
        ],
        compiler_params=params(60),
        cost_estimate=cost(5),
        name="project_gradient",
    )(live, places, maps, own, other, pre, bn, totals, *after)
    return out[:-1], out[-1]


def maps_kernel(grad_pre, weight, result, other, grad_maps, joined):
    joined[...] = result[...] + other[...]
    grad_maps[...] = dot_nt(grad_pre[...], weight[...])


def maps_gradient(grad_pre, weight, result, other):
    return pl.pallas_call(
        maps_kernel,
        out_shape=[
            jax.ShapeDtypeStruct((TLEN, weight.shape[0]), F32),
            jax.ShapeDtypeStruct((TLEN, D), BF16),
        ],
        in_specs=[VMEM] * 4,
        out_specs=[VMEM] * 2,
        compiler_params=params(60),
        cost_estimate=cost(1),
        name="maps_gradient",
    )(grad_pre, weight, result, other)


def nesterov(weight, moment, average, gradient, rate):
    moment_new = MOMENTUM * moment + gradient
    weight_new = weight - rate * (gradient + MOMENTUM * moment_new)
    return (weight_new, moment_new, AVERAGE * average + (1.0 - AVERAGE) * weight_new)


def stats_kernel(n_after, live, own, other, *refs):
    pre, stats = refs[n_after:]
    total = (own[...].astype(F32) + other[...].astype(F32)).astype(BF16).astype(F32)
    pre[...] = total
    count = live[0].astype(F32)
    mask = lax.broadcasted_iota(jnp.int32, (TLEN, 1), 0) < live[0]
    mean = jnp.sum(jnp.where(mask, total, 0.0), axis=0, keepdims=True) / count
    centre = jnp.where(mask, total - mean, 0.0)
    stats[...] = jnp.concatenate(
        [
            mean,
            jnp.sum(centre * centre, axis=0, keepdims=True),
            jnp.full((6, D), count, F32),
        ],
        axis=0,
    )


def local_stats(live, own, other, after):
    return pl.pallas_call(
        functools.partial(stats_kernel, len(after)),
        out_shape=[
            jax.ShapeDtypeStruct((TLEN, D), F32),
            jax.ShapeDtypeStruct((8, D), F32),
        ],
        in_specs=[SMEM, VMEM, VMEM] + [ANY] * len(after),
        out_specs=[VMEM, VMEM],
        compiler_params=params(60),
        cost_estimate=cost(40),
        name="local_statistics",
    )(live, own, other, *after)


def exchange_steps():
    bit, n = 1, lax.axis_size("batch")
    while bit < n:
        partners = [bit] if 2 * bit == n else [bit, 2 * bit, 3 * bit]
        bit *= 2 * len(partners) if len(partners) == 1 else 4
        yield partners, bit >= n


def merge_kernel(count, last, *refs):
    parts, out = refs[:count], refs[-1]
    total = parts[0][2:3, :]
    mean = parts[0][0:1, :] * total
    for part in parts[1:]:
        total = total + part[2:3, :]
        mean = mean + part[0:1, :] * part[2:3, :]
    mean = mean / total
    spread = jnp.zeros_like(mean)
    for part in parts:
        gap = part[0:1, :] - mean
        spread = spread + part[1:2, :] + gap * gap * part[2:3, :]
    out[0:1, :] = mean
    out[1:2, :] = spread
    out[2:8, :] = jnp.broadcast_to(total, (6, D))
    if last:
        out[1:2, :] = lax.rsqrt(spread / total + EPS)
        out[2:4, :] = refs[count][0:2, :]


def merge_stats(stats, gains, after):
    for partners, last in exchange_steps():
        parts = [stats] + [swap(stats, bit) for bit in partners]
        operands = parts + ([gains] if last else [])
        stats = pl.pallas_call(
            functools.partial(merge_kernel, len(parts), last),
            out_shape=jax.ShapeDtypeStruct((8, D), F32),
            in_specs=[VMEM] * len(operands) + [ANY] * len(after),
            out_specs=VMEM,
            cost_estimate=cost(15),
            name="merge_statistics",
        )(*operands, *after)
        after = []
    return stats


def add_kernel(count, *refs):
    total = refs[0][...]
    for part in refs[1:count]:
        total = total + part[...]
    refs[-1][...] = total


def sum_small(values, after, begin=0, end=None):
    for step, (partners, _) in enumerate(list(exchange_steps())[begin:end]):
        parts = [values] + [swap(values, bit) for bit in partners]
        ties = after[step] if step < len(after) else []
        values = pl.pallas_call(
            functools.partial(add_kernel, len(parts)),
            out_shape=jax.ShapeDtypeStruct(values.shape, F32),
            in_specs=[VMEM] * len(parts) + [ANY] * len(ties),
            out_specs=VMEM,
            cost_estimate=cost(0.5),
            name="sum_small",
        )(*parts, *ties)
    return values


def on_device(
    text_embed,
    visual_maps,
    visual_bucket,
    rel_bucket,
    joined_grad,
    attn_weight,
    attn_moment,
    attn_average,
    ffn_weight,
    ffn_moment,
    ffn_average,
    vector_weight,
    vector_moment,
    vector_average,
    project_weight,
    project_moment,
    project_average,
    shared_weight,
    shared_moment,
    shared_average,
):
    n_batch = lax.axis_size("batch")
    me = lax.axis_index("batch")
    ringed = n_batch == 16
    is_text = lax.axis_index("stream") == 0
    maps = visual_maps.reshape(TLEN, -1)

    small = jnp.zeros((16, D), BF16)
    small = small.at[0, : vector_weight.shape[1]].set(vector_weight[0].astype(BF16))
    small = small.at[1, : shared_weight.shape[0]].set(shared_weight.astype(BF16))
    attn_low = rounded(attn_weight[0], [])
    attn_full = lax.all_gather(attn_low, "batch", axis=0, tiled=True)
    packed = jnp.concatenate([project_weight.astype(BF16), small], axis=0)
    if ringed:
        sources = jnp.asarray(gather_sources())[me]
        targets = jnp.asarray(scatter_targets())[me]
        project_blocks = ring_gather(packed)
        project_blocks += swapped(project_blocks)
        ffn_low = rounded(ffn_weight[0], project_blocks[5:7])
        ffn_blocks = ring_gather(ffn_low, FF)
        ffn_other = swapped(ffn_blocks[:7])
        n_blocks = 16
    else:
        sources = jnp.zeros((1,), jnp.int32)
        targets = jnp.zeros((1,), jnp.int32)
        rows = lax.all_gather(project_weight.astype(BF16), "batch", axis=0, tiled=True)
        project_blocks = [jnp.concatenate([rows, jnp.zeros((16, D), BF16)], axis=0)]
        ffn_low = rounded(ffn_weight[0], [])
        ffn_blocks = [lax.all_gather(ffn_low, "batch", axis=0, tiled=True)]
        n_blocks = 1

    partial_pre, project_half, small_all = project(sources, maps, jnp.stack(project_blocks))
    if not ringed:
        small_all = lax.all_gather(small, "batch", axis=0, tiled=False)
    other_pre = across(partial_pre)
    vector_rows = small_all[:, 0, : vector_weight.shape[1]].reshape(12, D).astype(F32)
    vec = jnp.concatenate([vector_rows, jnp.zeros((4, D), F32)], axis=0)
    shared_full = small_all[:, 1, : shared_weight.shape[0]].reshape(-1).astype(F32)
    table = jnp.zeros((16, 128), F32)
    table = table.at[:HEADS, :BUCKETS].set(
        shared_full[: BUCKETS * HEADS].reshape(BUCKETS, HEADS).T
    )
    gains = shared_full[BUCKETS * HEADS :].reshape(2, D)

    bucket = rel_bucket.reshape(TLEN, TLEN)
    bias = spatial_bias(bucket, table, [])
    visual_len = ((visual_bucket + 1) * (TLEN // 2)).astype(jnp.int32)
    pre, stats = local_stats(
        visual_len, partial_pre, other_pre, [bias] + (ffn_blocks[1:3] if ringed else [])
    )
    bn = merge_stats(stats, gains, ffn_blocks[3:5] if ringed else [])
    text = is_text.astype(jnp.int32)
    live = jnp.stack([jnp.where(is_text, TLEN, visual_len[0]), text])
    visual_live = jnp.stack([visual_len[0], text])

    qkv, probs, x_low, ctx, normed, inverse = attn_fwd(
        live,
        attn_full,
        bias,
        text_embed.reshape(TLEN, D),
        pre,
        bn,
        vec,
        ffn_blocks[5:7] + ffn_other if ringed else [],
    )
    if ringed:
        ffn_last = list(tie(ffn_blocks[7:], [normed]))
        ffn_blocks = ffn_blocks[:7] + ffn_last + ffn_other + swapped(ffn_last)
    ffn_part, result, grad_residual, grad_attended, grad_ctx, grad_ctx_t, grads = feed_forward(
        live,
        sources,
        ffn_blocks,
        attn_full,
        normed,
        inverse,
        vec,
        joined_grad.reshape(TLEN, D),
    )
    ffn_sum = scatter_sum(ffn_part)
    queries, keys_t, values_t, score_grads = (
        [piece]
        for piece in attn_bwd_pairs(0, PAIRS, qkv, grad_ctx, ctx, grad_ctx_t, probs, [])
    )
    grad_qkv, grad_input, grad_bn, sums = attn_bwd_input(
        visual_live,
        attn_full,
        grads,
        grad_residual,
        pre,
        bn,
        queries,
        keys_t,
        values_t,
        [],
    )

    grad_bn_other = across(grad_bn)
    sums = table_grad(bucket, sums, score_grads, [])
    attn_parts = outer(
        targets,
        n_blocks,
        [x_low, ctx],
        [grad_qkv, grad_attended],
        [],
    )
    if ringed:
        attn_ring = RingSum(attn_parts)
        sent = [attn_ring.low, attn_ring.high]
    else:
        sent = []
    sums = sum_small(sums, [[attn_parts[0]], sent])
    shared_sums = sums[8:]
    shared_sums = (shared_sums + across(shared_sums))[4:7]
    project_parts, grad_pre = project_gradient(
        visual_live,
        targets,
        n_blocks,
        maps,
        grad_bn,
        grad_bn_other,
        pre,
        bn,
        shared_sums[:2],
        [],
    )
    (result,) = tie([result], [grad_pre])
    result_other = across(result)
    if ringed:
        project_ring = RingSum(project_parts)
        sent = [project_ring.low, project_ring.high]
        attn_ring.step()
        attn_ring.step(sent)
        later = project_ring.step()
        attn_ring.step(later + [result_other])
        project_ring.step()
        project_ring.step()
        attn_sum, project_grad = attn_ring.finish(), project_ring.finish()
    else:
        attn_sum, project_grad = scatter_sum(attn_parts[0][0]), scatter_sum(project_parts[0][0])
        sent = []
    ffn_grad, attn_grad = ffn_sum[None], attn_sum[None]
    grad_maps, joined = maps_gradient(grad_pre, project_half, result, result_other)
    width = shared_weight.shape[0]
    own_shared = lax.dynamic_slice(
        jnp.concatenate([shared_sums[2, : BUCKETS * HEADS], shared_sums[0], shared_sums[1]]),
        (me * width,),
        (width,),
    )

    all_tokens = n_batch * TLEN
    rate_attention = 1.5 / math.sqrt(D * all_tokens)
    rate_matrix = 0.6 / math.sqrt(D * all_tokens)
    rate_vector = 0.12 / math.sqrt(all_tokens)
    width = vector_weight.shape[1]
    vector_grad = lax.dynamic_slice(sums[:12].reshape(-1), (me * width,), (width,))[None]
    vector_new = nesterov(vector_weight, vector_moment, vector_average, vector_grad, rate_vector)
    ffn_new = nesterov(ffn_weight, ffn_moment, ffn_average, ffn_grad, rate_matrix)
    attn_new = nesterov(attn_weight, attn_moment, attn_average, attn_grad, rate_attention)
    project_new = nesterov(
        project_weight, project_moment, project_average, project_grad, rate_matrix
    )
    shared_new = nesterov(shared_weight, shared_moment, shared_average, own_shared, rate_vector)
    return (
        joined.reshape(1, TLEN, D),
        grad_input.reshape(1, 1, TLEN, D),
        grad_maps.reshape(1, TLEN, -1),
        attn_new[0],
        attn_new[1],
        attn_new[2],
        ffn_new[0],
        ffn_new[1],
        ffn_new[2],
        vector_new[0],
        vector_new[1],
        vector_new[2],
        project_new[0],
        project_new[1],
        project_new[2],
        shared_new[0],
        shared_new[1],
        shared_new[2],
    )


def solution(mesh):
    return jax.shard_map(
        on_device,
        mesh=mesh,
        in_specs=(
            P("batch", None, None),
            P("batch", None, "stream"),
            P("batch"),
            P("stream", "batch", None, None),
            P("batch", None, None),
            P("stream", "batch", None),
            P("stream", "batch", None),
            P("stream", "batch", None),
            P("stream", "batch", None),
            P("stream", "batch", None),
            P("stream", "batch", None),
            P("stream", "batch"),
            P("stream", "batch"),
            P("stream", "batch"),
            P(("stream", "batch"), None),
            P(("stream", "batch"), None),
            P(("stream", "batch"), None),
            P("batch"),
            P("batch"),
            P("batch"),
        ),
        out_specs=(
            P("batch", None, None),
            P("stream", "batch", None, None),
            P("batch", None, "stream"),
            P("stream", "batch", None),
            P("stream", "batch", None),
            P("stream", "batch", None),
            P("stream", "batch", None),
            P("stream", "batch", None),
            P("stream", "batch", None),
            P("stream", "batch"),
            P("stream", "batch"),
            P("stream", "batch"),
            P(("stream", "batch"), None),
            P(("stream", "batch"), None),
            P(("stream", "batch"), None),
            P("batch"),
            P("batch"),
            P("batch"),
        ),
        check_vma=False,
    )
```
